128 devices in a mesh: pack: 4 (over y), seq: 32 (over x, z, core).
Axes of the slice: x: 4, y: 4, z: 4, core: 2. Of those that a mesh axis runs over, the one named last changes fastest.
Arguments:
- query_rows: bfloat16 [4, 4096, 4096], P('pack', 'seq'), may hold values from -8 to 8
- key_rows: bfloat16 [4, 4096, 4096], P('pack', 'seq'), may hold values from -8 to 8
- value_rows: bfloat16 [4, 4096, 4096], P('pack', 'seq'), may hold values from -6 to 6
- target_rows: bfloat16 [4, 4096, 4096], P('pack', 'seq'), may hold values from -6 to 6
- norm_gains: float32 [2, 32, 128], P(None, 'seq'), may hold values from 0.5 to 3.2
- segment_ids: int32 [4, 4096], P('pack', 'seq'), may hold values from 0 to 15, never falling along the last dimension, each value on 1 to 1024 neighbouring positions
- group_labels: int32 [4, 16], P('pack'), may hold values from 0 to 7, as said below
- mixture: float32 [8], replicated, may hold values from 0.05 to 0.5
Outputs:
- attended: bfloat16 [4, 4096, 4096], P('pack', 'seq')
- grad_query: bfloat16 [4, 4096, 4096], P('pack', 'seq')
- grad_key: bfloat16 [4, 4096, 4096], P('pack', 'seq')
- grad_value: bfloat16 [4, 4096, 4096], P('pack', 'seq')
- grad_gains: float32 [2, 32, 128], P(None, 'seq')
- new_mixture: float32 [8], replicated
The draws below stay inside these ranges and needn't reach their ends.
Inputs may be any that keep to these rules, and one draw needn't show every extreme that they name: `segment_ids`: segment numbers never fall along a pack's rows; each image of a pack has 1 to 1024 patches, one exactly 1024. `group_labels`: every group labels one or more images of each pack.
All inputs are finite; a program needn't handle non-finite values.
Results may differ from the reference program's by a relative error of at most 0.0028.
The reference program's roundings to bfloat16 on the way (of `query_low`, `softmax_low`, `grad_low` and `score_grads`) count: a program that leaves them out, or rounds other values in their place, can miss the bound.
Values may be sent and summed in bfloat16 or wider, within the bound.
No kernel may reach another device: no remote copies, remote signals or barrier semaphores. Data moves between devices by JAX's collectives and lax.ppermute only.
A program may use at most 128 MiB of HBM per device.

```python
import math
import jax
import jax.numpy as jnp
import numpy as np
from jax import lax

HEADS = 32
HEAD_DIM = 128
IMAGES = 16
GROUPS = 8
PACKS = 4
LENGTH = 4096
MOST = 1024


def shared_keys(key):
    return jax.random.normal(key, (PACKS, LENGTH, HEADS * HEAD_DIM), jnp.float32)


def draw_key_rows(key, part):
    base = shared_keys(key)
    return jnp.clip(base, -8.0, 8.0).astype(jnp.bfloat16)


def draw_query_rows(key, part):
    base = shared_keys(key)
    key = jax.random.fold_in(key, 12)
    fresh = jax.random.normal(key, base.shape, jnp.float32)
    return jnp.clip(fresh, -8.0, 8.0).astype(jnp.bfloat16)


def draw_norm_gains(key, part):
    key = jax.random.fold_in(key, 13)
    gains = jax.random.uniform(key, (2, HEADS, HEAD_DIM), jnp.float32, 0.5, 1.6)
    return gains


def draw_group_labels(key, part):
    key = jax.random.fold_in(key, 14)
    first_key, rest_key = jax.random.split(key, 2)
    firsts = jax.vmap(lambda one_key: jax.random.permutation(one_key, GROUPS))(jax.random.split(first_key, PACKS))
    others = jax.random.randint(rest_key, (PACKS, IMAGES - GROUPS), 0, GROUPS)
    return jnp.concatenate([firsts.astype(jnp.int32), others.astype(jnp.int32)], 1)


def levels(key, shape, cuts, least, largest):
    level = 1.0
    for axis_at, shards_of in cuts:
        steps = jax.random.uniform(jax.random.fold_in(jax.random.fold_in(key, 6), axis_at), (shards_of,), jnp.float32, least / len(cuts), largest / len(cuts))
        level = level * jnp.repeat(jnp.exp(steps), shape[axis_at] // shards_of).reshape((-1,) + (1,) * (len(shape) - 1 - axis_at))
    return level


def length_profile(count, total, bound, skew):
    weights = [(1 << 20) // math.isqrt(grade ** skew) + 1 for grade in range(2, count + 1)]
    surplus, given = total - bound - (count - 1), [1] * (count - 1)
    while surplus > 0:
        free = [i for i in range(count - 1) if given[i] < bound]
        mass, left = sum([weights[i] for i in free]), surplus
        for i in free:
            more = min(bound - given[i], max(1, left * weights[i] // mass), surplus)
            given[i] = given[i] + more
            surplus = surplus - more
    return np.array([bound] + given)


def uneven_parts(key, amount, total, most, slope):
    if amount == 2:
        one = jax.random.randint(key, (), max(1, total - most), min(most, total - 1) + 1)
        return jnp.stack([one, total - one])
    tallies = jnp.asarray(length_profile(amount, total, most, slope), jnp.int32)
    pairs = (amount - 1) // 2
    donor, receiver = tallies[1:1 + 2 * pairs:2], tallies[2:2 + 2 * pairs:2]
    margin = jnp.minimum(donor - 1, most - receiver)
    passed = jax.random.randint(jax.random.fold_in(key, 1), (pairs,), 0, 1 << 20) % (margin + 1)
    tallies = tallies.at[1:1 + 2 * pairs:2].set(donor - passed).at[2:2 + 2 * pairs:2].set(receiver + passed)
    return tallies[jax.random.permutation(jax.random.fold_in(key, 2), amount)]


def scatter_about(own_key, extent, spread, reach, pieces=(), held_as=jnp.bfloat16):
    entries = spread * jax.random.normal(own_key, extent, jnp.float32)
    if pieces:
        entries = entries * levels(own_key, extent, pieces, -0.22, 0.18)
    return jnp.clip(entries, -reach, reach).astype(held_as)


def setup_inputs(seed: int = 0) -> dict:
    arg_keys = jax.random.split(jax.random.key(seed), 9)
    query_rows = draw_query_rows(jax.random.fold_in(arg_keys[8], 71), 0)
    key_rows = draw_key_rows(jax.random.fold_in(arg_keys[8], 71), 0)
    value_rows = scatter_about(arg_keys[2], (PACKS, LENGTH, HEADS * HEAD_DIM), 1.0, 6.0, ((0, 4), (1, 32)))
    target_rows = scatter_about(arg_keys[3], (PACKS, LENGTH, HEADS * HEAD_DIM), 1.0, 6.0, ((0, 4), (1, 32)))
    norm_gains = draw_norm_gains(jax.random.fold_in(arg_keys[8], 71), 0)
    segment_ids = jax.vmap(lambda own: jnp.searchsorted(jnp.cumsum(uneven_parts(own, IMAGES, LENGTH, MOST, 2)), jnp.arange(LENGTH), side="right"))(jax.random.split(arg_keys[5], PACKS)).reshape((PACKS, LENGTH)).astype(jnp.int32)
    group_labels = draw_group_labels(jax.random.fold_in(arg_keys[8], 71), 0)
    mixture = jnp.clip(jnp.exp(jax.random.uniform(arg_keys[7], (GROUPS,), jnp.float32, math.log(0.05), math.log(0.5))), 0.05, 0.5)
    return {"query_rows": query_rows, "key_rows": key_rows, "value_rows": value_rows, "target_rows": target_rows, "norm_gains": norm_gains, "segment_ids": segment_ids, "group_labels": group_labels, "mixture": mixture}


NEG = -1e+30
EPS = 1e-06
ETA = 2.0

def norm_forward(values, gain):
    centre = values - lax.optimization_barrier(jnp.mean(values, -1, keepdims=True))
    inverse = lax.rsqrt(lax.optimization_barrier(jnp.mean(centre * centre, -1, keepdims=True)) + EPS)
    normed = centre * inverse
    return (normed, inverse, normed * gain)

def norm_backward(grad_hat, normed, inverse, gain):
    grad_gain = lax.optimization_barrier(jnp.sum(grad_hat * normed, -2))
    grad_normed = grad_hat * gain
    inner = lax.optimization_barrier(jnp.mean(grad_normed * normed, -1, keepdims=True))
    grad_in = inverse * (grad_normed - lax.optimization_barrier(jnp.mean(grad_normed, -1, keepdims=True)) - normed * inner)
    return (grad_in, grad_gain)

def attend_head(query, keys_in, values_in, target, gain_query, gain_key, segments, coef):
    score_scale = HEAD_DIM ** (-0.5)
    q_normed, q_inverse, q_hat = norm_forward(query.astype(jnp.float32), gain_query[None, :])
    k_normed, k_inverse, k_hat = norm_forward(keys_in.astype(jnp.float32), gain_key[None, :])
    query_low = q_hat.astype(jnp.bfloat16)
    key_low = k_hat.astype(jnp.bfloat16)
    logits = jnp.dot(query_low, key_low.T, preferred_element_type=jnp.float32) * score_scale
    logits = jnp.where(segments[:, None] == segments[None, :], logits, NEG)
    row_top = lax.optimization_barrier(jnp.max(logits, -1, keepdims=True))
    exp_terms = jnp.exp(logits - row_top)
    softmax_rows = exp_terms / lax.optimization_barrier(jnp.sum(exp_terms, -1, keepdims=True))
    softmax_low = softmax_rows.astype(jnp.bfloat16)
    head_out = jnp.dot(softmax_low, values_in, preferred_element_type=jnp.float32)
    misfit = head_out - target.astype(jnp.float32)
    row_loss = 0.5 * lax.optimization_barrier(jnp.sum(misfit * misfit, -1))
    grad_out = coef[:, None] * misfit
    grad_low = grad_out.astype(jnp.bfloat16)
    row_inner = lax.optimization_barrier(jnp.sum(grad_out * head_out, -1))
    grad_value = jnp.dot(softmax_low.T, grad_low, preferred_element_type=jnp.float32)
    prob_grads = jnp.dot(grad_low, values_in.T, preferred_element_type=jnp.float32)
    score_grads = (softmax_rows * (prob_grads - row_inner[:, None]) * score_scale).astype(jnp.bfloat16)
    grad_qhat = jnp.dot(score_grads, key_low, preferred_element_type=jnp.float32)
    grad_khat = jnp.dot(score_grads.T, query_low, preferred_element_type=jnp.float32)
    grad_query, gain_grad_q = norm_backward(grad_qhat, q_normed, q_inverse, gain_query[None, :])
    grad_key, gain_grad_k = norm_backward(grad_khat, k_normed, k_inverse, gain_key[None, :])
    return (head_out.astype(jnp.bfloat16), grad_query.astype(jnp.bfloat16), grad_key.astype(jnp.bfloat16), grad_value.astype(jnp.bfloat16), gain_grad_q, gain_grad_k, row_loss)

def reference(query_rows, key_rows, value_rows, target_rows, norm_gains, segment_ids, group_labels, mixture):
    packs = query_rows.shape[0]
    seq_length = query_rows.shape[1]
    image_hot = (segment_ids[:, :, None] == jnp.arange(IMAGES, dtype=jnp.int32)[None, None, :]).astype(jnp.float32)
    label_hot = (group_labels[:, :, None] == jnp.arange(GROUPS, dtype=jnp.int32)[None, None, :]).astype(jnp.float32)
    group_hot = jnp.einsum('pli,pig->plg', image_hot, label_hot, precision=lax.Precision.HIGHEST)
    counts = lax.optimization_barrier(jnp.sum(group_hot, (0, 1)))
    shares = mixture / jnp.sum(mixture)
    row_coef = lax.optimization_barrier(jnp.sum(group_hot * (shares / (counts * (HEADS * HEAD_DIM)))[None, None, :], -1))

    def split_heads(values):
        return values.reshape(packs, seq_length, HEADS, HEAD_DIM).transpose(0, 2, 1, 3)

    def merge_heads(values):
        return values.transpose(0, 2, 1, 3).reshape(packs, seq_length, HEADS * HEAD_DIM)

    def one_pack(items):
        query, keys_in, values_in, target, segments, coef = items

        def one_head(head_items):
            head_q, head_k, head_v, head_t, gain_query, gain_key = head_items
            return attend_head(head_q, head_k, head_v, head_t, gain_query, gain_key, segments, coef)
        return lax.map(one_head, (query, keys_in, values_in, target, norm_gains[0], norm_gains[1]))
    results = lax.map(one_pack, (split_heads(query_rows), split_heads(key_rows), split_heads(value_rows), split_heads(target_rows), segment_ids, row_coef))
    head_out, grad_query, grad_key, grad_value, gain_grad_q, gain_grad_k, row_loss = results
    grad_gains = jnp.stack([lax.optimization_barrier(jnp.sum(gain_grad_q, 0)), lax.optimization_barrier(jnp.sum(gain_grad_k, 0))])
    losses = lax.optimization_barrier(jnp.sum(row_loss, 1))
    group_total = jnp.einsum('pl,plg->g', losses, group_hot, precision=lax.Precision.HIGHEST)
    group_loss = group_total / (counts * (HEADS * HEAD_DIM))
    raised = shares * jnp.exp(ETA * group_loss)
    return (merge_heads(head_out), merge_heads(grad_query), merge_heads(grad_key), merge_heads(grad_value), grad_gains, raised / jnp.sum(raised))
```

```python
import functools

import jax
import jax.numpy as jnp
from jax import lax
from jax.experimental import pallas as pl
from jax.experimental.pallas import tpu as pltpu
from jax.sharding import PartitionSpec as P

HEADS = 32
HEAD_DIM = 128
IMAGES = 16
GROUPS = 8
PACKS = 4
LENGTH = 4096

NEG = -1e30
EPS = 1e-06
ETA = 2.0
SCALE = HEAD_DIM ** (-0.5)
EXP_SCALE = SCALE * 1.4426950408889634

BLOCK = 128
BLOCKS = LENGTH // BLOCK
TILE = 512
TILES = LENGTH // TILE
PAIR = TILE // BLOCK
STATS_KEYS = 256
FORWARD_KEYS = 512
BACKWARD_KEYS = 256
EXTRA = 16
VMEM_LIMIT = 56 * 1024 * 1024

BF16 = jnp.bfloat16
F32 = jnp.float32
I32 = jnp.int32

VMEM_SPEC = pl.BlockSpec(memory_space=pltpu.VMEM)
SMEM_SPEC = pl.BlockSpec(memory_space=pltpu.SMEM)
ANY_SPEC = pl.BlockSpec(memory_space=pl.ANY)


def shape(dims, dtype):
    return jax.ShapeDtypeStruct(dims, dtype)


def head_columns(h):
    return pl.ds(h * HEAD_DIM, HEAD_DIM)


def pack_kernel(*refs):
    *row_refs, extra_ref, out_ref, sems = refs
    copies = []
    for n, ref in enumerate(row_refs):
        for h in range(HEADS):
            copy = pltpu.make_async_copy(
                ref.at[0, :, head_columns(h)],
                out_ref.at[h, pl.ds(n * BLOCK, BLOCK), :],
                sems.at[n, h],
            )
            copy.start()
            copies.append(copy)
    lines = extra_ref.shape[0]
    tile = extra_ref[...].astype(F32)
    tile = jnp.concatenate([tile, jnp.zeros((EXTRA - lines, 128), F32)], 0).astype(BF16)
    out_ref[:, len(row_refs) * BLOCK :, :] = jnp.broadcast_to(tile[None], (HEADS, EXTRA, 128))
    for copy in copies:
        copy.wait()


def pack_rows(rows, extra, name):
    return pl.pallas_call(
        pack_kernel,
        in_specs=[ANY_SPEC] * len(rows) + [VMEM_SPEC],
        out_specs=VMEM_SPEC,
        out_shape=shape((HEADS, len(rows) * BLOCK + EXTRA, 128), BF16),
        scratch_shapes=[pltpu.SemaphoreType.DMA((len(rows), HEADS))],
        compiler_params=pltpu.CompilerParams(vmem_limit_bytes=VMEM_LIMIT),
        name=name,
    )(*rows, extra)


def unpack_kernel(in_ref, *refs):
    *row_refs, sems = refs
    copies = []
    for n, ref in enumerate(row_refs):
        for h in range(HEADS):
            copy = pltpu.make_async_copy(
                in_ref.at[h, pl.ds(n * BLOCK, BLOCK), :],
                ref.at[0, :, head_columns(h)],
                sems.at[n, h],
            )
            copy.start()
            copies.append(copy)
    for copy in copies:
        copy.wait()


def unpack_rows(slab, count, name):
    return pl.pallas_call(
        unpack_kernel,
        in_specs=[VMEM_SPEC],
        out_specs=[ANY_SPEC] * count,
        out_shape=[shape((1, BLOCK, HEADS * HEAD_DIM), BF16)] * count,
        scratch_shapes=[pltpu.SemaphoreType.DMA((count, HEADS))],
        compiler_params=pltpu.CompilerParams(vmem_limit_bytes=VMEM_LIMIT),
        name=name,
    )(slab)


def normalise(rows):
    values = rows.astype(F32)
    centre = values - jnp.mean(values, -1, keepdims=True)
    inverse = lax.rsqrt(jnp.mean(centre * centre, -1, keepdims=True) + EPS)
    return centre * inverse, inverse


def denormalise(grad_hat, normed, inverse, gain):
    grad_gain = jnp.sum(grad_hat * normed, 0, keepdims=True)
    grad_normed = grad_hat * gain
    inner = jnp.mean(grad_normed * normed, -1, keepdims=True)
    grad_in = inverse * (grad_normed - jnp.mean(grad_normed, -1, keepdims=True) - normed * inner)
    return grad_in, grad_gain


def dot(a, b, contract=((1,), (0,))):
    return lax.dot_general(a, b, (contract, ((), ())), preferred_element_type=F32)


def tile_rows(ref, i, part, size=TILE):
    blocks = size // BLOCK
    return ref[pl.ds(i, blocks), part * BLOCK : (part + 1) * BLOCK, :].reshape(size, HEAD_DIM)


def key_span(span_ref, i, step):
    low, high = span_ref[0, i], span_ref[1, i]
    steps = (high - low + step - 1) // step
    return jnp.minimum(low, LENGTH - steps * step), steps


def key_mask(span_rows_ref, i, start, step):
    first = span_rows_ref[i, 0:1, :] - start
    count = span_rows_ref[i, 1:2, :]
    row = lax.broadcasted_iota(I32, (step, TILE), 0)
    return (row - first).astype(jnp.uint32) < count.astype(jnp.uint32)


def stats_kernel(
    recv_ref, gains_ref,
    q_hat_ref, k_hat_ref, k_turned_ref, span_ref, span_rows_ref, norm_ref,
    starts, scores,
):
    gain_q = gains_ref[0:1, :]
    gain_k = gains_ref[1:2, :]

    seg_all = recv_ref[:, 2 * BLOCK, :].astype(F32)
    for s in range(IMAGES + 1):
        starts[s] = jnp.sum((seg_all < float(s)).astype(F32)).astype(I32)
    first = jnp.zeros((BLOCKS, 128), I32)
    count = jnp.zeros((BLOCKS, 128), I32)
    for s in range(IMAGES):
        here = seg_all == float(s)
        first = jnp.where(here, starts[s], first)
        count = jnp.where(here, starts[s + 1] - starts[s], count)
    for b in range(BLOCKS):
        at = slice((b % PAIR) * BLOCK, (b % PAIR + 1) * BLOCK)
        span_rows_ref[b // PAIR, 0:1, at] = first[b : b + 1, :]
        span_rows_ref[b // PAIR, 1:2, at] = count[b : b + 1, :]

    def span(i, carry):
        low, high = jnp.int32(0), jnp.int32(LENGTH)
        for s in range(1, IMAGES):
            low = jnp.where(starts[s] <= i * TILE, starts[s], low)
        for s in range(IMAGES - 1, 0, -1):
            high = jnp.where(starts[s] > i * TILE + TILE - 1, starts[s], high)
        span_ref[0, i] = (low // BLOCK) * BLOCK
        span_ref[1, i] = high
        return carry

    lax.fori_loop(0, TILES, span, 0)

    def prepare(i, carry):
        rows = pl.ds(pl.multiple_of(i * TILE, TILE), TILE)
        normed, _ = normalise(tile_rows(recv_ref, i * PAIR, 0))
        q_hat_ref[rows, :] = (normed * gain_q).astype(BF16)
        normed, _ = normalise(tile_rows(recv_ref, i * PAIR, 1))
        low = (normed * gain_k).astype(BF16)
        k_hat_ref[rows, :] = low
        k_turned_ref[:, rows] = low.T
        return carry

    lax.fori_loop(0, TILES, prepare, 0)

    step = STATS_KEYS

    def query_tile(i, carry):
        start, steps = key_span(span_ref, i, step)
        query = q_hat_ref[pl.ds(pl.multiple_of(i * TILE, TILE), TILE), :]

        def score_tile(j, top):
            at = pl.multiple_of(start + j * step, BLOCK)
            tile = dot(k_hat_ref[pl.ds(at, step), :], query, ((1,), (1,)))
            tile = jnp.where(key_mask(span_rows_ref, i, at, step), tile, NEG)
            scores[j] = tile
            return jnp.maximum(top, jnp.max(tile.reshape(step // 8, 8, TILE), 0))

        top = lax.fori_loop(0, steps, score_tile, jnp.full((8, TILE), NEG, F32))
        top = jnp.max(top, 0, keepdims=True) * EXP_SCALE

        def exp_tile(j, total):
            tile = jnp.exp2(scores[j] * EXP_SCALE - top)
            return total + jnp.sum(tile.reshape(step // 8, 8, TILE), 0)

        total = lax.fori_loop(0, steps, exp_tile, jnp.zeros((8, TILE), F32))
        norm_ref[i, 0:1, :] = top
        norm_ref[i, 1:2, :] = 1.0 / jnp.sum(total, 0, keepdims=True)
        return carry

    lax.fori_loop(0, TILES, query_tile, 0)


def run_stats(received, gains):
    most = 2 * 1024 // STATS_KEYS + TILE // STATS_KEYS + 2
    return pl.pallas_call(
        stats_kernel,
        in_specs=[VMEM_SPEC, VMEM_SPEC],
        out_specs=[VMEM_SPEC] * 3 + [SMEM_SPEC] + [VMEM_SPEC] * 2,
        out_shape=[
            shape((LENGTH, HEAD_DIM), BF16),
            shape((LENGTH, HEAD_DIM), BF16),
            shape((HEAD_DIM, LENGTH), BF16),
            shape((2, TILES), I32),
            shape((TILES, 2, TILE), I32),
            shape((TILES, 2, TILE), F32),
        ],
        scratch_shapes=[
            pltpu.SMEM((IMAGES + 1,), I32),
            pltpu.VMEM((most, STATS_KEYS, TILE), F32),
        ],
        compiler_params=pltpu.CompilerParams(vmem_limit_bytes=VMEM_LIMIT),
        name="score_stats",
    )(received, gains)


def softmax_tile(k_hat_ref, query, span_rows_ref, top, inverse_total, i, at, step):
    tile = dot(k_hat_ref[pl.ds(at, step), :], query, ((1,), (1,)))
    tile = jnp.where(key_mask(span_rows_ref, i, at, step), tile, NEG)
    return jnp.exp2(tile * EXP_SCALE - top) * inverse_total


def forward_kernel(
    span_ref, labels_ref, mixture_ref,
    seg_ref, recv_ref, q_hat_ref, k_hat_ref, span_rows_ref, norm_ref,
    send_ref, grad_ref, grad_turned_ref, inner_ref, counts_ref,
    coef_rows, loss_rows, v_turned, acc,
):
    seg_all = seg_ref[:, 2 * BLOCK, :].astype(F32)
    group = jnp.zeros((BLOCKS, 128), F32)
    for s in range(IMAGES):
        group = jnp.where(seg_all == float(s), labels_ref[0, s].astype(F32), group)
    others = [recv_ref[:, 2 * BLOCK + p, :].astype(F32) for p in range(PACKS)]
    total_mix = mixture_ref[0]
    for g in range(1, GROUPS):
        total_mix = total_mix + mixture_ref[g]
    coef = jnp.zeros((BLOCKS, 128), F32)
    lane = lax.broadcasted_iota(I32, (1, 128), 1)
    count_row = jnp.zeros((1, 128), F32)
    for g in range(GROUPS):
        hits = sum((o == float(g)).astype(F32) for o in others)
        count = jnp.sum(jnp.sum(hits, 0, keepdims=True), 1, keepdims=True)
        share = jnp.full((1, 1), mixture_ref[g], F32) / total_mix
        coef = jnp.where(group == float(g), share / (count * (HEADS * HEAD_DIM)), coef)
        count_row = jnp.where(lane == g, count, count_row)
    counts_ref[...] = count_row
    for b in range(BLOCKS):
        at = slice((b % PAIR) * BLOCK, (b % PAIR + 1) * BLOCK)
        coef_rows[b // PAIR, 0:1, at] = coef[b : b + 1, :]

    def prepare(i, carry):
        rows = pl.ds(pl.multiple_of(i * TILE, TILE), TILE)
        v_turned[:, rows] = tile_rows(recv_ref, i * PAIR, 0).T
        return carry

    lax.fori_loop(0, TILES, prepare, 0)

    step = FORWARD_KEYS

    def query_tile(i, carry):
        start, steps = key_span(span_ref, i, step)
        query_rows = pl.ds(pl.multiple_of(i * TILE, TILE), TILE)
        query = q_hat_ref[query_rows, :]
        top, inverse_total = norm_ref[i, 0:1, :], norm_ref[i, 1:2, :]
        acc[...] = jnp.zeros_like(acc)

        def out_tile(j, inside):
            at = pl.multiple_of(start + j * step, BLOCK)
            tile = softmax_tile(k_hat_ref, query, span_rows_ref, top, inverse_total, i, at, step)
            acc[...] += dot(v_turned[:, pl.ds(at, step)], tile.astype(BF16))
            return inside

        lax.fori_loop(0, steps, out_tile, 0)

        head_out = acc[...]
        target = tile_rows(recv_ref, i * PAIR, 1).T
        misfit = head_out - target.astype(F32)
        loss_rows[i, 0:1, :] = 0.5 * jnp.sum(misfit * misfit, 0, keepdims=True)
        grad_out = coef_rows[i, 0:1, :] * misfit
        inner_ref[i, 0:1, :] = jnp.sum(grad_out * head_out, 0, keepdims=True)
        grad_turned = grad_out.astype(BF16)
        grad_turned_ref[:, query_rows] = grad_turned
        grad_ref[query_rows, :] = grad_turned.T
        send_ref[pl.ds(i * PAIR, PAIR), 0:BLOCK, :] = head_out.astype(BF16).T.reshape(
            PAIR, BLOCK, HEAD_DIM
        )
        return carry

    lax.fori_loop(0, TILES, query_tile, 0)

    losses = jnp.concatenate(
        [
            loss_rows[b // PAIR, 0:1, (b % PAIR) * BLOCK : (b % PAIR + 1) * BLOCK]
            for b in range(BLOCKS)
        ],
        0,
    )
    loss_row = jnp.zeros((1, 128), F32)
    for g in range(GROUPS):
        part = jnp.where(group == float(g), losses, 0.0)
        part = jnp.sum(jnp.sum(part, 0, keepdims=True), 1, keepdims=True)
        loss_row = jnp.where(lane == g, part, loss_row)
    high = loss_row.astype(BF16)
    left = loss_row - high.astype(F32)
    middle = left.astype(BF16)
    low = (left - middle.astype(F32)).astype(BF16)
    row = lax.broadcasted_iota(I32, (EXTRA, 128), 0)
    pieces = jnp.zeros((EXTRA, 128), F32)
    for n, piece in enumerate((high, middle, low)):
        pieces = jnp.where(row == n, piece.astype(F32), pieces)
    send_ref[:, BLOCK:, :] = jnp.broadcast_to(pieces.astype(BF16)[None], (BLOCKS, EXTRA, 128))


def run_forward(spans, labels, mixture, first, second, q_hat, k_hat, span_rows, norms):
    return pl.pallas_call(
        forward_kernel,
        in_specs=[SMEM_SPEC] * 3 + [VMEM_SPEC] * 6,
        out_specs=[VMEM_SPEC] * 5,
        out_shape=[
            shape((BLOCKS, BLOCK + EXTRA, 128), BF16),
            shape((LENGTH, HEAD_DIM), BF16),
            shape((HEAD_DIM, LENGTH), BF16),
            shape((TILES, 1, TILE), F32),
            shape((1, 128), F32),
        ],
        scratch_shapes=[
            pltpu.VMEM((TILES, 8, TILE), F32),
            pltpu.VMEM((TILES, 8, TILE), F32),
            pltpu.VMEM((HEAD_DIM, LENGTH), BF16),
            pltpu.VMEM((HEAD_DIM, TILE), F32),
        ],
        compiler_params=pltpu.CompilerParams(vmem_limit_bytes=VMEM_LIMIT),
        name="forward",
    )(spans, labels, mixture, first, second, q_hat, k_hat, span_rows, norms)


def backward_kernel(
    span_ref,
    first_ref, recv_ref, gains_ref, q_hat_ref, k_hat_ref, k_turned_ref, span_rows_ref, norm_ref,
    grad_ref, grad_turned_ref, inner_ref,
    send_ref, gain_out_ref,
    grad_k, grad_v, acc,
):
    gain_q = gains_ref[0:1, :]
    gain_k = gains_ref[1:2, :]
    zero_gain = jnp.zeros((1, HEAD_DIM), F32)
    grad_k[...] = jnp.zeros_like(grad_k)
    grad_v[...] = jnp.zeros_like(grad_v)

    step = BACKWARD_KEYS

    def query_tile(i, gain_sum):
        start, steps = key_span(span_ref, i, step)
        query_rows = pl.ds(pl.multiple_of(i * TILE, TILE), TILE)
        query = q_hat_ref[query_rows, :]
        top, inverse_total = norm_ref[i, 0:1, :], norm_ref[i, 1:2, :]
        grad_low = grad_ref[query_rows, :]
        grad_turned = grad_turned_ref[:, query_rows]
        row_inner = inner_ref[i, 0:1, :]
        acc[...] = jnp.zeros_like(acc)

        def back_tile(j, inside):
            at = pl.multiple_of(start + j * step, BLOCK)
            keys = pl.ds(at, step)
            tile = softmax_tile(k_hat_ref, query, span_rows_ref, top, inverse_total, i, at, step)
            value = tile_rows(recv_ref, at // BLOCK, 0, step)
            prob_grads = dot(value, grad_turned)
            grad_v[keys, :] += dot(tile.astype(BF16), grad_low)
            score_grads = (tile * (prob_grads - row_inner) * SCALE).astype(BF16)
            grad_k[keys, :] += dot(score_grads, query)
            acc[...] += dot(k_turned_ref[:, keys], score_grads)
            return inside

        lax.fori_loop(0, steps, back_tile, 0)

        normed, inverse = normalise(tile_rows(first_ref, i * PAIR, 0))
        grad_in, grad_gain = denormalise(acc[...].T, normed, inverse, gain_q)
        send_ref[pl.ds(i * PAIR, PAIR), 0:BLOCK, :] = grad_in.astype(BF16).reshape(
            PAIR, BLOCK, HEAD_DIM
        )
        return gain_sum + grad_gain

    gain_out_ref[0:1, :] = lax.fori_loop(0, TILES, query_tile, zero_gain)

    def key_tile(i, gain_sum):
        rows = pl.ds(pl.multiple_of(i * TILE, TILE), TILE)
        normed, inverse = normalise(tile_rows(first_ref, i * PAIR, 1))
        grad_in, grad_gain = denormalise(grad_k[rows, :], normed, inverse, gain_k)
        at = pl.ds(i * PAIR, PAIR)
        send_ref[at, BLOCK : 2 * BLOCK, :] = grad_in.astype(BF16).reshape(PAIR, BLOCK, HEAD_DIM)
        send_ref[at, 2 * BLOCK :, :] = grad_v[rows, :].astype(BF16).reshape(PAIR, BLOCK, HEAD_DIM)
        return gain_sum + grad_gain

    gain_out_ref[1:2, :] = lax.fori_loop(0, TILES, key_tile, zero_gain)


def run_backward(spans, first, second, gains, q_hat, k_hat, k_turned, span_rows, norms, grads):
    return pl.pallas_call(
        backward_kernel,
        in_specs=[SMEM_SPEC] + [VMEM_SPEC] * 11,
        out_specs=[VMEM_SPEC] * 2,
        out_shape=[shape((BLOCKS, 3 * BLOCK, 128), BF16), shape((2, HEAD_DIM), F32)],
        scratch_shapes=[
            pltpu.VMEM((LENGTH, HEAD_DIM), F32),
            pltpu.VMEM((LENGTH, HEAD_DIM), F32),
            pltpu.VMEM((HEAD_DIM, TILE), F32),
        ],
        compiler_params=pltpu.CompilerParams(vmem_limit_bytes=VMEM_LIMIT),
        name="backward",
    )(spans, first, second, gains, q_hat, k_hat, k_turned, span_rows, norms, *grads)


def over_packs(value):
    moved = [value]
    for shift in range(1, PACKS):
        pairs = [(i, (i + shift) % PACKS) for i in range(PACKS)]
        moved.append(lax.ppermute(value, "pack", pairs))
    return moved


def exchange(slab):
    return lax.all_to_all(slab, "seq", split_axis=0, concat_axis=0, tiled=True)


def on_device(
    query_rows, key_rows, value_rows, target_rows, norm_gains, segment_ids, group_labels, mixture
):
    gains = norm_gains.reshape(2, HEAD_DIM)
    first = exchange(pack_rows((query_rows, key_rows), segment_ids, "pack_first"))

    image_hot = segment_ids[0][:, None] == jnp.arange(IMAGES, dtype=I32)[None, :]
    labels = jnp.sum(jnp.where(image_hot, group_labels[0][None, :], 0), 1)[None, :]
    extra = jnp.concatenate(over_packs(labels.astype(F32)), 0)
    second = exchange(pack_rows((value_rows, target_rows), extra, "pack_second"))

    q_hat, k_hat, k_turned, spans, span_rows, norms = run_stats(first, gains)
    send, *grads, counts = run_forward(
        spans, group_labels, mixture, first, second, q_hat, k_hat, span_rows, norms
    )
    back = exchange(send)
    send, gain_part = run_backward(
        spans, first, second, gains, q_hat, k_hat, k_turned, span_rows, norms, grads
    )
    last = exchange(send)
    (attended,) = unpack_rows(back, 1, "unpack_first")
    losses = jnp.sum(back[:, BLOCK : BLOCK + 3, :GROUPS].astype(F32), (0, 1))
    group_total = sum(over_packs(losses))
    group_loss = group_total / (counts[0, :GROUPS] * (HEADS * HEAD_DIM))
    shares = mixture / jnp.sum(mixture)
    raised = shares * jnp.exp(ETA * group_loss)
    new_mixture = raised / jnp.sum(raised)
    grad_gains = sum(over_packs(gain_part)).reshape(2, 1, HEAD_DIM)
    grad_query, grad_key, grad_value = unpack_rows(last, 3, "unpack_last")
    return (attended, grad_query, grad_key, grad_value, grad_gains, new_mixture)


def solution(mesh):
    rows = P("pack", "seq", None)
    gains = P(None, "seq", None)
    return jax.shard_map(
        on_device,
        mesh=mesh,
        in_specs=(rows, rows, rows, rows, gains, P("pack", "seq"), P("pack", None), P()),
        out_specs=(rows, rows, rows, rows, gains, P()),
        check_vma=False,
    )
```

```python
import functools

import jax
import jax.numpy as jnp
from jax import lax
from jax.experimental import pallas as pl
from jax.experimental.pallas import tpu as pltpu
from jax.sharding import PartitionSpec as P

HEADS = 32
HEAD_DIM = 128
IMAGES = 16
GROUPS = 8
PACKS = 4
LENGTH = 4096

NEG = -1e30
EPS = 1e-06
ETA = 2.0
SCALE = HEAD_DIM ** (-0.5)
EXP_SCALE = SCALE * 1.4426950408889634

BLOCK = 128
BLOCKS = LENGTH // BLOCK
TILE = 256
TILES = LENGTH // TILE
PAIR = TILE // BLOCK
KEYS = 256
STATS_KEYS = 512
FORWARD_UNROLL = 4
BACKWARD_UNROLL = 4
MOST_UNROLL = max(FORWARD_UNROLL, BACKWARD_UNROLL)
MOST_PAIRS = TILES * 10 + MOST_UNROLL
EXTRA = 16
VMEM_LIMIT = 28 * 1024 * 1024

BF16 = jnp.bfloat16
F32 = jnp.float32
I32 = jnp.int32

VMEM_SPEC = pl.BlockSpec(memory_space=pltpu.VMEM)
SMEM_SPEC = pl.BlockSpec(memory_space=pltpu.SMEM)
ANY_SPEC = pl.BlockSpec(memory_space=pl.ANY)


def shape(dims, dtype):
    return jax.ShapeDtypeStruct(dims, dtype)


def head_columns(h):
    return pl.ds(h * HEAD_DIM, HEAD_DIM)


def pack_kernel(count, *refs):
    row_refs, extra_refs, (out_ref, sems) = refs[:count], refs[count:-2], refs[-2:]
    copies = []
    for n, ref in enumerate(row_refs):
        for h in range(HEADS):
            copy = pltpu.make_async_copy(
                ref.at[0, :, head_columns(h)],
                out_ref.at[h, pl.ds(n * BLOCK, BLOCK), :],
                sems.at[n, h],
            )
            copy.start()
            copies.append(copy)
    for extra_ref in extra_refs:
        tile = jnp.broadcast_to(extra_ref[...].astype(F32), (EXTRA, 128)).astype(BF16)
        out_ref[:, len(row_refs) * BLOCK :, :] = jnp.broadcast_to(tile[None], (HEADS, EXTRA, 128))
    for copy in copies:
        copy.wait()


def pack_rows(rows, extra, name):
    extras = () if extra is None else (extra,)
    return pl.pallas_call(
        functools.partial(pack_kernel, len(rows)),
        in_specs=[ANY_SPEC] * len(rows) + [VMEM_SPEC] * len(extras),
        out_specs=VMEM_SPEC,
        out_shape=shape((HEADS, len(rows) * BLOCK + EXTRA * len(extras), 128), BF16),
        scratch_shapes=[pltpu.SemaphoreType.DMA((len(rows), HEADS))],
        compiler_params=pltpu.CompilerParams(vmem_limit_bytes=VMEM_LIMIT),
        name=name,
    )(*rows, *extras)


def unpack_kernel(in_ref, *refs):
    *row_refs, sems = refs
    copies = []
    for n, ref in enumerate(row_refs):
        for h in range(HEADS):
            copy = pltpu.make_async_copy(
                in_ref.at[h, pl.ds(n * BLOCK, BLOCK), :],
                ref.at[0, :, head_columns(h)],
                sems.at[n, h],
            )
            copy.start()
            copies.append(copy)
    for copy in copies:
        copy.wait()


def unpack_rows(slab, count, name):
    return pl.pallas_call(
        unpack_kernel,
        in_specs=[VMEM_SPEC],
        out_specs=[ANY_SPEC] * count,
        out_shape=[shape((1, BLOCK, HEADS * HEAD_DIM), BF16)] * count,
        scratch_shapes=[pltpu.SemaphoreType.DMA((count, HEADS))],
        compiler_params=pltpu.CompilerParams(vmem_limit_bytes=VMEM_LIMIT),
        name=name,
    )(slab)


def dot(a, b, contract=((1,), (0,))):
    return lax.dot_general(a, b, (contract, ((), ())), preferred_element_type=F32)


def tile_rows(ref, i, part, size=TILE):
    blocks = size // BLOCK
    return ref[pl.ds(i, blocks), part * BLOCK : (part + 1) * BLOCK, :].reshape(size, HEAD_DIM)


def tile_at(i, size=TILE):
    return pl.ds(pl.multiple_of(i * size, size), size)


def mean_down(values):
    return jnp.sum(values, 0, keepdims=True) * (1.0 / HEAD_DIM)


def block_row(b):
    return b // PAIR, slice((b % PAIR) * BLOCK, (b % PAIR + 1) * BLOCK)


def group_sums(group, values):
    lane = lax.broadcasted_iota(I32, (1, 128), 1)
    sums = jnp.zeros((1, 128), F32)
    for g in range(GROUPS):
        part = jnp.sum(jnp.where(group == float(g), values, 0.0), 0, keepdims=True)
        sums = jnp.where(lane == g, jnp.sum(part, 1, keepdims=True), sums)
    return sums


def groups_kernel(labels_ref, seg_ref, group_ref, counts_ref, span_ref, pair_ref, span_rows_ref, starts):
    seg_all = seg_ref[:, 0, :].astype(F32)
    group = jnp.zeros((BLOCKS, 128), F32)
    for s in range(IMAGES):
        group = jnp.where(seg_all == float(s), labels_ref[0, s].astype(F32), group)
    group_ref[...] = group
    counts_ref[...] = group_sums(group, jnp.ones((BLOCKS, 128), F32))

    for s in range(IMAGES + 1):
        starts[s] = jnp.sum((seg_all < float(s)).astype(F32)).astype(I32)
    first = jnp.zeros((BLOCKS, 128), I32)
    count = jnp.zeros((BLOCKS, 128), I32)
    for s in range(IMAGES):
        here = seg_all == float(s)
        first = jnp.where(here, starts[s], first)
        count = jnp.where(here, starts[s + 1] - starts[s], count)
    for b in range(BLOCKS):
        tile, at = block_row(b)
        span_rows_ref[tile, 0:1, at] = first[b : b + 1, :]
        span_rows_ref[tile, 1:2, at] = count[b : b + 1, :]

    def span(i, total):
        low, high = jnp.int32(0), jnp.int32(LENGTH)
        for s in range(1, IMAGES):
            low = jnp.where(starts[s] <= i * TILE, starts[s], low)
        for s in range(IMAGES - 1, 0, -1):
            high = jnp.where(starts[s] > i * TILE + TILE - 1, starts[s], high)
        low = (low // BLOCK) * BLOCK
        span_ref[0, i] = low
        span_ref[1, i] = high
        steps = (high - low + KEYS - 1) // KEYS
        low = jnp.minimum(low, LENGTH - steps * KEYS)

        def add(j, carry):
            pair_ref[0, total + j] = i
            pair_ref[1, total + j] = low + j * KEYS
            pair_ref[2, total + j] = low + j * KEYS
            return carry

        lax.fori_loop(0, steps, add, 0)
        return total + steps

    total = lax.fori_loop(0, TILES, span, jnp.int32(0))
    span_ref[0, TILES] = total
    span_ref[1, TILES] = total
    for u in range(MOST_UNROLL):
        pair_ref[0, total + u] = 0
        pair_ref[1, total + u] = 0
        pair_ref[2, total + u] = -(1 << 20)


def run_groups(labels, received):
    return pl.pallas_call(
        groups_kernel,
        grid=(1,),
        in_specs=[SMEM_SPEC, pl.BlockSpec((BLOCKS, EXTRA, 128), lambda i: (0, 2 * BLOCK // EXTRA, 0))],
        out_specs=[VMEM_SPEC, VMEM_SPEC, SMEM_SPEC, SMEM_SPEC, VMEM_SPEC],
        out_shape=[
            shape((BLOCKS, 128), F32),
            shape((1, 128), F32),
            shape((2, TILES + 1), I32),
            shape((3, MOST_PAIRS), I32),
            shape((TILES, 2, TILE), I32),
        ],
        scratch_shapes=[pltpu.SMEM((IMAGES + 1,), I32)],
        name="row_groups",
    )(labels, received)


def key_mask(span_rows_ref, i, start, step):
    first = span_rows_ref[i, 0:1, :] - start
    count = span_rows_ref[i, 1:2, :]
    row = lax.broadcasted_iota(I32, (step, TILE), 0)
    return (row - first).astype(jnp.uint32) < count.astype(jnp.uint32)


def stats_kernel(
    span_ref, recv_ref, gains_ref, span_rows_ref,
    q_hat_ref, k_hat_ref, q_turned_ref, k_turned_ref, raw_q_ref, raw_k_ref, moments_ref, norm_ref,
    scores,
):
    gains = jnp.concatenate([gains_ref[...], jnp.zeros((6, HEAD_DIM), F32)], 0).T

    def prepare(i, carry):
        rows = tile_at(i)
        outs = ((q_hat_ref, q_turned_ref, raw_q_ref), (k_hat_ref, k_turned_ref, raw_k_ref))
        for n, (hat_ref, turned_ref, raw_ref) in enumerate(outs):
            raw = tile_rows(recv_ref, i * PAIR, n).T
            raw_ref[:, rows] = raw
            values = raw.astype(F32)
            mean = mean_down(values)
            centre = values - mean
            inverse = lax.rsqrt(mean_down(centre * centre) + EPS)
            moments_ref[i, 2 * n : 2 * n + 1, :] = mean
            moments_ref[i, 2 * n + 1 : 2 * n + 2, :] = inverse
            hat = (centre * inverse * gains[:, n : n + 1]).astype(BF16)
            turned_ref[:, rows] = hat
            hat_ref[rows, :] = hat.T
        return carry

    lax.fori_loop(0, TILES, prepare, 0)

    step = STATS_KEYS

    def query_tile(i, carry):
        low, high = span_ref[0, i], span_ref[1, i]
        steps = (high - low + step - 1) // step
        start = jnp.minimum(low, LENGTH - steps * step)
        query = q_turned_ref[:, tile_at(i)]

        def score_tile(j, top):
            at = pl.multiple_of(start + j * step, BLOCK)
            tile = dot(k_hat_ref[pl.ds(at, step), :], query)
            tile = jnp.where(key_mask(span_rows_ref, i, at, step), tile, NEG)
            scores[j] = tile
            return jnp.maximum(top, jnp.max(tile.reshape(step // 8, 8, TILE), 0))

        top = lax.fori_loop(0, steps, score_tile, jnp.full((8, TILE), NEG, F32))
        top = jnp.max(top, 0, keepdims=True) * EXP_SCALE

        def exp_tile(j, total):
            tile = jnp.exp2(scores[j] * EXP_SCALE - top)
            return total + jnp.sum(tile.reshape(step // 8, 8, TILE), 0)

        total = lax.fori_loop(0, steps, exp_tile, jnp.zeros((8, TILE), F32))
        norm_ref[i, 0:1, :] = top
        norm_ref[i, 1:2, :] = 1.0 / jnp.sum(total, 0, keepdims=True)
        return carry

    lax.fori_loop(0, TILES, query_tile, 0)


def run_stats(spans, received, gains, span_rows):
    most = 2 * 1024 // STATS_KEYS + TILE // STATS_KEYS + 2
    return pl.pallas_call(
        stats_kernel,
        in_specs=[SMEM_SPEC] + [VMEM_SPEC] * 3,
        out_specs=[VMEM_SPEC] * 8,
        out_shape=[
            shape((LENGTH, HEAD_DIM), BF16),
            shape((LENGTH, HEAD_DIM), BF16),
            shape((HEAD_DIM, LENGTH), BF16),
            shape((HEAD_DIM, LENGTH), BF16),
            shape((HEAD_DIM, LENGTH), BF16),
            shape((HEAD_DIM, LENGTH), BF16),
            shape((TILES, 4, TILE), F32),
            shape((TILES, 2, TILE), F32),
        ],
        scratch_shapes=[pltpu.VMEM((most, STATS_KEYS, TILE), F32)],
        compiler_params=pltpu.CompilerParams(vmem_limit_bytes=VMEM_LIMIT),
        name="score_stats",
    )(spans, received, gains, span_rows)


def softmax_tile(scores, span_rows_ref, norm_ref, i, mask_at):
    scores = jnp.where(key_mask(span_rows_ref, i, mask_at, KEYS), scores, NEG)
    top, inverse_total = norm_ref[i, 0:1, :], norm_ref[i, 1:2, :]
    return jnp.exp2(scores * EXP_SCALE - top) * inverse_total


def each_pairs(total, unroll, pair_ref, body):
    def some(n, carry):
        pairs = []
        for u in range(unroll):
            p = n * unroll + u
            pairs.append((pair_ref[0, p], pl.multiple_of(pair_ref[1, p], BLOCK), pair_ref[2, p]))
        body(pairs)
        return carry

    lax.fori_loop(0, (total + unroll - 1) // unroll, some, 0)


def forward_kernel(
    span_ref, pair_ref, mixture_ref,
    counts_ref, group_ref, recv_ref, q_turned_ref, k_hat_ref, span_rows_ref, norm_ref,
    send_ref, grad_ref, grad_turned_ref, inner_ref,
    coef_rows, loss_rows, v_turned, out_turned,
):
    def prepare(i, carry):
        v_turned[:, tile_at(i)] = tile_rows(recv_ref, i * PAIR, 0).T
        out_turned[i] = jnp.zeros((HEAD_DIM, TILE), F32)
        return carry

    lax.fori_loop(0, TILES, prepare, 0)

    group = group_ref[...]
    counts = jnp.sum(counts_ref[...], 0, keepdims=True)
    total_mix = mixture_ref[0]
    for g in range(1, GROUPS):
        total_mix = total_mix + mixture_ref[g]
    coef = jnp.zeros((BLOCKS, 128), F32)
    for g in range(GROUPS):
        share = jnp.full((1, 1), mixture_ref[g], F32) / total_mix
        share = share / (counts[:, g : g + 1] * (HEADS * HEAD_DIM))
        coef = jnp.where(group == float(g), share, coef)
    for b in range(BLOCKS):
        tile, at = block_row(b)
        coef_rows[tile, 0:1, at] = coef[b : b + 1, :]

    def add_pairs(pairs):
        tiles = [
            dot(k_hat_ref[pl.ds(at, KEYS), :], q_turned_ref[:, tile_at(i)]) for i, at, _ in pairs
        ]
        tiles = [
            softmax_tile(tile, span_rows_ref, norm_ref, i, mask_at).astype(BF16)
            for tile, (i, _, mask_at) in zip(tiles, pairs)
        ]
        tiles = [dot(v_turned[:, pl.ds(at, KEYS)], tile) for tile, (_, at, _) in zip(tiles, pairs)]
        for tile, (i, _, _) in zip(tiles, pairs):
            out_turned[i] += tile

    each_pairs(span_ref[0, TILES], FORWARD_UNROLL, pair_ref, add_pairs)

    def finish(i, carry):
        rows = tile_at(i)
        head_out = out_turned[i]
        misfit = head_out - tile_rows(recv_ref, i * PAIR, 1).T.astype(F32)
        loss_rows[i, 0:1, :] = 0.5 * jnp.sum(misfit * misfit, 0, keepdims=True)
        grad_out = coef_rows[i, 0:1, :] * misfit
        inner_ref[i, 0:1, :] = jnp.sum(grad_out * head_out, 0, keepdims=True)
        grad_turned = grad_out.astype(BF16)
        grad_turned_ref[:, rows] = grad_turned
        grad_ref[rows, :] = grad_turned.T
        send_ref[pl.ds(i * PAIR, PAIR), 0:BLOCK, :] = head_out.astype(BF16).T.reshape(
            PAIR, BLOCK, HEAD_DIM
        )
        return carry

    lax.fori_loop(0, TILES, finish, 0)

    rows = [block_row(b) for b in range(BLOCKS)]
    losses = jnp.concatenate([loss_rows[tile, 0:1, at] for tile, at in rows], 0)
    loss_row = group_sums(group, losses)
    high = loss_row.astype(BF16)
    left = loss_row - high.astype(F32)
    middle = left.astype(BF16)
    low = (left - middle.astype(F32)).astype(BF16)
    row = lax.broadcasted_iota(I32, (EXTRA, 128), 0)
    pieces = jnp.zeros((EXTRA, 128), F32)
    for n, piece in enumerate((high, middle, low)):
        pieces = jnp.where(row == n, piece.astype(F32), pieces)
    send_ref[:, BLOCK:, :] = jnp.broadcast_to(pieces.astype(BF16)[None], (BLOCKS, EXTRA, 128))


def run_forward(spans, pairs, mixture, counts, group, second, q_turned, k_hat, span_rows, norms):
    return pl.pallas_call(
        forward_kernel,
        in_specs=[SMEM_SPEC] * 3 + [VMEM_SPEC] * 7,
        out_specs=[VMEM_SPEC] * 4,
        out_shape=[
            shape((BLOCKS, BLOCK + EXTRA, 128), BF16),
            shape((LENGTH, HEAD_DIM), BF16),
            shape((HEAD_DIM, LENGTH), BF16),
            shape((TILES, 1, TILE), F32),
        ],
        scratch_shapes=[
            pltpu.VMEM((TILES, 1, TILE), F32),
            pltpu.VMEM((TILES, 1, TILE), F32),
            pltpu.VMEM((HEAD_DIM, LENGTH), BF16),
            pltpu.VMEM((TILES, HEAD_DIM, TILE), F32),
        ],
        compiler_params=pltpu.CompilerParams(vmem_limit_bytes=VMEM_LIMIT),
        name="forward",
    )(spans, pairs, mixture, counts, group, second, q_turned, k_hat, span_rows, norms)


def backward_kernel(
    span_ref, pair_ref,
    recv_ref, gains_ref, q_hat_ref, k_hat_ref, q_turned_ref, k_turned_ref, raw_q_ref, raw_k_ref,
    moments_ref, span_rows_ref, norm_ref, grad_ref, grad_turned_ref, inner_ref,
    send_ref, gain_out_ref,
    grad_q, grad_k, grad_v,
):
    def clear(i, carry):
        grad_q[i] = jnp.zeros((HEAD_DIM, TILE), F32)
        grad_k[tile_at(i), :] = jnp.zeros((TILE, HEAD_DIM), F32)
        grad_v[tile_at(i), :] = jnp.zeros((TILE, HEAD_DIM), F32)
        return carry

    lax.fori_loop(0, TILES, clear, 0)

    def add_pairs(pairs):
        tiles = [
            dot(k_hat_ref[pl.ds(at, KEYS), :], q_turned_ref[:, tile_at(i)]) for i, at, _ in pairs
        ]
        prob_grads = [
            dot(tile_rows(recv_ref, at // BLOCK, 0, KEYS), grad_turned_ref[:, tile_at(i)])
            for i, at, _ in pairs
        ]
        tiles = [
            softmax_tile(tile, span_rows_ref, norm_ref, i, mask_at)
            for tile, (i, _, mask_at) in zip(tiles, pairs)
        ]
        values = [
            dot(tile.astype(BF16), grad_ref[tile_at(i), :]) for tile, (i, _, _) in zip(tiles, pairs)
        ]
        tiles = [
            (tile * (prob - inner_ref[i, 0:1, :]) * SCALE).astype(BF16)
            for tile, prob, (i, _, _) in zip(tiles, prob_grads, pairs)
        ]
        keys = [dot(tile, q_hat_ref[tile_at(i), :]) for tile, (i, _, _) in zip(tiles, pairs)]
        queries = [
            dot(k_turned_ref[:, pl.ds(at, KEYS)], tile) for tile, (_, at, _) in zip(tiles, pairs)
        ]
        for value, key, query, (i, at, _) in zip(values, keys, queries, pairs):
            grad_v[pl.ds(at, KEYS), :] += value
            grad_k[pl.ds(at, KEYS), :] += key
            grad_q[i] += query

    each_pairs(span_ref[0, TILES], BACKWARD_UNROLL, pair_ref, add_pairs)

    gains = jnp.concatenate([gains_ref[...], jnp.zeros((6, HEAD_DIM), F32)], 0).T

    def norm_backward(i, n, grad_hat, raw_ref):
        mean = moments_ref[i, 2 * n : 2 * n + 1, :]
        inverse = moments_ref[i, 2 * n + 1 : 2 * n + 2, :]
        normed = (raw_ref[:, tile_at(i)].astype(F32) - mean) * inverse
        grad_normed = grad_hat * gains[:, n : n + 1]
        inner = mean_down(grad_normed * normed)
        grad_in = inverse * (grad_normed - mean_down(grad_normed) - normed * inner)
        send_ref[pl.ds(i * PAIR, PAIR), n * BLOCK : (n + 1) * BLOCK, :] = grad_in.astype(
            BF16
        ).T.reshape(PAIR, BLOCK, HEAD_DIM)
        grad_gain = grad_hat * normed
        return sum(grad_gain[:, c : c + 128] for c in range(0, TILE, 128))

    def finish(i, gain_sums):
        gain_q, gain_k = gain_sums
        gain_q = gain_q + norm_backward(i, 0, grad_q[i], raw_q_ref)
        gain_k = gain_k + norm_backward(i, 1, grad_k[tile_at(i), :].T, raw_k_ref)
        send_ref[pl.ds(i * PAIR, PAIR), 2 * BLOCK :, :] = (
            grad_v[tile_at(i), :].astype(BF16).reshape(PAIR, BLOCK, HEAD_DIM)
        )
        return gain_q, gain_k

    zero = jnp.zeros((HEAD_DIM, 128), F32)
    gain_q, gain_k = lax.fori_loop(0, TILES, finish, (zero, zero))
    gain_out_ref[0:1, :] = jnp.sum(gain_q.T, 0, keepdims=True)
    gain_out_ref[1:2, :] = jnp.sum(gain_k.T, 0, keepdims=True)


def run_backward(spans, pairs, *arrays):
    return pl.pallas_call(
        backward_kernel,
        in_specs=[SMEM_SPEC] * 2 + [VMEM_SPEC] * len(arrays),
        out_specs=[VMEM_SPEC] * 2,
        out_shape=[shape((BLOCKS, 3 * BLOCK, 128), BF16), shape((2, HEAD_DIM), F32)],
        scratch_shapes=[
            pltpu.VMEM((TILES, HEAD_DIM, TILE), F32),
            pltpu.VMEM((LENGTH, HEAD_DIM), F32),
            pltpu.VMEM((LENGTH, HEAD_DIM), F32),
        ],
        compiler_params=pltpu.CompilerParams(vmem_limit_bytes=VMEM_LIMIT),
        name="backward",
    )(spans, pairs, *arrays)


def over_packs(value):
    moved = [value]
    for shift in range(1, PACKS):
        pairs = [(i, (i + shift) % PACKS) for i in range(PACKS)]
        moved.append(lax.ppermute(value, "pack", pairs))
    return moved


def exchange(slab):
    return lax.all_to_all(slab, "seq", split_axis=0, concat_axis=0, tiled=True)


def on_device(
    query_rows, key_rows, value_rows, target_rows, norm_gains, segment_ids, group_labels, mixture
):
    gains = norm_gains.reshape(2, HEAD_DIM)
    first = exchange(pack_rows((query_rows, key_rows), segment_ids, "pack_first"))
    second = exchange(pack_rows((value_rows, target_rows), None, "pack_second"))

    group, own_counts, spans, pairs, span_rows = run_groups(group_labels, first)
    counts = jnp.concatenate(over_packs(own_counts), 0)
    q_hat, k_hat, q_turned, k_turned, raw_q, raw_k, moments, norms = run_stats(
        spans, first, gains, span_rows
    )
    send, *grads = run_forward(
        spans, pairs, mixture, counts, group, second, q_turned, k_hat, span_rows, norms
    )
    back = exchange(send)
    send, gain_part = run_backward(
        spans, pairs, second, gains, q_hat, k_hat, q_turned, k_turned, raw_q, raw_k,
        moments, span_rows, norms, *grads,
    )
    last = exchange(send)
    (attended,) = unpack_rows(back, 1, "unpack_first")
    losses = jnp.sum(back[:, BLOCK : BLOCK + 3, :GROUPS].astype(F32), (0, 1))
    group_total = sum(over_packs(losses))
    group_loss = group_total / (jnp.sum(counts, 0)[:GROUPS] * (HEADS * HEAD_DIM))
    shares = mixture / jnp.sum(mixture)
    raised = shares * jnp.exp(ETA * group_loss)
    new_mixture = raised / jnp.sum(raised)
    grad_gains = sum(over_packs(gain_part)).reshape(2, 1, HEAD_DIM)
    grad_query, grad_key, grad_value = unpack_rows(last, 3, "unpack_last")
    return (attended, grad_query, grad_key, grad_value, grad_gains, new_mixture)


def solution(mesh):
    rows = P("pack", "seq", None)
    gains = P(None, "seq", None)
    return jax.shard_map(
        on_device,
        mesh=mesh,
        in_specs=(rows, rows, rows, rows, gains, P("pack", "seq"), P("pack", None), P()),
        out_specs=(rows, rows, rows, rows, gains, P()),
        check_vma=False,
    )
```

```python
import functools

import jax
import jax.numpy as jnp
from jax import lax
from jax.experimental import pallas as pl
from jax.experimental.pallas import tpu as pltpu
from jax.sharding import PartitionSpec as P

HEADS = 32
HEAD_DIM = 128
IMAGES = 16
GROUPS = 8
PACKS = 4
LENGTH = 4096

NEG = -1e30
EPS = 1e-06
ETA = 2.0
SCALE = HEAD_DIM ** (-0.5)
EXP_SCALE = SCALE * 1.4426950408889634

BLOCK = 128
BLOCKS = LENGTH // BLOCK
TILE = 256
TILES = LENGTH // TILE
PAIR = TILE // BLOCK
KEYS = 256
UNROLL = 4
MOST_PAIRS = (LENGTH * (1024 // TILE + 2) + TILES * (BLOCK - 1 + KEYS - 1)) // KEYS + UNROLL
SAFE_LOGIT = 70.0
EXTRA = 16
VMEM_LIMIT = 56 * 1024 * 1024

BF16 = jnp.bfloat16
F32 = jnp.float32
I32 = jnp.int32

VMEM_SPEC = pl.BlockSpec(memory_space=pltpu.VMEM)
SMEM_SPEC = pl.BlockSpec(memory_space=pltpu.SMEM)
ANY_SPEC = pl.BlockSpec(memory_space=pl.ANY)


def shape(dims, dtype):
    return jax.ShapeDtypeStruct(dims, dtype)


def head_columns(h):
    return pl.ds(h * HEAD_DIM, HEAD_DIM)


def pack_kernel(count, *refs):
    row_refs, extra_refs, (out_ref, sems) = refs[:count], refs[count:-2], refs[-2:]
    copies = []
    for n, ref in enumerate(row_refs):
        for h in range(HEADS):
            copy = pltpu.make_async_copy(
                ref.at[0, :, head_columns(h)],
                out_ref.at[h, pl.ds(n * BLOCK, BLOCK), :],
                sems.at[n, h],
            )
            copy.start()
            copies.append(copy)
    for extra_ref in extra_refs:
        tile = extra_ref[...].astype(F32)
        left = jnp.zeros((EXTRA - tile.shape[0], 128), F32)
        tile = jnp.concatenate([tile, left], 0).astype(BF16)
        out_ref[:, len(row_refs) * BLOCK :, :] = jnp.broadcast_to(tile[None], (HEADS, EXTRA, 128))
    for copy in copies:
        copy.wait()


def pack_rows(rows, extra, name):
    extras = () if extra is None else (extra,)
    return pl.pallas_call(
        functools.partial(pack_kernel, len(rows)),
        in_specs=[ANY_SPEC] * len(rows) + [VMEM_SPEC] * len(extras),
        out_specs=VMEM_SPEC,
        out_shape=shape((HEADS, len(rows) * BLOCK + EXTRA * len(extras), 128), BF16),
        scratch_shapes=[pltpu.SemaphoreType.DMA((len(rows), HEADS))],
        compiler_params=pltpu.CompilerParams(vmem_limit_bytes=VMEM_LIMIT),
        name=name,
    )(*rows, *extras)


def unpack_kernel(in_ref, *refs):
    *row_refs, sems = refs
    copies = []
    for n, ref in enumerate(row_refs):
        for h in range(HEADS):
            copy = pltpu.make_async_copy(
                in_ref.at[h, pl.ds(n * BLOCK, BLOCK), :],
                ref.at[0, :, head_columns(h)],
                sems.at[n, h],
            )
            copy.start()
            copies.append(copy)
    for copy in copies:
        copy.wait()


def unpack_rows(slab, count, name):
    return pl.pallas_call(
        unpack_kernel,
        in_specs=[VMEM_SPEC],
        out_specs=[ANY_SPEC] * count,
        out_shape=[shape((1, BLOCK, HEADS * HEAD_DIM), BF16)] * count,
        scratch_shapes=[pltpu.SemaphoreType.DMA((count, HEADS))],
        compiler_params=pltpu.CompilerParams(vmem_limit_bytes=VMEM_LIMIT),
        name=name,
    )(slab)


def dot(a, b, contract=((1,), (0,))):
    return lax.dot_general(a, b, (contract, ((), ())), preferred_element_type=F32)


def tile_rows(ref, i, part, size=TILE):
    blocks = size // BLOCK
    return ref[pl.ds(i, blocks), part * BLOCK : (part + 1) * BLOCK, :].reshape(size, HEAD_DIM)


def tile_at(i, size=TILE):
    return pl.ds(pl.multiple_of(i * size, size), size)


def mean_down(values):
    return jnp.sum(values, 0, keepdims=True) * (1.0 / HEAD_DIM)


def block_row(b):
    return b // PAIR, slice((b % PAIR) * BLOCK, (b % PAIR + 1) * BLOCK)


def group_sums(group, values):
    lane = lax.broadcasted_iota(I32, (1, 128), 1)
    sums = jnp.zeros((1, 128), F32)
    for g in range(GROUPS):
        part = jnp.sum(jnp.where(group == float(g), values, 0.0), 0, keepdims=True)
        sums = jnp.where(lane == g, jnp.sum(part, 1, keepdims=True), sums)
    return sums


def key_mask(span_rows_ref, i, start, step):
    first = span_rows_ref[i, 0:1, :] - start
    count = span_rows_ref[i, 1:2, :]
    row = lax.broadcasted_iota(I32, (step, TILE), 0)
    return (row - first).astype(jnp.uint32) < count.astype(jnp.uint32)


def masked(scores, span_rows_ref, i, mask_at):
    return jnp.where(key_mask(span_rows_ref, i, mask_at, KEYS), scores, NEG)


def each_pairs(total, pair_ref, body):
    def some(n, carry):
        pairs = []
        for u in range(UNROLL):
            p = n * UNROLL + u
            at = pl.multiple_of(pair_ref[1, p], BLOCK)
            pairs.append((p, pair_ref[0, p], at, pair_ref[2, p]))
        body(pairs)
        return carry

    lax.fori_loop(0, (total + UNROLL - 1) // UNROLL, some, 0)


def find_pairs(seg_all, starts, pair_ref, span_rows_ref):
    for s in range(IMAGES + 1):
        starts[s] = jnp.sum((seg_all < float(s)).astype(F32)).astype(I32)
    first = jnp.zeros((BLOCKS, 128), I32)
    count = jnp.zeros((BLOCKS, 128), I32)
    for s in range(IMAGES):
        here = seg_all == float(s)
        first = jnp.where(here, starts[s], first)
        count = jnp.where(here, starts[s + 1] - starts[s], count)
    for b in range(BLOCKS):
        tile, at = block_row(b)
        span_rows_ref[tile, 0:1, at] = first[b : b + 1, :]
        span_rows_ref[tile, 1:2, at] = count[b : b + 1, :]

    def span(i, total):
        low, high = jnp.int32(0), jnp.int32(LENGTH)
        for s in range(1, IMAGES):
            low = jnp.where(starts[s] <= i * TILE, starts[s], low)
        for s in range(IMAGES - 1, 0, -1):
            high = jnp.where(starts[s] > i * TILE + TILE - 1, starts[s], high)
        low = (low // BLOCK) * BLOCK
        steps = (high - low + KEYS - 1) // KEYS
        low = jnp.minimum(low, LENGTH - steps * KEYS)

        def add(j, carry):
            pair_ref[0, total + j] = i
            pair_ref[1, total + j] = low + j * KEYS
            pair_ref[2, total + j] = low + j * KEYS
            return carry

        lax.fori_loop(0, steps, add, 0)
        return total + steps

    total = lax.fori_loop(0, TILES, span, jnp.int32(0))
    for u in range(UNROLL):
        pair_ref[0, total + u] = 0
        pair_ref[1, total + u] = 0
        pair_ref[2, total + u] = -(1 << 20)
    return total


def attend_kernel(
    recv_ref, gains_ref,
    pair_ref, total_ref, span_rows_ref,
    q_hat_ref, k_hat_ref, q_turned_ref, k_turned_ref, raw_q_ref, raw_k_ref, moments_ref, norm_ref,
    out_ref,
    starts, v_turned, terms, fold,
):
    total = find_pairs(recv_ref[:, 3 * BLOCK, :].astype(F32), starts, pair_ref, span_rows_ref)
    total_ref[0] = total
    gains = jnp.concatenate([gains_ref[...], jnp.zeros((6, HEAD_DIM), F32)], 0).T

    def prepare(i, most):
        rows = tile_at(i)
        v_turned[:, rows] = tile_rows(recv_ref, i * PAIR, 2).T
        outs = ((q_hat_ref, q_turned_ref, raw_q_ref), (k_hat_ref, k_turned_ref, raw_k_ref))
        sizes = []
        for n, (hat_ref, turned_ref, raw_ref) in enumerate(outs):
            raw = tile_rows(recv_ref, i * PAIR, n).T
            raw_ref[:, rows] = raw
            values = raw.astype(F32)
            mean = mean_down(values)
            centre = values - mean
            inverse = lax.rsqrt(mean_down(centre * centre) + EPS)
            moments_ref[i, 2 * n : 2 * n + 1, :] = mean
            moments_ref[i, 2 * n + 1 : 2 * n + 2, :] = inverse
            hat = centre * inverse * gains[:, n : n + 1]
            sizes.append(jnp.maximum(most[n], mean_down(hat * hat)))
            hat = hat.astype(BF16)
            turned_ref[:, rows] = hat
            hat_ref[rows, :] = hat.T
        out_ref[i] = jnp.zeros((HEAD_DIM, TILE), F32)
        norm_ref[i] = jnp.zeros((2, TILE), F32)
        fold[i] = jnp.zeros((8, TILE), F32)
        return tuple(sizes)

    zero = jnp.zeros((1, TILE), F32)
    most_q, most_k = lax.fori_loop(0, TILES, prepare, (zero, zero))
    bound = jnp.max(most_q) * jnp.max(most_k) * HEAD_DIM

    def scores_of(pairs):
        tiles = [
            dot(k_hat_ref[pl.ds(at, KEYS), :], q_turned_ref[:, tile_at(i)]) for _, i, at, _ in pairs
        ]
        return [
            masked(tile, span_rows_ref, i, mask_at)
            for tile, (_, i, _, mask_at) in zip(tiles, pairs)
        ]

    @pl.when(jnp.logical_not(bound <= SAFE_LOGIT * SAFE_LOGIT))
    def _():
        def clear(i, carry):
            fold[i] = jnp.full((8, TILE), NEG, F32)
            return carry

        lax.fori_loop(0, TILES, clear, 0)

        def top_pairs(pairs):
            for tile, (_, i, _, _) in zip(scores_of(pairs), pairs):
                top = jnp.max(tile.reshape(KEYS // 8, 8, TILE), 0)
                fold[i] = jnp.maximum(fold[i], top)

        each_pairs(total, pair_ref, top_pairs)

        def finish(i, carry):
            norm_ref[i, 0:1, :] = jnp.max(fold[i], 0, keepdims=True) * EXP_SCALE
            fold[i] = jnp.zeros((8, TILE), F32)
            return carry

        lax.fori_loop(0, TILES, finish, 0)

    def exp_pairs(pairs):
        sums = []
        for tile, (p, i, _, _) in zip(scores_of(pairs), pairs):
            tile = jnp.exp2(tile * EXP_SCALE - norm_ref[i, 0:1, :])
            terms[p] = tile
            sums.append(jnp.sum(tile.reshape(KEYS // 8, 8, TILE), 0))
        for part, (_, i, _, _) in zip(sums, pairs):
            fold[i] += part

    each_pairs(total, pair_ref, exp_pairs)

    def invert(i, carry):
        norm_ref[i, 1:2, :] = 1.0 / jnp.sum(fold[i], 0, keepdims=True)
        return carry

    lax.fori_loop(0, TILES, invert, 0)

    def out_pairs(pairs):
        tiles = [(terms[p] * norm_ref[i, 1:2, :]).astype(BF16) for p, i, _, _ in pairs]
        tiles = [
            dot(v_turned[:, pl.ds(at, KEYS)], tile) for tile, (_, _, at, _) in zip(tiles, pairs)
        ]
        for tile, (_, i, _, _) in zip(tiles, pairs):
            out_ref[i] += tile

    each_pairs(total, pair_ref, out_pairs)


def run_attend(received, gains):
    return pl.pallas_call(
        attend_kernel,
        in_specs=[VMEM_SPEC] * 2,
        out_specs=[SMEM_SPEC] * 2 + [VMEM_SPEC] * 10,
        out_shape=[
            shape((3, MOST_PAIRS), I32),
            shape((1,), I32),
            shape((TILES, 2, TILE), I32),
            shape((LENGTH, HEAD_DIM), BF16),
            shape((LENGTH, HEAD_DIM), BF16),
            shape((HEAD_DIM, LENGTH), BF16),
            shape((HEAD_DIM, LENGTH), BF16),
            shape((HEAD_DIM, LENGTH), BF16),
            shape((HEAD_DIM, LENGTH), BF16),
            shape((TILES, 4, TILE), F32),
            shape((TILES, 2, TILE), F32),
            shape((TILES, HEAD_DIM, TILE), F32),
        ],
        scratch_shapes=[
            pltpu.SMEM((IMAGES + 1,), I32),
            pltpu.VMEM((HEAD_DIM, LENGTH), BF16),
            pltpu.VMEM((MOST_PAIRS, KEYS, TILE), F32),
            pltpu.VMEM((TILES, 8, TILE), F32),
        ],
        compiler_params=pltpu.CompilerParams(vmem_limit_bytes=VMEM_LIMIT),
        name="attend",
    )(received, gains)


def loss_kernel(
    labels_ref, mixture_ref,
    recv_ref, out_ref,
    send_ref, grad_ref, grad_turned_ref, inner_ref, counts_ref,
    coef_rows, loss_rows,
):
    seg_all = recv_ref[:, BLOCK, :].astype(F32)
    group = jnp.zeros((BLOCKS, 128), F32)
    for s in range(IMAGES):
        group = jnp.where(seg_all == float(s), labels_ref[0, s].astype(F32), group)
    others = [recv_ref[:, BLOCK + 1 + p, :].astype(F32) for p in range(PACKS)]
    total_mix = mixture_ref[0]
    for g in range(1, GROUPS):
        total_mix = total_mix + mixture_ref[g]
    lane = lax.broadcasted_iota(I32, (1, 128), 1)
    coef = jnp.zeros((BLOCKS, 128), F32)
    count_row = jnp.zeros((1, 128), F32)
    for g in range(GROUPS):
        hits = sum((other == float(g)).astype(F32) for other in others)
        count = jnp.sum(jnp.sum(hits, 0, keepdims=True), 1, keepdims=True)
        share = jnp.full((1, 1), mixture_ref[g], F32) / total_mix
        coef = jnp.where(group == float(g), share / (count * (HEADS * HEAD_DIM)), coef)
        count_row = jnp.where(lane == g, count, count_row)
    counts_ref[...] = count_row
    for b in range(BLOCKS):
        tile, at = block_row(b)
        coef_rows[tile, 0:1, at] = coef[b : b + 1, :]

    def finish(i, carry):
        rows = tile_at(i)
        head_out = out_ref[i]
        misfit = head_out - tile_rows(recv_ref, i * PAIR, 0).T.astype(F32)
        loss_rows[i, 0:1, :] = 0.5 * jnp.sum(misfit * misfit, 0, keepdims=True)
        grad_out = coef_rows[i, 0:1, :] * misfit
        inner_ref[i, 0:1, :] = jnp.sum(grad_out * head_out, 0, keepdims=True)
        grad_turned = grad_out.astype(BF16)
        grad_turned_ref[:, rows] = grad_turned
        grad_ref[rows, :] = grad_turned.T
        send_ref[pl.ds(i * PAIR, PAIR), 0:BLOCK, :] = head_out.astype(BF16).T.reshape(
            PAIR, BLOCK, HEAD_DIM
        )
        return carry

    lax.fori_loop(0, TILES, finish, 0)

    rows = [block_row(b) for b in range(BLOCKS)]
    losses = jnp.concatenate([loss_rows[tile, 0:1, at] for tile, at in rows], 0)
    loss_row = group_sums(group, losses)
    high = loss_row.astype(BF16)
    left = loss_row - high.astype(F32)
    middle = left.astype(BF16)
    low = (left - middle.astype(F32)).astype(BF16)
    row = lax.broadcasted_iota(I32, (EXTRA, 128), 0)
    pieces = jnp.zeros((EXTRA, 128), F32)
    for n, piece in enumerate((high, middle, low)):
        pieces = jnp.where(row == n, piece.astype(F32), pieces)
    send_ref[:, BLOCK:, :] = jnp.broadcast_to(pieces.astype(BF16)[None], (BLOCKS, EXTRA, 128))


def run_loss(labels, mixture, second, head_out):
    return pl.pallas_call(
        loss_kernel,
        in_specs=[SMEM_SPEC] * 2 + [VMEM_SPEC] * 2,
        out_specs=[VMEM_SPEC] * 5,
        out_shape=[
            shape((BLOCKS, BLOCK + EXTRA, 128), BF16),
            shape((LENGTH, HEAD_DIM), BF16),
            shape((HEAD_DIM, LENGTH), BF16),
            shape((TILES, 1, TILE), F32),
            shape((1, 128), F32),
        ],
        scratch_shapes=[pltpu.VMEM((TILES, 1, TILE), F32), pltpu.VMEM((TILES, 1, TILE), F32)],
        compiler_params=pltpu.CompilerParams(vmem_limit_bytes=VMEM_LIMIT),
        name="loss",
    )(labels, mixture, second, head_out)


def backward_kernel(
    pair_ref, total_ref,
    recv_ref, gains_ref, q_hat_ref, k_hat_ref, q_turned_ref, k_turned_ref, raw_q_ref, raw_k_ref,
    moments_ref, span_rows_ref, norm_ref, grad_ref, grad_turned_ref, inner_ref,
    send_ref, gain_out_ref,
    grad_q, grad_k, grad_v,
):
    def clear(i, carry):
        grad_q[i] = jnp.zeros((HEAD_DIM, TILE), F32)
        grad_k[tile_at(i), :] = jnp.zeros((TILE, HEAD_DIM), F32)
        grad_v[tile_at(i), :] = jnp.zeros((TILE, HEAD_DIM), F32)
        return carry

    lax.fori_loop(0, TILES, clear, 0)

    def add_pairs(pairs):
        tiles = [
            dot(k_hat_ref[pl.ds(at, KEYS), :], q_turned_ref[:, tile_at(i)]) for _, i, at, _ in pairs
        ]
        prob_grads = [
            dot(tile_rows(recv_ref, at // BLOCK, 2, KEYS), grad_turned_ref[:, tile_at(i)])
            for _, i, at, _ in pairs
        ]
        tiles = [
            jnp.exp2(
                masked(tile, span_rows_ref, i, mask_at) * EXP_SCALE - norm_ref[i, 0:1, :]
            ) * norm_ref[i, 1:2, :]
            for tile, (_, i, _, mask_at) in zip(tiles, pairs)
        ]
        values = [
            dot(tile.astype(BF16), grad_ref[tile_at(i), :])
            for tile, (_, i, _, _) in zip(tiles, pairs)
        ]
        tiles = [
            (tile * (prob - inner_ref[i, 0:1, :]) * SCALE).astype(BF16)
            for tile, prob, (_, i, _, _) in zip(tiles, prob_grads, pairs)
        ]
        keys = [dot(tile, q_hat_ref[tile_at(i), :]) for tile, (_, i, _, _) in zip(tiles, pairs)]
        queries = [
            dot(k_turned_ref[:, pl.ds(at, KEYS)], tile) for tile, (_, _, at, _) in zip(tiles, pairs)
        ]
        for value, key, query, (_, i, at, _) in zip(values, keys, queries, pairs):
            grad_v[pl.ds(at, KEYS), :] += value
            grad_k[pl.ds(at, KEYS), :] += key
            grad_q[i] += query

    each_pairs(total_ref[0], pair_ref, add_pairs)

    gains = jnp.concatenate([gains_ref[...], jnp.zeros((6, HEAD_DIM), F32)], 0).T

    def norm_backward(i, n, grad_hat, raw_ref):
        mean = moments_ref[i, 2 * n : 2 * n + 1, :]
        inverse = moments_ref[i, 2 * n + 1 : 2 * n + 2, :]
        normed = (raw_ref[:, tile_at(i)].astype(F32) - mean) * inverse
        grad_normed = grad_hat * gains[:, n : n + 1]
        inner = mean_down(grad_normed * normed)
        grad_in = inverse * (grad_normed - mean_down(grad_normed) - normed * inner)
        send_ref[pl.ds(i * PAIR, PAIR), n * BLOCK : (n + 1) * BLOCK, :] = grad_in.astype(
            BF16
        ).T.reshape(PAIR, BLOCK, HEAD_DIM)
        grad_gain = grad_hat * normed
        return sum(grad_gain[:, c : c + 128] for c in range(0, TILE, 128))

    def finish(i, gain_sums):
        gain_q, gain_k = gain_sums
        gain_q = gain_q + norm_backward(i, 0, grad_q[i], raw_q_ref)
        gain_k = gain_k + norm_backward(i, 1, grad_k[tile_at(i), :].T, raw_k_ref)
        send_ref[pl.ds(i * PAIR, PAIR), 2 * BLOCK :, :] = (
            grad_v[tile_at(i), :].astype(BF16).reshape(PAIR, BLOCK, HEAD_DIM)
        )
        return gain_q, gain_k

    zero = jnp.zeros((HEAD_DIM, 128), F32)
    gain_q, gain_k = lax.fori_loop(0, TILES, finish, (zero, zero))
    gain_out_ref[0:1, :] = jnp.sum(gain_q.T, 0, keepdims=True)
    gain_out_ref[1:2, :] = jnp.sum(gain_k.T, 0, keepdims=True)


def run_backward(pairs, total, *arrays):
    return pl.pallas_call(
        backward_kernel,
        in_specs=[SMEM_SPEC] * 2 + [VMEM_SPEC] * len(arrays),
        out_specs=[VMEM_SPEC] * 2,
        out_shape=[shape((BLOCKS, 3 * BLOCK, 128), BF16), shape((2, HEAD_DIM), F32)],
        scratch_shapes=[
            pltpu.VMEM((TILES, HEAD_DIM, TILE), F32),
            pltpu.VMEM((LENGTH, HEAD_DIM), F32),
            pltpu.VMEM((LENGTH, HEAD_DIM), F32),
        ],
        compiler_params=pltpu.CompilerParams(vmem_limit_bytes=VMEM_LIMIT),
        name="backward",
    )(pairs, total, *arrays)


def over_packs(value):
    moved = [value]
    for shift in range(1, PACKS):
        pairs = [(i, (i + shift) % PACKS) for i in range(PACKS)]
        moved.append(lax.ppermute(value, "pack", pairs))
    return moved


def exchange(slab):
    return lax.all_to_all(slab, "seq", split_axis=0, concat_axis=0, tiled=True)


def on_device(
    query_rows, key_rows, value_rows, target_rows, norm_gains, segment_ids, group_labels, mixture
):
    gains = norm_gains.reshape(2, HEAD_DIM)
    first = exchange(pack_rows((query_rows, key_rows, value_rows), segment_ids, "pack_first"))

    image_hot = segment_ids[0][:, None] == jnp.arange(IMAGES, dtype=I32)[None, :]
    labels = jnp.sum(jnp.where(image_hot, group_labels[0][None, :], 0), 1)[None, :]
    extra = jnp.concatenate([segment_ids.astype(F32), *over_packs(labels.astype(F32))], 0)
    second = exchange(pack_rows((target_rows,), extra, "pack_second"))

    pairs, total, span_rows, *hats, moments, norms, head_out = run_attend(first, gains)
    send, *grads, counts = run_loss(group_labels, mixture, second, head_out)
    back = exchange(send)
    send, gain_part = run_backward(
        pairs, total, first, gains, *hats, moments, span_rows, norms, *grads
    )
    last = exchange(send)
    (attended,) = unpack_rows(back, 1, "unpack_first")
    losses = jnp.sum(back[:, BLOCK : BLOCK + 3, :GROUPS].astype(F32), (0, 1))
    group_total = sum(over_packs(losses))
    group_loss = group_total / (counts[0, :GROUPS] * (HEADS * HEAD_DIM))
    shares = mixture / jnp.sum(mixture)
    raised = shares * jnp.exp(ETA * group_loss)
    new_mixture = raised / jnp.sum(raised)
    grad_gains = sum(over_packs(gain_part)).reshape(2, 1, HEAD_DIM)
    grad_query, grad_key, grad_value = unpack_rows(last, 3, "unpack_last")
    return (attended, grad_query, grad_key, grad_value, grad_gains, new_mixture)


def solution(mesh):
    rows = P("pack", "seq", None)
    gains = P(None, "seq", None)
    return jax.shard_map(
        on_device,
        mesh=mesh,
        in_specs=(rows, rows, rows, rows, gains, P("pack", "seq"), P("pack", None), P()),
        out_specs=(rows, rows, rows, rows, gains, P()),
        check_vma=False,
    )
```

```python
import functools

import jax
import jax.numpy as jnp
from jax import lax
from jax.experimental import pallas as pl
from jax.experimental.pallas import tpu as pltpu
from jax.sharding import PartitionSpec as P

HEADS = 32
HEAD_DIM = 128
IMAGES = 16
GROUPS = 8
PACKS = 4
LENGTH = 4096

NEG = -1e30
EPS = 1e-06
ETA = 2.0
SCALE = HEAD_DIM ** (-0.5)
EXP_SCALE = SCALE * 1.4426950408889634

BLOCK = 128
BLOCKS = LENGTH // BLOCK
TILE = 256
TILES = LENGTH // TILE
PAIR = TILE // BLOCK
KEYS = 256
UNROLL = 6
MOST_PAIRS = (LENGTH * (1024 // TILE + 1) + TILES * (BLOCK - 1 + KEYS - 1)) // KEYS
MOST_STEPS = MOST_PAIRS // UNROLL + 1
MOST_PAIRS = MOST_STEPS * UNROLL
RING = 4
SAFE_LOGIT = 70.0
EXTRA = 16
VMEM_LIMIT = 56 * 1024 * 1024

BF16 = jnp.bfloat16
F32 = jnp.float32
I32 = jnp.int32

VMEM_SPEC = pl.BlockSpec(memory_space=pltpu.VMEM)
SMEM_SPEC = pl.BlockSpec(memory_space=pltpu.SMEM)
ANY_SPEC = pl.BlockSpec(memory_space=pl.ANY)


def shape(dims, dtype):
    return jax.ShapeDtypeStruct(dims, dtype)


def head_columns(h):
    return pl.ds(h * HEAD_DIM, HEAD_DIM)


def pack_kernel(count, *refs):
    row_refs, extra_refs, (out_ref, sems) = refs[:count], refs[count:-2], refs[-2:]
    copies = []
    for n, ref in enumerate(row_refs):
        for h in range(HEADS):
            copy = pltpu.make_async_copy(
                ref.at[0, :, head_columns(h)],
                out_ref.at[h, pl.ds(n * BLOCK, BLOCK), :],
                sems.at[n, h],
            )
            copy.start()
            copies.append(copy)
    for extra_ref in extra_refs:
        tile = extra_ref[...].astype(F32)
        left = jnp.zeros((EXTRA - tile.shape[0], 128), F32)
        tile = jnp.concatenate([tile, left], 0).astype(BF16)
        out_ref[:, len(row_refs) * BLOCK :, :] = jnp.broadcast_to(tile[None], (HEADS, EXTRA, 128))
    for copy in copies:
        copy.wait()


def pack_rows(rows, extra, name):
    extras = () if extra is None else (extra,)
    return pl.pallas_call(
        functools.partial(pack_kernel, len(rows)),
        in_specs=[ANY_SPEC] * len(rows) + [VMEM_SPEC] * len(extras),
        out_specs=VMEM_SPEC,
        out_shape=shape((HEADS, len(rows) * BLOCK + EXTRA * len(extras), 128), BF16),
        scratch_shapes=[pltpu.SemaphoreType.DMA((len(rows), HEADS))],
        compiler_params=pltpu.CompilerParams(vmem_limit_bytes=VMEM_LIMIT),
        name=name,
    )(*rows, *extras)


def unpack_kernel(in_ref, *refs):
    *row_refs, sems = refs
    copies = []
    for n, ref in enumerate(row_refs):
        for h in range(HEADS):
            copy = pltpu.make_async_copy(
                in_ref.at[h, pl.ds(n * BLOCK, BLOCK), :],
                ref.at[0, :, head_columns(h)],
                sems.at[n, h],
            )
            copy.start()
            copies.append(copy)
    for copy in copies:
        copy.wait()


def unpack_rows(slab, count, name):
    return pl.pallas_call(
        unpack_kernel,
        in_specs=[VMEM_SPEC],
        out_specs=[ANY_SPEC] * count,
        out_shape=[shape((1, BLOCK, HEADS * HEAD_DIM), BF16)] * count,
        scratch_shapes=[pltpu.SemaphoreType.DMA((count, HEADS))],
        compiler_params=pltpu.CompilerParams(vmem_limit_bytes=VMEM_LIMIT),
        name=name,
    )(slab)


def dot(a, b, contract=((1,), (0,))):
    return lax.dot_general(a, b, (contract, ((), ())), preferred_element_type=F32)


def tile_rows(ref, i, part, size=TILE):
    blocks = size // BLOCK
    return ref[pl.ds(i, blocks), part * BLOCK : (part + 1) * BLOCK, :].reshape(size, HEAD_DIM)


def tile_at(i, size=TILE):
    return pl.ds(pl.multiple_of(i * size, size), size)


def mean_down(values):
    return jnp.sum(values, 0, keepdims=True) * (1.0 / HEAD_DIM)


def block_row(b):
    return b // PAIR, slice((b % PAIR) * BLOCK, (b % PAIR + 1) * BLOCK)


def group_sums(group, values):
    lane = lax.broadcasted_iota(I32, (1, 128), 1)
    sums = jnp.zeros((1, 128), F32)
    for g in range(GROUPS):
        part = jnp.sum(jnp.where(group == float(g), values, 0.0), 0, keepdims=True)
        sums = jnp.where(lane == g, jnp.sum(part, 1, keepdims=True), sums)
    return sums


def key_mask(span_rows_ref, i, start, step):
    first = span_rows_ref[i, 0:1, :] - start
    count = span_rows_ref[i, 1:2, :]
    row = lax.broadcasted_iota(I32, (step, TILE), 0)
    return (row - first).astype(jnp.uint32) < count.astype(jnp.uint32)


def masked(scores, span_rows_ref, i, mask_at):
    return jnp.where(key_mask(span_rows_ref, i, mask_at, KEYS), scores, NEG)


def pair_steps(total):
    return (total + UNROLL - 1) // UNROLL


def each_pairs(total, pair_ref, body):
    def some(n, carry):
        pairs = []
        for u in range(UNROLL):
            p = n * UNROLL + u
            at = pl.multiple_of(pair_ref[1, p], BLOCK)
            pairs.append((p, pair_ref[0, p], at, pair_ref[2, p]))
        body(n, pairs)
        return carry

    lax.fori_loop(0, pair_steps(total), some, 0)


def softmax_tile(scores, span_rows_ref, norm_ref, i, mask_at):
    scores = masked(scores, span_rows_ref, i, mask_at)
    return jnp.exp2(scores * EXP_SCALE - norm_ref[i, 0:1, :]) * norm_ref[i, 1:2, :]


def find_pairs(seg_all, starts, pair_ref, span_rows_ref):
    for s in range(IMAGES + 1):
        starts[s] = jnp.sum((seg_all < float(s)).astype(F32)).astype(I32)
    first = jnp.zeros((BLOCKS, 128), I32)
    count = jnp.zeros((BLOCKS, 128), I32)
    for s in range(IMAGES):
        here = seg_all == float(s)
        first = jnp.where(here, starts[s], first)
        count = jnp.where(here, starts[s + 1] - starts[s], count)
    for b in range(BLOCKS):
        tile, at = block_row(b)
        span_rows_ref[tile, 0:1, at] = first[b : b + 1, :]
        span_rows_ref[tile, 1:2, at] = count[b : b + 1, :]

    def span(i, total):
        low, high = jnp.int32(0), jnp.int32(LENGTH)
        for s in range(1, IMAGES):
            low = jnp.where(starts[s] <= i * TILE, starts[s], low)
        for s in range(IMAGES - 1, 0, -1):
            high = jnp.where(starts[s] > i * TILE + TILE - 1, starts[s], high)
        low = (low // BLOCK) * BLOCK
        steps = (high - low + KEYS - 1) // KEYS
        low = jnp.minimum(low, LENGTH - steps * KEYS)

        def add(j, carry):
            pair_ref[0, total + j] = i
            pair_ref[1, total + j] = low + j * KEYS
            pair_ref[2, total + j] = low + j * KEYS
            return carry

        lax.fori_loop(0, steps, add, 0)
        return total + steps

    total = lax.fori_loop(0, TILES, span, jnp.int32(0))
    for u in range(UNROLL):
        pair_ref[0, total + u] = 0
        pair_ref[1, total + u] = 0
        pair_ref[2, total + u] = -(1 << 20)
    return total


def each_tile(what):
    def one(i, carry):
        what(i)
        return carry

    lax.fori_loop(0, TILES, one, 0)


def tile_blocks(i):
    return pl.ds(i * PAIR, PAIR)


def attend_kernel(
    all_ref, gains_ref,
    pair_ref, total_ref, span_rows_ref, *refs,
):
    hat_outs, probs_out, refs = refs[:2], refs[2], refs[3:]
    (moments_ref, norm_ref, out_ref), refs = refs[:3], refs[3:]
    hats, refs = refs[:2], refs[2:]
    q_turned_ref, k_hat_ref = hats
    recv_ref, extra_ref, starts, v_turned, terms, fold, probs, sums = refs[:8]
    in_sems, extra_sem, out_sems, prob_sems = refs[8:]

    def arrival(i):
        return pltpu.make_async_copy(
            all_ref.at[tile_blocks(i), pl.ds(0, 3 * BLOCK), :],
            recv_ref.at[tile_blocks(i)],
            in_sems.at[i],
        )

    def leaving(i, n):
        rows = tile_at(i)
        source, target = (
            (q_turned_ref.at[:, rows], hat_outs[0].at[:, rows]),
            (k_hat_ref.at[rows, :], hat_outs[1].at[rows, :]),
            (sums.at[i], out_ref.at[i]),
        )[n]
        return pltpu.make_async_copy(source, target, out_sems.at[n, i])

    extra = pltpu.make_async_copy(
        all_ref.at[:, pl.ds(3 * BLOCK, EXTRA), :], extra_ref, extra_sem.at[0]
    )
    extra.start()
    each_tile(lambda i: arrival(i).start())
    extra.wait()
    total = find_pairs(extra_ref[:, 0, :].astype(F32), starts, pair_ref, span_rows_ref)
    total_ref[0] = total
    gains = jnp.concatenate([gains_ref[...], jnp.zeros((6, HEAD_DIM), F32)], 0).T

    def prepare(i, most):
        arrival(i).wait()
        rows = tile_at(i)
        v_turned[:, rows] = tile_rows(recv_ref, i * PAIR, 2).T
        sizes = []
        for n in range(2):
            values = tile_rows(recv_ref, i * PAIR, n).T.astype(F32)
            mean = mean_down(values)
            centre = values - mean
            inverse = lax.rsqrt(mean_down(centre * centre) + EPS)
            moments_ref[i, 2 * n : 2 * n + 1, :] = mean
            moments_ref[i, 2 * n + 1 : 2 * n + 2, :] = inverse
            hat = centre * inverse * gains[:, n : n + 1]
            sizes.append(jnp.maximum(most[n], mean_down(hat * hat)))
            if n == 0:
                q_turned_ref[:, rows] = hat.astype(BF16)
            else:
                k_hat_ref[rows, :] = hat.astype(BF16).T
        for n in range(2):
            leaving(i, n).start()
        sums[i] = jnp.zeros((HEAD_DIM, TILE), F32)
        norm_ref[i] = jnp.zeros((2, TILE), F32)
        fold[i] = jnp.zeros((8, TILE), F32)
        return tuple(sizes)

    zero = jnp.zeros((1, TILE), F32)
    most_q, most_k = lax.fori_loop(0, TILES, prepare, (zero, zero), unroll=TILES)
    bound = jnp.max(most_q) * jnp.max(most_k) * HEAD_DIM

    def scores_of(pairs):
        tiles = [
            dot(k_hat_ref[pl.ds(at, KEYS), :], q_turned_ref[:, tile_at(i)]) for _, i, at, _ in pairs
        ]
        return [
            masked(tile, span_rows_ref, i, mask_at)
            for tile, (_, i, _, mask_at) in zip(tiles, pairs)
        ]

    @pl.when(jnp.logical_not(bound <= SAFE_LOGIT * SAFE_LOGIT))
    def _():
        def clear(i, carry):
            fold[i] = jnp.full((8, TILE), NEG, F32)
            return carry

        lax.fori_loop(0, TILES, clear, 0)

        def top_pairs(n, pairs):
            for tile, (_, i, _, _) in zip(scores_of(pairs), pairs):
                top = jnp.max(tile.reshape(KEYS // 8, 8, TILE), 0)
                fold[i] = jnp.maximum(fold[i], top)

        each_pairs(total, pair_ref, top_pairs)

        def finish(i, carry):
            norm_ref[i, 0:1, :] = jnp.max(fold[i], 0, keepdims=True) * EXP_SCALE
            fold[i] = jnp.zeros((8, TILE), F32)
            return carry

        lax.fori_loop(0, TILES, finish, 0)

    def exp_pairs(n, pairs):
        sums = []
        for tile, (p, i, _, _) in zip(scores_of(pairs), pairs):
            tile = jnp.exp2(tile * EXP_SCALE - norm_ref[i, 0:1, :])
            terms[p] = tile
            sums.append(jnp.sum(tile.reshape(KEYS // 8, 8, TILE), 0))
        for part, (_, i, _, _) in zip(sums, pairs):
            fold[i] += part

    each_pairs(total, pair_ref, exp_pairs)

    def invert(i, carry):
        norm_ref[i, 1:2, :] = 1.0 / jnp.sum(fold[i], 0, keepdims=True)
        return carry

    lax.fori_loop(0, TILES, invert, 0)

    def give_probs(n):
        slot = lax.rem(n, RING)
        return pltpu.make_async_copy(probs.at[slot], probs_out.at[n], prob_sems.at[slot])

    def out_pairs(n, pairs):
        slot = lax.rem(n, RING)

        @pl.when(n >= RING)
        def _():
            give_probs(n - RING).wait()

        tiles = [(terms[p] * norm_ref[i, 1:2, :]).astype(BF16) for p, i, _, _ in pairs]
        for u, tile in enumerate(tiles):
            probs[slot, u] = tile
        give_probs(n).start()
        tiles = [
            dot(v_turned[:, pl.ds(at, KEYS)], tile) for tile, (_, _, at, _) in zip(tiles, pairs)
        ]
        for tile, (_, i, _, _) in zip(tiles, pairs):
            sums[i] += tile

    each_pairs(total, pair_ref, out_pairs)
    each_tile(lambda i: leaving(i, 2).start())
    steps = pair_steps(total)

    def end(n, carry):
        give_probs(n).wait()
        return carry

    lax.fori_loop(jnp.maximum(steps - RING, 0), steps, end, 0)
    for n in range(3):
        each_tile(lambda i, n=n: leaving(i, n).wait())


def run_attend(received, gains):
    hats = [((HEAD_DIM, LENGTH), BF16), ((LENGTH, HEAD_DIM), BF16)]
    return pl.pallas_call(
        attend_kernel,
        in_specs=[ANY_SPEC, VMEM_SPEC],
        out_specs=[SMEM_SPEC] * 2 + [VMEM_SPEC] + [ANY_SPEC] * 3 + [VMEM_SPEC] * 2 + [ANY_SPEC],
        out_shape=[
            shape((3, MOST_PAIRS), I32),
            shape((1,), I32),
            shape((TILES, 2, TILE), I32),
            *[shape(*hat) for hat in hats],
            shape((MOST_STEPS, UNROLL, KEYS, TILE), BF16),
            shape((TILES, 4, TILE), F32),
            shape((TILES, 2, TILE), F32),
            shape((TILES, HEAD_DIM, TILE), F32),
        ],
        scratch_shapes=[
            *[pltpu.VMEM(*hat) for hat in hats],
            pltpu.VMEM((BLOCKS, 3 * BLOCK, 128), BF16),
            pltpu.VMEM((BLOCKS, EXTRA, 128), BF16),
            pltpu.SMEM((IMAGES + 1,), I32),
            pltpu.VMEM((HEAD_DIM, LENGTH), BF16),
            pltpu.VMEM((MOST_PAIRS, KEYS, TILE), F32),
            pltpu.VMEM((TILES, 8, TILE), F32),
            pltpu.VMEM((RING, UNROLL, KEYS, TILE), BF16),
            pltpu.VMEM((TILES, HEAD_DIM, TILE), F32),
            pltpu.SemaphoreType.DMA((TILES,)),
            pltpu.SemaphoreType.DMA((1,)),
            pltpu.SemaphoreType.DMA((3, TILES)),
            pltpu.SemaphoreType.DMA((RING,)),
        ],
        compiler_params=pltpu.CompilerParams(vmem_limit_bytes=VMEM_LIMIT),
        name="attend",
    )(received, gains)


def loss_kernel(
    labels_ref, mixture_ref, pair_ref, total_ref,
    all_ref, out_in, probs_in,
    send_out, grad_turned_out, inner_ref, counts_ref,
    coef_rows, loss_rows, grad_low, grad_v, probs, recv_ref, extra_ref, out_ref, first_ref, value_ref,
    grad_turned_ref, sems, in_sems, extra_sem, out_sems,
):
    def arrival(i, n):
        source, target = (
            (all_ref.at[tile_blocks(i), pl.ds(0, BLOCK), :], recv_ref.at[tile_blocks(i)]),
            (out_in.at[i], out_ref.at[i]),
        )[n]
        return pltpu.make_async_copy(source, target, in_sems.at[n, i])

    def leaving(i, n):
        rows = tile_at(i)
        blocks = tile_blocks(i)
        source, target = (
            (first_ref.at[blocks], send_out.at[blocks, pl.ds(0, BLOCK), :]),
            (grad_turned_ref.at[:, rows], grad_turned_out.at[:, rows]),
            (value_ref.at[blocks], send_out.at[blocks, pl.ds(BLOCK, BLOCK + EXTRA), :]),
        )[n]
        return pltpu.make_async_copy(source, target, out_sems.at[n, i])

    def take_probs(n):
        return pltpu.make_async_copy(probs_in.at[n], probs.at[n], sems.at[n])

    def start_probs(n, carry):
        take_probs(n).start()
        return carry

    extra = pltpu.make_async_copy(
        all_ref.at[:, pl.ds(BLOCK, EXTRA), :], extra_ref, extra_sem.at[0]
    )
    extra.start()
    for n in range(2):
        each_tile(lambda i, n=n: arrival(i, n).start())
    lax.fori_loop(0, pair_steps(total_ref[0]), start_probs, 0)

    extra.wait()
    seg_all = extra_ref[:, 0, :].astype(F32)
    group = jnp.zeros((BLOCKS, 128), F32)
    for s in range(IMAGES):
        group = jnp.where(seg_all == float(s), labels_ref[0, s].astype(F32), group)
    others = [extra_ref[:, 1 + p, :].astype(F32) for p in range(PACKS)]
    total_mix = mixture_ref[0]
    for g in range(1, GROUPS):
        total_mix = total_mix + mixture_ref[g]
    lane = lax.broadcasted_iota(I32, (1, 128), 1)
    coef = jnp.zeros((BLOCKS, 128), F32)
    count_row = jnp.zeros((1, 128), F32)
    for g in range(GROUPS):
        hits = sum((other == float(g)).astype(F32) for other in others)
        count = jnp.sum(jnp.sum(hits, 0, keepdims=True), 1, keepdims=True)
        share = jnp.full((1, 1), mixture_ref[g], F32) / total_mix
        coef = jnp.where(group == float(g), share / (count * (HEADS * HEAD_DIM)), coef)
        count_row = jnp.where(lane == g, count, count_row)
    counts_ref[...] = count_row
    for b in range(BLOCKS):
        tile, at = block_row(b)
        coef_rows[tile, 0:1, at] = coef[b : b + 1, :]

    def finish(i, carry):
        for n in range(2):
            arrival(i, n).wait()
        rows = tile_at(i)
        head_out = out_ref[i]
        misfit = head_out - tile_rows(recv_ref, i * PAIR, 0).T.astype(F32)
        loss_rows[i, 0:1, :] = 0.5 * jnp.sum(misfit * misfit, 0, keepdims=True)
        grad_out = coef_rows[i, 0:1, :] * misfit
        inner_ref[i, 0:1, :] = jnp.sum(grad_out * head_out, 0, keepdims=True)
        grad_turned = grad_out.astype(BF16)
        grad_turned_ref[:, rows] = grad_turned
        grad_low[rows, :] = grad_turned.T
        grad_v[rows, :] = jnp.zeros((TILE, HEAD_DIM), F32)
        first_ref[tile_blocks(i)] = head_out.astype(BF16).T.reshape(PAIR, BLOCK, HEAD_DIM)
        for n in range(2):
            leaving(i, n).start()
        return carry

    lax.fori_loop(0, TILES, finish, 0, unroll=TILES)

    rows = [block_row(b) for b in range(BLOCKS)]
    losses = jnp.concatenate([loss_rows[tile, 0:1, at] for tile, at in rows], 0)
    loss_row = group_sums(group, losses)
    high = loss_row.astype(BF16)
    left = loss_row - high.astype(F32)
    middle = left.astype(BF16)
    low = (left - middle.astype(F32)).astype(BF16)
    row = lax.broadcasted_iota(I32, (EXTRA, 128), 0)
    pieces = jnp.zeros((EXTRA, 128), F32)
    for n, piece in enumerate((high, middle, low)):
        pieces = jnp.where(row == n, piece.astype(F32), pieces)
    value_ref[:, BLOCK:, :] = jnp.broadcast_to(pieces.astype(BF16)[None], (BLOCKS, EXTRA, 128))

    def add_pairs(n, pairs):
        take_probs(n).wait()
        tiles = [dot(probs[n, u], grad_low[tile_at(pair[1]), :]) for u, pair in enumerate(pairs)]
        for tile, (_, _, at, _) in zip(tiles, pairs):
            grad_v[pl.ds(at, KEYS), :] += tile

    each_pairs(total_ref[0], pair_ref, add_pairs)

    def give(i, carry):
        value_ref[pl.ds(i * PAIR, PAIR), 0:BLOCK, :] = (
            grad_v[tile_at(i), :].astype(BF16).reshape(PAIR, BLOCK, HEAD_DIM)
        )
        leaving(i, 2).start()
        return carry

    lax.fori_loop(0, TILES, give, 0, unroll=TILES)
    for n in range(3):
        each_tile(lambda i, n=n: leaving(i, n).wait())


def run_loss(labels, mixture, pairs, total, second, head_out, probs):
    return pl.pallas_call(
        loss_kernel,
        in_specs=[SMEM_SPEC] * 4 + [ANY_SPEC] * 3,
        out_specs=[ANY_SPEC] * 2 + [VMEM_SPEC] * 2,
        out_shape=[
            shape((BLOCKS, 2 * BLOCK + EXTRA, 128), BF16),
            shape((HEAD_DIM, LENGTH), BF16),
            shape((TILES, 1, TILE), F32),
            shape((1, 128), F32),
        ],
        scratch_shapes=[
            pltpu.VMEM((TILES, 1, TILE), F32),
            pltpu.VMEM((TILES, 1, TILE), F32),
            pltpu.VMEM((LENGTH, HEAD_DIM), BF16),
            pltpu.VMEM((LENGTH, HEAD_DIM), F32),
            pltpu.VMEM((MOST_STEPS, UNROLL, KEYS, TILE), BF16),
            pltpu.VMEM((BLOCKS, BLOCK, 128), BF16),
            pltpu.VMEM((BLOCKS, EXTRA, 128), BF16),
            pltpu.VMEM((TILES, HEAD_DIM, TILE), F32),
            pltpu.VMEM((BLOCKS, BLOCK, 128), BF16),
            pltpu.VMEM((BLOCKS, BLOCK + EXTRA, 128), BF16),
            pltpu.VMEM((HEAD_DIM, LENGTH), BF16),
            pltpu.SemaphoreType.DMA((MOST_STEPS,)),
            pltpu.SemaphoreType.DMA((2, TILES)),
            pltpu.SemaphoreType.DMA((1,)),
            pltpu.SemaphoreType.DMA((3, TILES)),
        ],
        compiler_params=pltpu.CompilerParams(vmem_limit_bytes=VMEM_LIMIT),
        name="loss_and_grad_value",
    )(labels, mixture, pairs, total, second, head_out, probs)


def backward_kernel(
    pair_ref, total_ref,
    all_ref, q_turned_in, k_hat_in, grad_turned_in,
    gains_ref, moments_ref, span_rows_ref, norm_ref, inner_ref,
    send_out, gain_out_ref,
    grad_q, grad_k, q_hat_ref, k_turned_ref, value_ref, raw_ref, q_turned_ref, k_hat_ref,
    grad_turned_ref, send_ref, in_sems, out_sems,
):
    def arrival(i, n):
        rows = tile_at(i)
        blocks = tile_blocks(i)
        source, target = (
            (q_turned_in.at[:, rows], q_turned_ref.at[:, rows]),
            (k_hat_in.at[rows, :], k_hat_ref.at[rows, :]),
            (all_ref.at[blocks, pl.ds(2 * BLOCK, BLOCK), :], value_ref.at[blocks]),
            (grad_turned_in.at[:, rows], grad_turned_ref.at[:, rows]),
            (all_ref.at[blocks, pl.ds(0, 2 * BLOCK), :], raw_ref.at[blocks]),
        )[n]
        return pltpu.make_async_copy(source, target, in_sems.at[n, i])

    def leaving(i):
        blocks = tile_blocks(i)
        return pltpu.make_async_copy(send_ref.at[blocks], send_out.at[blocks], out_sems.at[i])

    for n in range(5):
        each_tile(lambda i, n=n: arrival(i, n).start())

    def clear(i, carry):
        for n in range(2):
            arrival(i, n).wait()
        q_hat_ref[tile_at(i), :] = q_turned_ref[:, tile_at(i)].T
        k_turned_ref[:, tile_at(i)] = k_hat_ref[tile_at(i), :].T
        grad_q[i] = jnp.zeros((HEAD_DIM, TILE), F32)
        grad_k[tile_at(i), :] = jnp.zeros((TILE, HEAD_DIM), F32)
        return carry

    lax.fori_loop(0, TILES, clear, 0, unroll=TILES)
    for n in (2, 3):
        each_tile(lambda i, n=n: arrival(i, n).wait())

    def add_pairs(n, pairs):
        tiles = [
            dot(k_hat_ref[pl.ds(at, KEYS), :], q_turned_ref[:, tile_at(i)]) for _, i, at, _ in pairs
        ]
        prob_grads = [
            dot(tile_rows(value_ref, at // BLOCK, 0, KEYS), grad_turned_ref[:, tile_at(i)])
            for _, i, at, _ in pairs
        ]
        tiles = [
            softmax_tile(tile, span_rows_ref, norm_ref, i, mask_at)
            for tile, (_, i, _, mask_at) in zip(tiles, pairs)
        ]
        tiles = [
            (tile * (prob - inner_ref[i, 0:1, :]) * SCALE).astype(BF16)
            for tile, prob, (_, i, _, _) in zip(tiles, prob_grads, pairs)
        ]
        keys = [dot(tile, q_hat_ref[tile_at(i), :]) for tile, (_, i, _, _) in zip(tiles, pairs)]
        queries = [
            dot(k_turned_ref[:, pl.ds(at, KEYS)], tile) for tile, (_, _, at, _) in zip(tiles, pairs)
        ]
        for key, query, (_, i, at, _) in zip(keys, queries, pairs):
            grad_k[pl.ds(at, KEYS), :] += key
            grad_q[i] += query

    each_pairs(total_ref[0], pair_ref, add_pairs)

    gains = jnp.concatenate([gains_ref[...], jnp.zeros((6, HEAD_DIM), F32)], 0).T

    def norm_backward(i, n, grad_hat):
        mean = moments_ref[i, 2 * n : 2 * n + 1, :]
        inverse = moments_ref[i, 2 * n + 1 : 2 * n + 2, :]
        normed = (tile_rows(raw_ref, i * PAIR, n).T.astype(F32) - mean) * inverse
        grad_normed = grad_hat * gains[:, n : n + 1]
        inner = mean_down(grad_normed * normed)
        grad_in = inverse * (grad_normed - mean_down(grad_normed) - normed * inner)
        send_ref[pl.ds(i * PAIR, PAIR), n * BLOCK : (n + 1) * BLOCK, :] = grad_in.astype(
            BF16
        ).T.reshape(PAIR, BLOCK, HEAD_DIM)
        grad_gain = grad_hat * normed
        return sum(grad_gain[:, c : c + 128] for c in range(0, TILE, 128))

    def finish(i, gain_sums):
        arrival(i, 4).wait()
        gain_q, gain_k = gain_sums
        gain_q = gain_q + norm_backward(i, 0, grad_q[i])
        gain_k = gain_k + norm_backward(i, 1, grad_k[tile_at(i), :].T)
        leaving(i).start()
        return gain_q, gain_k

    zero = jnp.zeros((HEAD_DIM, 128), F32)
    gain_q, gain_k = lax.fori_loop(0, TILES, finish, (zero, zero), unroll=TILES)
    gain_out_ref[0:1, :] = jnp.sum(gain_q.T, 0, keepdims=True)
    gain_out_ref[1:2, :] = jnp.sum(gain_k.T, 0, keepdims=True)
    each_tile(lambda i: leaving(i).wait())


def run_backward(pairs, total, received, q_turned, k_hat, grad_turned, *arrays):
    return pl.pallas_call(
        backward_kernel,
        in_specs=[SMEM_SPEC] * 2 + [ANY_SPEC] * 4 + [VMEM_SPEC] * len(arrays),
        out_specs=[ANY_SPEC, VMEM_SPEC],
        out_shape=[shape((BLOCKS, 2 * BLOCK, 128), BF16), shape((2, HEAD_DIM), F32)],
        scratch_shapes=[
            pltpu.VMEM((TILES, HEAD_DIM, TILE), F32),
            pltpu.VMEM((LENGTH, HEAD_DIM), F32),
            pltpu.VMEM((LENGTH, HEAD_DIM), BF16),
            pltpu.VMEM((HEAD_DIM, LENGTH), BF16),
            pltpu.VMEM((BLOCKS, BLOCK, 128), BF16),
            pltpu.VMEM((BLOCKS, 2 * BLOCK, 128), BF16),
            pltpu.VMEM((HEAD_DIM, LENGTH), BF16),
            pltpu.VMEM((LENGTH, HEAD_DIM), BF16),
            pltpu.VMEM((HEAD_DIM, LENGTH), BF16),
            pltpu.VMEM((BLOCKS, 2 * BLOCK, 128), BF16),
            pltpu.SemaphoreType.DMA((5, TILES)),
            pltpu.SemaphoreType.DMA((TILES,)),
        ],
        compiler_params=pltpu.CompilerParams(vmem_limit_bytes=VMEM_LIMIT),
        name="backward",
    )(pairs, total, received, q_turned, k_hat, grad_turned, *arrays)


def over_packs(value):
    moved = [value]
    for shift in range(1, PACKS):
        pairs = [(i, (i + shift) % PACKS) for i in range(PACKS)]
        moved.append(lax.ppermute(value, "pack", pairs))
    return moved


def exchange(slab):
    return lax.all_to_all(slab, "seq", split_axis=0, concat_axis=0, tiled=True)


def on_device(
    query_rows, key_rows, value_rows, target_rows, norm_gains, segment_ids, group_labels, mixture
):
    gains = norm_gains.reshape(2, HEAD_DIM)
    first = exchange(pack_rows((query_rows, key_rows, value_rows), segment_ids, "pack_first"))

    image_hot = segment_ids[0][:, None] == jnp.arange(IMAGES, dtype=I32)[None, :]
    labels = jnp.sum(jnp.where(image_hot, group_labels[0][None, :], 0), 1)[None, :]
    extra = jnp.concatenate([segment_ids.astype(F32), *over_packs(labels.astype(F32))], 0)
    second = exchange(pack_rows((target_rows,), extra, "pack_second"))

    pairs, total, span_rows, *hats, probs, moments, norms, head_out = run_attend(first, gains)
    send, grad_turned, inner, counts = run_loss(
        group_labels, mixture, pairs, total, second, head_out, probs
    )
    back = exchange(send)
    send, gain_part = run_backward(
        pairs, total, first, *hats, grad_turned, gains, moments, span_rows, norms, inner
    )
    last = exchange(send)
    attended, grad_value = unpack_rows(back, 2, "unpack_first")
    losses = jnp.sum(back[:, 2 * BLOCK : 2 * BLOCK + 3, :GROUPS].astype(F32), (0, 1))
    group_total = sum(over_packs(losses))
    group_loss = group_total / (counts[0, :GROUPS] * (HEADS * HEAD_DIM))
    shares = mixture / jnp.sum(mixture)
    raised = shares * jnp.exp(ETA * group_loss)
    new_mixture = raised / jnp.sum(raised)
    grad_gains = sum(over_packs(gain_part)).reshape(2, 1, HEAD_DIM)
    grad_query, grad_key = unpack_rows(last, 2, "unpack_last")
    return (attended, grad_query, grad_key, grad_value, grad_gains, new_mixture)


def solution(mesh):
    rows = P("pack", "seq", None)
    gains = P(None, "seq", None)
    return jax.shard_map(
        on_device,
        mesh=mesh,
        in_specs=(rows, rows, rows, rows, gains, P("pack", "seq"), P("pack", None), P()),
        out_specs=(rows, rows, rows, rows, gains, P()),
        check_vma=False,
    )
```

```python
import functools

import jax
import jax.numpy as jnp
from jax import lax
from jax.experimental import pallas as pl
from jax.experimental.pallas import tpu as pltpu
from jax.sharding import PartitionSpec as P

HEADS = 32
HEAD_DIM = 128
IMAGES = 16
GROUPS = 8
PACKS = 4
LENGTH = 4096

NEG = -1e30
EPS = 1e-06
ETA = 2.0
SCALE = HEAD_DIM ** (-0.5)
EXP_SCALE = SCALE * 1.4426950408889634

BLOCK = 128
BLOCKS = LENGTH // BLOCK
TILE = 256
TILES = LENGTH // TILE
PAIR = TILE // BLOCK
KEYS = 256
UNROLL = 6
MOST_PAIRS = (LENGTH * (1024 // TILE + 1) + TILES * (BLOCK - 1 + KEYS - 1)) // KEYS
MOST_STEPS = MOST_PAIRS // UNROLL + 1
MOST_PAIRS = MOST_STEPS * UNROLL
RING = 4
SAFE_LOGIT = 70.0
EXTRA = 16
VMEM_LIMIT = 56 * 1024 * 1024

BF16 = jnp.bfloat16
F32 = jnp.float32
I32 = jnp.int32

WORK = pl.CostEstimate(flops=1 << 33, bytes_accessed=1 << 25, transcendentals=1 << 22)

VMEM_SPEC = pl.BlockSpec(memory_space=pltpu.VMEM)
SMEM_SPEC = pl.BlockSpec(memory_space=pltpu.SMEM)
ANY_SPEC = pl.BlockSpec(memory_space=pl.ANY)


def shape(dims, dtype):
    return jax.ShapeDtypeStruct(dims, dtype)


def head_columns(h):
    return pl.ds(h * HEAD_DIM, HEAD_DIM)


def pack_kernel(count, *refs):
    row_refs, extra_refs, (out_ref, sems) = refs[:count], refs[count:-2], refs[-2:]
    copies = []
    for n, ref in enumerate(row_refs):
        for h in range(HEADS):
            copy = pltpu.make_async_copy(
                ref.at[0, :, head_columns(h)],
                out_ref.at[h, pl.ds(n * BLOCK, BLOCK), :],
                sems.at[n, h],
            )
            copy.start()
            copies.append(copy)
    for extra_ref in extra_refs:
        tile = extra_ref[...].astype(F32)
        left = jnp.zeros((EXTRA - tile.shape[0], 128), F32)
        tile = jnp.concatenate([tile, left], 0).astype(BF16)
        out_ref[:, len(row_refs) * BLOCK :, :] = jnp.broadcast_to(tile[None], (HEADS, EXTRA, 128))
    for copy in copies:
        copy.wait()


def pack_rows(rows, extra, name):
    extras = () if extra is None else (extra,)
    return pl.pallas_call(
        functools.partial(pack_kernel, len(rows)),
        in_specs=[ANY_SPEC] * len(rows) + [VMEM_SPEC] * len(extras),
        out_specs=VMEM_SPEC,
        out_shape=shape((HEADS, len(rows) * BLOCK + EXTRA * len(extras), 128), BF16),
        scratch_shapes=[pltpu.SemaphoreType.DMA((len(rows), HEADS))],
        compiler_params=pltpu.CompilerParams(vmem_limit_bytes=VMEM_LIMIT),
        name=name,
    )(*rows, *extras)


def unpack_kernel(in_ref, *refs):
    *row_refs, sems = refs
    copies = []
    for n, ref in enumerate(row_refs):
        for h in range(HEADS):
            copy = pltpu.make_async_copy(
                in_ref.at[h, pl.ds(n * BLOCK, BLOCK), :],
                ref.at[0, :, head_columns(h)],
                sems.at[n, h],
            )
            copy.start()
            copies.append(copy)
    for copy in copies:
        copy.wait()


def unpack_rows(slab, count, name):
    return pl.pallas_call(
        unpack_kernel,
        in_specs=[VMEM_SPEC],
        out_specs=[ANY_SPEC] * count,
        out_shape=[shape((1, BLOCK, HEADS * HEAD_DIM), BF16)] * count,
        scratch_shapes=[pltpu.SemaphoreType.DMA((count, HEADS))],
        compiler_params=pltpu.CompilerParams(vmem_limit_bytes=VMEM_LIMIT),
        name=name,
    )(slab)


def dot(a, b, contract=((1,), (0,))):
    return lax.dot_general(a, b, (contract, ((), ())), preferred_element_type=F32)


def tile_rows(ref, i, part, size=TILE):
    blocks = size // BLOCK
    return ref[pl.ds(i, blocks), part * BLOCK : (part + 1) * BLOCK, :].reshape(size, HEAD_DIM)


def tile_at(i, size=TILE):
    return pl.ds(pl.multiple_of(i * size, size), size)


def mean_down(values):
    return jnp.sum(values, 0, keepdims=True) * (1.0 / HEAD_DIM)


def block_row(b):
    return b // PAIR, slice((b % PAIR) * BLOCK, (b % PAIR + 1) * BLOCK)


def group_sums(group, values):
    lane = lax.broadcasted_iota(I32, (1, 128), 1)
    sums = jnp.zeros((1, 128), F32)
    for g in range(GROUPS):
        part = jnp.sum(jnp.where(group == float(g), values, 0.0), 0, keepdims=True)
        sums = jnp.where(lane == g, jnp.sum(part, 1, keepdims=True), sums)
    return sums


def key_mask(span_rows_ref, i, start, step):
    first = span_rows_ref[i, 0:1, :] - start
    count = span_rows_ref[i, 1:2, :]
    row = lax.broadcasted_iota(I32, (step, TILE), 0)
    return (row - first).astype(jnp.uint32) < count.astype(jnp.uint32)


def masked(scores, span_rows_ref, i, mask_at):
    return jnp.where(key_mask(span_rows_ref, i, mask_at, KEYS), scores, NEG)


def pair_steps(total):
    return (total + UNROLL - 1) // UNROLL


def each_pairs(total, pair_ref, body):
    def some(n, carry):
        pairs = []
        for u in range(UNROLL):
            p = n * UNROLL + u
            at = pl.multiple_of(pair_ref[1, p], BLOCK)
            pairs.append((p, pair_ref[0, p], at, pair_ref[2, p]))
        body(n, pairs)
        return carry

    lax.fori_loop(0, pair_steps(total), some, 0)


def softmax_tile(scores, span_rows_ref, norm_ref, i, mask_at):
    scores = masked(scores, span_rows_ref, i, mask_at)
    return jnp.exp2(scores * EXP_SCALE - norm_ref[i, 0:1, :]) * norm_ref[i, 1:2, :]


def find_pairs(seg_all, starts, pair_ref, span_rows_ref):
    for s in range(IMAGES + 1):
        starts[s] = jnp.sum((seg_all < float(s)).astype(F32)).astype(I32)
    first = jnp.zeros((BLOCKS, 128), I32)
    count = jnp.zeros((BLOCKS, 128), I32)
    for s in range(IMAGES):
        here = seg_all == float(s)
        first = jnp.where(here, starts[s], first)
        count = jnp.where(here, starts[s + 1] - starts[s], count)
    for b in range(BLOCKS):
        tile, at = block_row(b)
        span_rows_ref[tile, 0:1, at] = first[b : b + 1, :]
        span_rows_ref[tile, 1:2, at] = count[b : b + 1, :]

    def span(i, total):
        low, high = jnp.int32(0), jnp.int32(LENGTH)
        for s in range(1, IMAGES):
            low = jnp.where(starts[s] <= i * TILE, starts[s], low)
        for s in range(IMAGES - 1, 0, -1):
            high = jnp.where(starts[s] > i * TILE + TILE - 1, starts[s], high)
        low = (low // BLOCK) * BLOCK
        steps = (high - low + KEYS - 1) // KEYS
        low = jnp.minimum(low, LENGTH - steps * KEYS)

        def add(j, carry):
            pair_ref[0, total + j] = i
            pair_ref[1, total + j] = low + j * KEYS
            pair_ref[2, total + j] = low + j * KEYS
            return carry

        lax.fori_loop(0, steps, add, 0)
        return total + steps

    total = lax.fori_loop(0, TILES, span, jnp.int32(0))
    for u in range(UNROLL):
        pair_ref[0, total + u] = 0
        pair_ref[1, total + u] = 0
        pair_ref[2, total + u] = -(1 << 20)
    return total


def each_tile(what):
    def one(i, carry):
        what(i)
        return carry

    lax.fori_loop(0, TILES, one, 0)


def tile_blocks(i):
    return pl.ds(i * PAIR, PAIR)


def attend_kernel(
    all_ref, gains_ref,
    pair_ref, total_ref, span_rows_ref, *refs,
):
    hat_outs, probs_out, refs = refs[:2], refs[2], refs[3:]
    (moments_ref, norm_ref, out_ref), refs = refs[:3], refs[3:]
    hats, refs = refs[:2], refs[2:]
    q_turned_ref, k_hat_ref = hats
    recv_ref, extra_ref, starts, v_turned, terms, fold, probs, sums = refs[:8]
    in_sems, extra_sem, out_sems, prob_sems = refs[8:]

    def arrival(i):
        return pltpu.make_async_copy(
            all_ref.at[tile_blocks(i), pl.ds(0, 3 * BLOCK), :],
            recv_ref.at[tile_blocks(i)],
            in_sems.at[i],
        )

    def leaving(i, n):
        rows = tile_at(i)
        source, target = (
            (q_turned_ref.at[:, rows], hat_outs[0].at[:, rows]),
            (k_hat_ref.at[rows, :], hat_outs[1].at[rows, :]),
            (sums.at[i], out_ref.at[i]),
        )[n]
        return pltpu.make_async_copy(source, target, out_sems.at[n, i])

    extra = pltpu.make_async_copy(
        all_ref.at[:, pl.ds(3 * BLOCK, EXTRA), :], extra_ref, extra_sem.at[0]
    )
    extra.start()
    each_tile(lambda i: arrival(i).start())
    extra.wait()
    total = find_pairs(extra_ref[:, 0, :].astype(F32), starts, pair_ref, span_rows_ref)
    total_ref[0] = total
    gains = jnp.concatenate([gains_ref[...], jnp.zeros((6, HEAD_DIM), F32)], 0).T

    def prepare(i, most):
        arrival(i).wait()
        rows = tile_at(i)
        v_turned[:, rows] = tile_rows(recv_ref, i * PAIR, 2).T
        sizes = []
        for n in range(2):
            values = tile_rows(recv_ref, i * PAIR, n).T.astype(F32)
            mean = mean_down(values)
            centre = values - mean
            inverse = lax.rsqrt(mean_down(centre * centre) + EPS)
            moments_ref[i, 2 * n : 2 * n + 1, :] = mean
            moments_ref[i, 2 * n + 1 : 2 * n + 2, :] = inverse
            hat = centre * inverse * gains[:, n : n + 1]
            sizes.append(jnp.maximum(most[n], mean_down(hat * hat)))
            if n == 0:
                q_turned_ref[:, rows] = hat.astype(BF16)
            else:
                k_hat_ref[rows, :] = hat.astype(BF16).T
        for n in range(2):
            leaving(i, n).start()
        sums[i] = jnp.zeros((HEAD_DIM, TILE), F32)
        norm_ref[i] = jnp.zeros((2, TILE), F32)
        fold[i] = jnp.zeros((8, TILE), F32)
        return tuple(sizes)

    zero = jnp.zeros((1, TILE), F32)
    most_q, most_k = lax.fori_loop(0, TILES, prepare, (zero, zero), unroll=TILES)
    bound = jnp.max(most_q) * jnp.max(most_k) * HEAD_DIM

    def scores_of(pairs):
        tiles = [
            dot(k_hat_ref[pl.ds(at, KEYS), :], q_turned_ref[:, tile_at(i)]) for _, i, at, _ in pairs
        ]
        return [
            masked(tile, span_rows_ref, i, mask_at)
            for tile, (_, i, _, mask_at) in zip(tiles, pairs)
        ]

    @pl.when(jnp.logical_not(bound <= SAFE_LOGIT * SAFE_LOGIT))
    def _():
        def clear(i, carry):
            fold[i] = jnp.full((8, TILE), NEG, F32)
            return carry

        lax.fori_loop(0, TILES, clear, 0)

        def top_pairs(n, pairs):
            for tile, (_, i, _, _) in zip(scores_of(pairs), pairs):
                top = jnp.max(tile.reshape(KEYS // 8, 8, TILE), 0)
                fold[i] = jnp.maximum(fold[i], top)

        each_pairs(total, pair_ref, top_pairs)

        def finish(i, carry):
            norm_ref[i, 0:1, :] = jnp.max(fold[i], 0, keepdims=True) * EXP_SCALE
            fold[i] = jnp.zeros((8, TILE), F32)
            return carry

        lax.fori_loop(0, TILES, finish, 0)

    def exp_pairs(n, pairs):
        sums = []
        for tile, (p, i, _, _) in zip(scores_of(pairs), pairs):
            tile = jnp.exp2(tile * EXP_SCALE - norm_ref[i, 0:1, :])
            terms[p] = tile
            sums.append(jnp.sum(tile.reshape(KEYS // 8, 8, TILE), 0))
        for part, (_, i, _, _) in zip(sums, pairs):
            fold[i] += part

    each_pairs(total, pair_ref, exp_pairs)

    def invert(i, carry):
        norm_ref[i, 1:2, :] = 1.0 / jnp.sum(fold[i], 0, keepdims=True)
        return carry

    lax.fori_loop(0, TILES, invert, 0)

    def give_probs(n):
        slot = lax.rem(n, RING)
        return pltpu.make_async_copy(probs.at[slot], probs_out.at[n], prob_sems.at[slot])

    def out_pairs(n, pairs):
        slot = lax.rem(n, RING)

        @pl.when(n >= RING)
        def _():
            give_probs(n - RING).wait()

        tiles = [(terms[p] * norm_ref[i, 1:2, :]).astype(BF16) for p, i, _, _ in pairs]
        for u, tile in enumerate(tiles):
            probs[slot, u] = tile
        give_probs(n).start()
        tiles = [
            dot(v_turned[:, pl.ds(at, KEYS)], tile) for tile, (_, _, at, _) in zip(tiles, pairs)
        ]
        for tile, (_, i, _, _) in zip(tiles, pairs):
            sums[i] += tile

    each_pairs(total, pair_ref, out_pairs)
    each_tile(lambda i: leaving(i, 2).start())
    steps = pair_steps(total)

    def end(n, carry):
        give_probs(n).wait()
        return carry

    lax.fori_loop(jnp.maximum(steps - RING, 0), steps, end, 0)
    for n in range(3):
        each_tile(lambda i, n=n: leaving(i, n).wait())


def run_attend(received, gains):
    hats = [((HEAD_DIM, LENGTH), BF16), ((LENGTH, HEAD_DIM), BF16)]
    return pl.pallas_call(
        attend_kernel,
        in_specs=[ANY_SPEC, VMEM_SPEC],
        out_specs=[SMEM_SPEC] * 2 + [VMEM_SPEC] + [ANY_SPEC] * 3 + [VMEM_SPEC] * 2 + [ANY_SPEC],
        out_shape=[
            shape((3, MOST_PAIRS), I32),
            shape((1,), I32),
            shape((TILES, 2, TILE), I32),
            *[shape(*hat) for hat in hats],
            shape((MOST_STEPS, UNROLL, KEYS, TILE), BF16),
            shape((TILES, 4, TILE), F32),
            shape((TILES, 2, TILE), F32),
            shape((TILES, HEAD_DIM, TILE), F32),
        ],
        scratch_shapes=[
            *[pltpu.VMEM(*hat) for hat in hats],
            pltpu.VMEM((BLOCKS, 3 * BLOCK, 128), BF16),
            pltpu.VMEM((BLOCKS, EXTRA, 128), BF16),
            pltpu.SMEM((IMAGES + 1,), I32),
            pltpu.VMEM((HEAD_DIM, LENGTH), BF16),
            pltpu.VMEM((MOST_PAIRS, KEYS, TILE), F32),
            pltpu.VMEM((TILES, 8, TILE), F32),
            pltpu.VMEM((RING, UNROLL, KEYS, TILE), BF16),
            pltpu.VMEM((TILES, HEAD_DIM, TILE), F32),
            pltpu.SemaphoreType.DMA((TILES,)),
            pltpu.SemaphoreType.DMA((1,)),
            pltpu.SemaphoreType.DMA((3, TILES)),
            pltpu.SemaphoreType.DMA((RING,)),
        ],
        compiler_params=pltpu.CompilerParams(vmem_limit_bytes=VMEM_LIMIT),
        cost_estimate=WORK,
        name="attend",
    )(received, gains)


def loss_kernel(
    labels_ref, mixture_ref, pair_ref, total_ref,
    all_ref, out_in, probs_in,
    send_out, grad_turned_out, inner_ref, counts_ref,
    coef_rows, loss_rows, grad_low, grad_v, probs, recv_ref, extra_ref, out_ref, first_ref, value_ref,
    grad_turned_ref, sems, in_sems, extra_sem, out_sems,
):
    def arrival(i, n):
        source, target = (
            (all_ref.at[tile_blocks(i), pl.ds(0, BLOCK), :], recv_ref.at[tile_blocks(i)]),
            (out_in.at[i], out_ref.at[i]),
        )[n]
        return pltpu.make_async_copy(source, target, in_sems.at[n, i])

    def leaving(i, n):
        rows = tile_at(i)
        blocks = tile_blocks(i)
        source, target = (
            (first_ref.at[blocks], send_out.at[blocks, pl.ds(0, BLOCK), :]),
            (grad_turned_ref.at[:, rows], grad_turned_out.at[:, rows]),
            (value_ref.at[blocks], send_out.at[blocks, pl.ds(BLOCK, BLOCK + EXTRA), :]),
        )[n]
        return pltpu.make_async_copy(source, target, out_sems.at[n, i])

    def take_probs(n):
        return pltpu.make_async_copy(probs_in.at[n], probs.at[n], sems.at[n])

    def start_probs(n, carry):
        take_probs(n).start()
        return carry

    extra = pltpu.make_async_copy(
        all_ref.at[:, pl.ds(BLOCK, EXTRA), :], extra_ref, extra_sem.at[0]
    )
    extra.start()
    for n in range(2):
        each_tile(lambda i, n=n: arrival(i, n).start())
    lax.fori_loop(0, pair_steps(total_ref[0]), start_probs, 0)

    extra.wait()
    seg_all = extra_ref[:, 0, :].astype(F32)
    group = jnp.zeros((BLOCKS, 128), F32)
    for s in range(IMAGES):
        group = jnp.where(seg_all == float(s), labels_ref[0, s].astype(F32), group)
    others = [extra_ref[:, 1 + p, :].astype(F32) for p in range(PACKS)]
    total_mix = mixture_ref[0]
    for g in range(1, GROUPS):
        total_mix = total_mix + mixture_ref[g]
    lane = lax.broadcasted_iota(I32, (1, 128), 1)
    coef = jnp.zeros((BLOCKS, 128), F32)
    count_row = jnp.zeros((1, 128), F32)
    for g in range(GROUPS):
        hits = sum((other == float(g)).astype(F32) for other in others)
        count = jnp.sum(jnp.sum(hits, 0, keepdims=True), 1, keepdims=True)
        share = jnp.full((1, 1), mixture_ref[g], F32) / total_mix
        coef = jnp.where(group == float(g), share / (count * (HEADS * HEAD_DIM)), coef)
        count_row = jnp.where(lane == g, count, count_row)
    counts_ref[...] = count_row
    for b in range(BLOCKS):
        tile, at = block_row(b)
        coef_rows[tile, 0:1, at] = coef[b : b + 1, :]

    def finish(i, carry):
        for n in range(2):
            arrival(i, n).wait()
        rows = tile_at(i)
        head_out = out_ref[i]
        misfit = head_out - tile_rows(recv_ref, i * PAIR, 0).T.astype(F32)
        loss_rows[i, 0:1, :] = 0.5 * jnp.sum(misfit * misfit, 0, keepdims=True)
        grad_out = coef_rows[i, 0:1, :] * misfit
        inner_ref[i, 0:1, :] = jnp.sum(grad_out * head_out, 0, keepdims=True)
        grad_turned = grad_out.astype(BF16)
        grad_turned_ref[:, rows] = grad_turned
        grad_low[rows, :] = grad_turned.T
        grad_v[rows, :] = jnp.zeros((TILE, HEAD_DIM), F32)
        first_ref[tile_blocks(i)] = head_out.astype(BF16).T.reshape(PAIR, BLOCK, HEAD_DIM)
        for n in range(2):
            leaving(i, n).start()
        return carry

    lax.fori_loop(0, TILES, finish, 0, unroll=TILES)

    rows = [block_row(b) for b in range(BLOCKS)]
    losses = jnp.concatenate([loss_rows[tile, 0:1, at] for tile, at in rows], 0)
    loss_row = group_sums(group, losses)
    high = loss_row.astype(BF16)
    left = loss_row - high.astype(F32)
    middle = left.astype(BF16)
    low = (left - middle.astype(F32)).astype(BF16)
    row = lax.broadcasted_iota(I32, (EXTRA, 128), 0)
    pieces = jnp.zeros((EXTRA, 128), F32)
    for n, piece in enumerate((high, middle, low)):
        pieces = jnp.where(row == n, piece.astype(F32), pieces)
    value_ref[:, BLOCK:, :] = jnp.broadcast_to(pieces.astype(BF16)[None], (BLOCKS, EXTRA, 128))

    def add_pairs(n, pairs):
        take_probs(n).wait()
        tiles = [dot(probs[n, u], grad_low[tile_at(pair[1]), :]) for u, pair in enumerate(pairs)]
        for tile, (_, _, at, _) in zip(tiles, pairs):
            grad_v[pl.ds(at, KEYS), :] += tile

    each_pairs(total_ref[0], pair_ref, add_pairs)

    def give(i, carry):
        value_ref[pl.ds(i * PAIR, PAIR), 0:BLOCK, :] = (
            grad_v[tile_at(i), :].astype(BF16).reshape(PAIR, BLOCK, HEAD_DIM)
        )
        leaving(i, 2).start()
        return carry

    lax.fori_loop(0, TILES, give, 0, unroll=TILES)
    for n in range(3):
        each_tile(lambda i, n=n: leaving(i, n).wait())


def run_loss(labels, mixture, pairs, total, second, head_out, probs):
    return pl.pallas_call(
        loss_kernel,
        in_specs=[SMEM_SPEC] * 4 + [ANY_SPEC] * 3,
        out_specs=[ANY_SPEC] * 2 + [VMEM_SPEC] * 2,
        out_shape=[
            shape((BLOCKS, 2 * BLOCK + EXTRA, 128), BF16),
            shape((HEAD_DIM, LENGTH), BF16),
            shape((TILES, 1, TILE), F32),
            shape((1, 128), F32),
        ],
        scratch_shapes=[
            pltpu.VMEM((TILES, 1, TILE), F32),
            pltpu.VMEM((TILES, 1, TILE), F32),
            pltpu.VMEM((LENGTH, HEAD_DIM), BF16),
            pltpu.VMEM((LENGTH, HEAD_DIM), F32),
            pltpu.VMEM((MOST_STEPS, UNROLL, KEYS, TILE), BF16),
            pltpu.VMEM((BLOCKS, BLOCK, 128), BF16),
            pltpu.VMEM((BLOCKS, EXTRA, 128), BF16),
            pltpu.VMEM((TILES, HEAD_DIM, TILE), F32),
            pltpu.VMEM((BLOCKS, BLOCK, 128), BF16),
            pltpu.VMEM((BLOCKS, BLOCK + EXTRA, 128), BF16),
            pltpu.VMEM((HEAD_DIM, LENGTH), BF16),
            pltpu.SemaphoreType.DMA((MOST_STEPS,)),
            pltpu.SemaphoreType.DMA((2, TILES)),
            pltpu.SemaphoreType.DMA((1,)),
            pltpu.SemaphoreType.DMA((3, TILES)),
        ],
        compiler_params=pltpu.CompilerParams(vmem_limit_bytes=VMEM_LIMIT),
        name="loss_and_grad_value",
    )(labels, mixture, pairs, total, second, head_out, probs)


def backward_kernel(
    pair_ref, total_ref,
    all_ref, q_turned_in, k_hat_in, grad_turned_in,
    gains_ref, moments_ref, span_rows_ref, norm_ref, inner_ref,
    send_out, gain_out_ref,
    grad_q, grad_k, q_hat_ref, k_turned_ref, value_ref, raw_ref, q_turned_ref, k_hat_ref,
    grad_turned_ref, send_ref, in_sems, out_sems,
):
    def arrival(i, n):
        rows = tile_at(i)
        blocks = tile_blocks(i)
        source, target = (
            (q_turned_in.at[:, rows], q_turned_ref.at[:, rows]),
            (k_hat_in.at[rows, :], k_hat_ref.at[rows, :]),
            (all_ref.at[blocks, pl.ds(2 * BLOCK, BLOCK), :], value_ref.at[blocks]),
            (grad_turned_in.at[:, rows], grad_turned_ref.at[:, rows]),
            (all_ref.at[blocks, pl.ds(0, 2 * BLOCK), :], raw_ref.at[blocks]),
        )[n]
        return pltpu.make_async_copy(source, target, in_sems.at[n, i])

    def leaving(i):
        blocks = tile_blocks(i)
        return pltpu.make_async_copy(send_ref.at[blocks], send_out.at[blocks], out_sems.at[i])

    for n in range(5):
        each_tile(lambda i, n=n: arrival(i, n).start())

    def clear(i, carry):
        for n in range(2):
            arrival(i, n).wait()
        q_hat_ref[tile_at(i), :] = q_turned_ref[:, tile_at(i)].T
        k_turned_ref[:, tile_at(i)] = k_hat_ref[tile_at(i), :].T
        grad_q[i] = jnp.zeros((HEAD_DIM, TILE), F32)
        grad_k[tile_at(i), :] = jnp.zeros((TILE, HEAD_DIM), F32)
        return carry

    lax.fori_loop(0, TILES, clear, 0, unroll=TILES)
    for n in (2, 3):
        each_tile(lambda i, n=n: arrival(i, n).wait())

    def add_pairs(n, pairs):
        tiles = [
            dot(k_hat_ref[pl.ds(at, KEYS), :], q_turned_ref[:, tile_at(i)]) for _, i, at, _ in pairs
        ]
        prob_grads = [
            dot(tile_rows(value_ref, at // BLOCK, 0, KEYS), grad_turned_ref[:, tile_at(i)])
            for _, i, at, _ in pairs
        ]
        tiles = [
            softmax_tile(tile, span_rows_ref, norm_ref, i, mask_at)
            for tile, (_, i, _, mask_at) in zip(tiles, pairs)
        ]
        tiles = [
            (tile * (prob - inner_ref[i, 0:1, :]) * SCALE).astype(BF16)
            for tile, prob, (_, i, _, _) in zip(tiles, prob_grads, pairs)
        ]
        keys = [dot(tile, q_hat_ref[tile_at(i), :]) for tile, (_, i, _, _) in zip(tiles, pairs)]
        queries = [
            dot(k_turned_ref[:, pl.ds(at, KEYS)], tile) for tile, (_, _, at, _) in zip(tiles, pairs)
        ]
        for key, query, (_, i, at, _) in zip(keys, queries, pairs):
            grad_k[pl.ds(at, KEYS), :] += key
            grad_q[i] += query

    each_pairs(total_ref[0], pair_ref, add_pairs)

    gains = jnp.concatenate([gains_ref[...], jnp.zeros((6, HEAD_DIM), F32)], 0).T

    def norm_backward(i, n, grad_hat):
        mean = moments_ref[i, 2 * n : 2 * n + 1, :]
        inverse = moments_ref[i, 2 * n + 1 : 2 * n + 2, :]
        normed = (tile_rows(raw_ref, i * PAIR, n).T.astype(F32) - mean) * inverse
        grad_normed = grad_hat * gains[:, n : n + 1]
        inner = mean_down(grad_normed * normed)
        grad_in = inverse * (grad_normed - mean_down(grad_normed) - normed * inner)
        send_ref[pl.ds(i * PAIR, PAIR), n * BLOCK : (n + 1) * BLOCK, :] = grad_in.astype(
            BF16
        ).T.reshape(PAIR, BLOCK, HEAD_DIM)
        grad_gain = grad_hat * normed
        return sum(grad_gain[:, c : c + 128] for c in range(0, TILE, 128))

    def finish(i, gain_sums):
        arrival(i, 4).wait()
        gain_q, gain_k = gain_sums
        gain_q = gain_q + norm_backward(i, 0, grad_q[i])
        gain_k = gain_k + norm_backward(i, 1, grad_k[tile_at(i), :].T)
        leaving(i).start()
        return gain_q, gain_k

    zero = jnp.zeros((HEAD_DIM, 128), F32)
    gain_q, gain_k = lax.fori_loop(0, TILES, finish, (zero, zero), unroll=TILES)
    gain_out_ref[0:1, :] = jnp.sum(gain_q.T, 0, keepdims=True)
    gain_out_ref[1:2, :] = jnp.sum(gain_k.T, 0, keepdims=True)
    each_tile(lambda i: leaving(i).wait())


def run_backward(pairs, total, received, q_turned, k_hat, grad_turned, *arrays):
    return pl.pallas_call(
        backward_kernel,
        in_specs=[SMEM_SPEC] * 2 + [ANY_SPEC] * 4 + [VMEM_SPEC] * len(arrays),
        out_specs=[ANY_SPEC, VMEM_SPEC],
        out_shape=[shape((BLOCKS, 2 * BLOCK, 128), BF16), shape((2, HEAD_DIM), F32)],
        scratch_shapes=[
            pltpu.VMEM((TILES, HEAD_DIM, TILE), F32),
            pltpu.VMEM((LENGTH, HEAD_DIM), F32),
            pltpu.VMEM((LENGTH, HEAD_DIM), BF16),
            pltpu.VMEM((HEAD_DIM, LENGTH), BF16),
            pltpu.VMEM((BLOCKS, BLOCK, 128), BF16),
            pltpu.VMEM((BLOCKS, 2 * BLOCK, 128), BF16),
            pltpu.VMEM((HEAD_DIM, LENGTH), BF16),
            pltpu.VMEM((LENGTH, HEAD_DIM), BF16),
            pltpu.VMEM((HEAD_DIM, LENGTH), BF16),
            pltpu.VMEM((BLOCKS, 2 * BLOCK, 128), BF16),
            pltpu.SemaphoreType.DMA((5, TILES)),
            pltpu.SemaphoreType.DMA((TILES,)),
        ],
        compiler_params=pltpu.CompilerParams(vmem_limit_bytes=VMEM_LIMIT),
        cost_estimate=WORK,
        name="backward",
    )(pairs, total, received, q_turned, k_hat, grad_turned, *arrays)


def over_packs(value):
    moved = [value]
    for shift in range(1, PACKS):
        pairs = [(i, (i + shift) % PACKS) for i in range(PACKS)]
        moved.append(lax.ppermute(value, "pack", pairs))
    return moved


def exchange(slab):
    return lax.all_to_all(slab, "seq", split_axis=0, concat_axis=0, tiled=True)


def on_device(
    query_rows, key_rows, value_rows, target_rows, norm_gains, segment_ids, group_labels, mixture
):
    gains = norm_gains.reshape(2, HEAD_DIM)
    first = exchange(pack_rows((query_rows, key_rows, value_rows), segment_ids, "pack_first"))

    image_hot = segment_ids[0][:, None] == jnp.arange(IMAGES, dtype=I32)[None, :]
    labels = jnp.sum(jnp.where(image_hot, group_labels[0][None, :], 0), 1)[None, :]
    extra = jnp.concatenate([segment_ids.astype(F32), *over_packs(labels.astype(F32))], 0)
    second = exchange(pack_rows((target_rows,), extra, "pack_second"))

    pairs, total, span_rows, *hats, probs, moments, norms, head_out = run_attend(first, gains)
    send, grad_turned, inner, counts = run_loss(
        group_labels, mixture, pairs, total, second, head_out, probs
    )
    back = exchange(send)
    send, gain_part = run_backward(
        pairs, total, first, *hats, grad_turned, gains, moments, span_rows, norms, inner
    )
    back, send = lax.optimization_barrier((back, send))
    last = exchange(send)
    attended, grad_value = unpack_rows(back, 2, "unpack_first")
    losses = jnp.sum(back[:, 2 * BLOCK : 2 * BLOCK + 3, :GROUPS].astype(F32), (0, 1))
    group_total = sum(over_packs(losses))
    group_loss = group_total / (counts[0, :GROUPS] * (HEADS * HEAD_DIM))
    shares = mixture / jnp.sum(mixture)
    raised = shares * jnp.exp(ETA * group_loss)
    new_mixture = raised / jnp.sum(raised)
    grad_gains = sum(over_packs(gain_part)).reshape(2, 1, HEAD_DIM)
    grad_query, grad_key = unpack_rows(last, 2, "unpack_last")
    return (attended, grad_query, grad_key, grad_value, grad_gains, new_mixture)


def solution(mesh):
    rows = P("pack", "seq", None)
    gains = P(None, "seq", None)
    return jax.shard_map(
        on_device,
        mesh=mesh,
        in_specs=(rows, rows, rows, rows, gains, P("pack", "seq"), P("pack", None), P()),
        out_specs=(rows, rows, rows, rows, gains, P()),
        check_vma=False,
    )
```

```python
import functools

import jax
import jax.numpy as jnp
from jax import lax
from jax.experimental import pallas as pl
from jax.experimental.pallas import tpu as pltpu
from jax.sharding import PartitionSpec as P

HEADS = 32
HEAD_DIM = 128
IMAGES = 16
GROUPS = 8
PACKS = 4
LENGTH = 4096

NEG = -1e30
EPS = 1e-06
ETA = 2.0
SCALE = HEAD_DIM ** (-0.5)
EXP_SCALE = SCALE * 1.4426950408889634

BLOCK = 128
BLOCKS = LENGTH // BLOCK
TILE = 256
TILES = LENGTH // TILE
PAIR = TILE // BLOCK
KEYS = 256
UNROLL = 6
MOST_PAIRS = (LENGTH * (1024 // TILE + 1) + TILES * (BLOCK - 1 + KEYS - 1)) // KEYS
MOST_STEPS = MOST_PAIRS // UNROLL + 1
MOST_PAIRS = MOST_STEPS * UNROLL
RING = 4
SAFE_LOGIT = 70.0
EXTRA = 16
CHUNK = 4
CHUNKS = HEADS // CHUNK
VMEM_LIMIT = 63 * 1024 * 1024

BF16 = jnp.bfloat16
F32 = jnp.float32
I32 = jnp.int32

WORK = pl.CostEstimate(flops=1 << 33, bytes_accessed=1 << 25, transcendentals=1 << 22)

VMEM_SPEC = pl.BlockSpec(memory_space=pltpu.VMEM)
SMEM_SPEC = pl.BlockSpec(memory_space=pltpu.SMEM)
HBM_SPEC = pl.BlockSpec(memory_space=pltpu.HBM)


def shape(dims, dtype):
    return jax.ShapeDtypeStruct(dims, dtype)


def head_columns(h):
    return pl.ds(h * HEAD_DIM, HEAD_DIM)


def pack_kernel(count, *refs):
    row_refs, (extra_ref, out_ref, rows, slab, in_sems, out_sems) = refs[:count], refs[count:]

    def arrival(c, n):
        columns = pl.ds(c * CHUNK * HEAD_DIM, CHUNK * HEAD_DIM)
        return pltpu.make_async_copy(
            row_refs[n].at[0, :, columns], rows.at[n, :, columns], in_sems.at[n, c]
        )

    def leaving(c):
        heads = pl.ds(c * CHUNK, CHUNK)
        return pltpu.make_async_copy(slab.at[heads], out_ref.at[heads], out_sems.at[c])

    for c in range(CHUNKS):
        for n in range(count):
            arrival(c, n).start()
    extra = extra_ref[...].astype(F32)
    extra = jnp.concatenate([extra, jnp.zeros((EXTRA - extra.shape[0], 128), F32)], 0)
    slab[:, count * BLOCK :, :] = jnp.broadcast_to(extra.astype(BF16)[None], (HEADS, EXTRA, 128))
    for c in range(CHUNKS):
        for n in range(count):
            arrival(c, n).wait()
            for h in range(c * CHUNK, (c + 1) * CHUNK):
                block = rows[n, :, h * HEAD_DIM : (h + 1) * HEAD_DIM]
                slab[h, n * BLOCK : (n + 1) * BLOCK, :] = block.T
        leaving(c).start()
    for c in range(CHUNKS):
        leaving(c).wait()


def pack_rows(rows, extra, name):
    count = len(rows)
    slab = (HEADS, count * BLOCK + EXTRA, 128)
    return pl.pallas_call(
        functools.partial(pack_kernel, count),
        in_specs=[HBM_SPEC] * count + [VMEM_SPEC],
        out_specs=HBM_SPEC,
        out_shape=shape(slab, BF16),
        scratch_shapes=[
            pltpu.VMEM((count, BLOCK, HEADS * HEAD_DIM), BF16),
            pltpu.VMEM(slab, BF16),
            pltpu.SemaphoreType.DMA((count, CHUNKS)),
            pltpu.SemaphoreType.DMA((CHUNKS,)),
        ],
        compiler_params=pltpu.CompilerParams(vmem_limit_bytes=VMEM_LIMIT),
        name=name,
    )(*rows, extra)


def unpack_kernel(turned, in_ref, *refs):
    *row_refs, slab, rows, in_sems, out_sems = refs
    lines = len(row_refs) * BLOCK

    def arrival(c):
        heads = pl.ds(c * CHUNK, CHUNK)
        return pltpu.make_async_copy(
            in_ref.at[heads, pl.ds(0, lines), :], slab.at[heads], in_sems.at[c]
        )

    def leaving(h, n):
        columns = head_columns(h)
        source = slab.at[h, pl.ds(n * BLOCK, BLOCK), :]
        if n in turned:
            source = rows.at[:, columns]
        return pltpu.make_async_copy(source, row_refs[n].at[0, :, columns], out_sems.at[n, h])

    for c in range(CHUNKS):
        arrival(c).start()
    for c in range(CHUNKS):
        arrival(c).wait()
        for h in range(c * CHUNK, (c + 1) * CHUNK):
            for n in range(len(row_refs)):
                if n in turned:
                    block = slab[h, n * BLOCK : (n + 1) * BLOCK, :]
                    rows[:, h * HEAD_DIM : (h + 1) * HEAD_DIM] = block.T
                leaving(h, n).start()
    for h in range(HEADS):
        for n in range(len(row_refs)):
            leaving(h, n).wait()


def unpack_rows(slab, count, turned, name):
    return pl.pallas_call(
        functools.partial(unpack_kernel, turned),
        in_specs=[HBM_SPEC],
        out_specs=[HBM_SPEC] * count,
        out_shape=[shape((1, BLOCK, HEADS * HEAD_DIM), BF16)] * count,
        scratch_shapes=[
            pltpu.VMEM((HEADS, count * BLOCK, 128), BF16),
            pltpu.VMEM((BLOCK, HEADS * HEAD_DIM), BF16),
            pltpu.SemaphoreType.DMA((CHUNKS,)),
            pltpu.SemaphoreType.DMA((count, HEADS)),
        ],
        compiler_params=pltpu.CompilerParams(vmem_limit_bytes=VMEM_LIMIT),
        name=name,
    )(slab)


def dot(a, b, contract=((1,), (0,))):
    return lax.dot_general(a, b, (contract, ((), ())), preferred_element_type=F32)


def tile_turned(ref, block, part):
    lines = slice(part * BLOCK, (part + 1) * BLOCK)
    return jnp.concatenate([ref[block + b, lines, :] for b in range(PAIR)], 1)


def tile_at(i, size=TILE):
    return pl.ds(pl.multiple_of(i * size, size), size)


def mean_down(values):
    return jnp.sum(values, 0, keepdims=True) * (1.0 / HEAD_DIM)


def block_row(b):
    return b // PAIR, slice((b % PAIR) * BLOCK, (b % PAIR + 1) * BLOCK)


def group_sums(group, values):
    lane = lax.broadcasted_iota(I32, (1, 128), 1)
    sums = jnp.zeros((1, 128), F32)
    for g in range(GROUPS):
        part = jnp.sum(jnp.where(group == float(g), values, 0.0), 0, keepdims=True)
        sums = jnp.where(lane == g, jnp.sum(part, 1, keepdims=True), sums)
    return sums


def key_mask(span_rows_ref, i, start, step):
    first = span_rows_ref[i, 0:1, :] - start
    count = span_rows_ref[i, 1:2, :]
    row = lax.broadcasted_iota(I32, (step, TILE), 0)
    return (row - first).astype(jnp.uint32) < count.astype(jnp.uint32)


def masked(scores, span_rows_ref, i, mask_at):
    return jnp.where(key_mask(span_rows_ref, i, mask_at, KEYS), scores, NEG)


def pair_steps(total):
    return (total + UNROLL - 1) // UNROLL


def each_pairs(total, pair_ref, body):
    def some(n, carry):
        pairs = []
        for u in range(UNROLL):
            p = n * UNROLL + u
            at = pl.multiple_of(pair_ref[1, p], BLOCK)
            pairs.append((p, pair_ref[0, p], at, pair_ref[2, p]))
        body(n, pairs)
        return carry

    lax.fori_loop(0, pair_steps(total), some, 0)


def softmax_tile(scores, span_rows_ref, norm_ref, i, mask_at):
    scores = masked(scores, span_rows_ref, i, mask_at)
    return jnp.exp2(scores * EXP_SCALE - norm_ref[i, 0:1, :]) * norm_ref[i, 1:2, :]


def find_pairs(seg_all, starts, pair_ref, span_rows_ref):
    for s in range(IMAGES + 1):
        starts[s] = jnp.sum((seg_all < float(s)).astype(F32)).astype(I32)
    first = jnp.zeros((BLOCKS, 128), I32)
    count = jnp.zeros((BLOCKS, 128), I32)
    for s in range(IMAGES):
        here = seg_all == float(s)
        first = jnp.where(here, starts[s], first)
        count = jnp.where(here, starts[s + 1] - starts[s], count)
    for b in range(BLOCKS):
        tile, at = block_row(b)
        span_rows_ref[tile, 0:1, at] = first[b : b + 1, :]
        span_rows_ref[tile, 1:2, at] = count[b : b + 1, :]

    def span(i, total):
        low, high = jnp.int32(0), jnp.int32(LENGTH)
        for s in range(1, IMAGES):
            low = jnp.where(starts[s] <= i * TILE, starts[s], low)
        for s in range(IMAGES - 1, 0, -1):
            high = jnp.where(starts[s] > i * TILE + TILE - 1, starts[s], high)
        low = (low // BLOCK) * BLOCK
        steps = (high - low + KEYS - 1) // KEYS
        low = jnp.minimum(low, LENGTH - steps * KEYS)

        def add(j, carry):
            pair_ref[0, total + j] = i
            pair_ref[1, total + j] = low + j * KEYS
            pair_ref[2, total + j] = low + j * KEYS
            return carry

        lax.fori_loop(0, steps, add, 0)
        return total + steps

    total = lax.fori_loop(0, TILES, span, jnp.int32(0))
    for u in range(UNROLL):
        pair_ref[0, total + u] = 0
        pair_ref[1, total + u] = 0
        pair_ref[2, total + u] = -(1 << 20)
    return total


def each_tile(what):
    def one(i, carry):
        what(i)
        return carry

    lax.fori_loop(0, TILES, one, 0)


def tile_blocks(i):
    return pl.ds(i * PAIR, PAIR)


def attend_kernel(
    all_ref, gains_ref,
    pair_ref, total_ref, span_rows_ref, *refs,
):
    hat_outs, probs_out, refs = refs[:2], refs[2], refs[3:]
    (moments_ref, norm_ref, out_ref), refs = refs[:3], refs[3:]
    hats, refs = refs[:2], refs[2:]
    q_turned_ref, k_hat_ref = hats
    recv_ref, extra_ref, starts, terms, fold, probs, sums = refs[:7]
    in_sems, extra_sem, out_sems, prob_sems = refs[7:]

    def arrival(i):
        return pltpu.make_async_copy(
            all_ref.at[tile_blocks(i), pl.ds(0, 3 * BLOCK), :],
            recv_ref.at[tile_blocks(i)],
            in_sems.at[i],
        )

    def leaving(i, n):
        rows = tile_at(i)
        source, target = (
            (q_turned_ref.at[:, rows], hat_outs[0].at[:, rows]),
            (k_hat_ref.at[rows, :], hat_outs[1].at[rows, :]),
            (sums.at[i], out_ref.at[i]),
        )[n]
        return pltpu.make_async_copy(source, target, out_sems.at[n, i])

    extra = pltpu.make_async_copy(
        all_ref.at[:, pl.ds(3 * BLOCK, EXTRA), :], extra_ref, extra_sem.at[0]
    )
    extra.start()
    each_tile(lambda i: arrival(i).start())
    extra.wait()
    total = find_pairs(extra_ref[:, 0, :].astype(F32), starts, pair_ref, span_rows_ref)
    total_ref[0] = total
    gains = jnp.concatenate([gains_ref[...], jnp.zeros((6, HEAD_DIM), F32)], 0).T

    def prepare(i, most):
        arrival(i).wait()
        rows = tile_at(i)
        sizes = []
        for n in range(2):
            values = tile_turned(recv_ref, i * PAIR, n).astype(F32)
            mean = mean_down(values)
            centre = values - mean
            inverse = lax.rsqrt(mean_down(centre * centre) + EPS)
            moments_ref[i, 2 * n : 2 * n + 1, :] = mean
            moments_ref[i, 2 * n + 1 : 2 * n + 2, :] = inverse
            hat = centre * inverse * gains[:, n : n + 1]
            sizes.append(jnp.maximum(most[n], mean_down(hat * hat)))
            if n == 0:
                q_turned_ref[:, rows] = hat.astype(BF16)
            else:
                k_hat_ref[rows, :] = hat.astype(BF16).T
        for n in range(2):
            leaving(i, n).start()
        sums[i] = jnp.zeros((HEAD_DIM, TILE), F32)
        norm_ref[i] = jnp.zeros((2, TILE), F32)
        fold[i] = jnp.zeros((8, TILE), F32)
        return tuple(sizes)

    zero = jnp.zeros((1, TILE), F32)
    most_q, most_k = lax.fori_loop(0, TILES, prepare, (zero, zero), unroll=TILES)
    bound = jnp.max(most_q) * jnp.max(most_k) * HEAD_DIM

    def scores_of(pairs):
        tiles = [
            dot(k_hat_ref[pl.ds(at, KEYS), :], q_turned_ref[:, tile_at(i)]) for _, i, at, _ in pairs
        ]
        return [
            masked(tile, span_rows_ref, i, mask_at)
            for tile, (_, i, _, mask_at) in zip(tiles, pairs)
        ]

    @pl.when(jnp.logical_not(bound <= SAFE_LOGIT * SAFE_LOGIT))
    def _():
        def clear(i, carry):
            fold[i] = jnp.full((8, TILE), NEG, F32)
            return carry

        lax.fori_loop(0, TILES, clear, 0)

        def top_pairs(n, pairs):
            for tile, (_, i, _, _) in zip(scores_of(pairs), pairs):
                top = jnp.max(tile.reshape(KEYS // 8, 8, TILE), 0)
                fold[i] = jnp.maximum(fold[i], top)

        each_pairs(total, pair_ref, top_pairs)

        def finish(i, carry):
            norm_ref[i, 0:1, :] = jnp.max(fold[i], 0, keepdims=True) * EXP_SCALE
            fold[i] = jnp.zeros((8, TILE), F32)
            return carry

        lax.fori_loop(0, TILES, finish, 0)

    def exp_pairs(n, pairs):
        sums = []
        for tile, (p, i, _, _) in zip(scores_of(pairs), pairs):
            tile = jnp.exp2(tile * EXP_SCALE - norm_ref[i, 0:1, :])
            terms[p] = tile
            sums.append(jnp.sum(tile.reshape(KEYS // 8, 8, TILE), 0))
        for part, (_, i, _, _) in zip(sums, pairs):
            fold[i] += part

    each_pairs(total, pair_ref, exp_pairs)

    def invert(i, carry):
        norm_ref[i, 1:2, :] = 1.0 / jnp.sum(fold[i], 0, keepdims=True)
        return carry

    lax.fori_loop(0, TILES, invert, 0)

    def give_probs(n):
        slot = lax.rem(n, RING)
        return pltpu.make_async_copy(probs.at[slot], probs_out.at[n], prob_sems.at[slot])

    def out_pairs(n, pairs):
        slot = lax.rem(n, RING)

        @pl.when(n >= RING)
        def _():
            give_probs(n - RING).wait()

        tiles = [(terms[p] * norm_ref[i, 1:2, :]).astype(BF16) for p, i, _, _ in pairs]
        for u, tile in enumerate(tiles):
            probs[slot, u] = tile
        give_probs(n).start()
        tiles = [
            dot(tile_turned(recv_ref, at // BLOCK, 2), tile)
            for tile, (_, _, at, _) in zip(tiles, pairs)
        ]
        for tile, (_, i, _, _) in zip(tiles, pairs):
            sums[i] += tile

    each_pairs(total, pair_ref, out_pairs)
    each_tile(lambda i: leaving(i, 2).start())
    steps = pair_steps(total)

    def end(n, carry):
        give_probs(n).wait()
        return carry

    lax.fori_loop(jnp.maximum(steps - RING, 0), steps, end, 0)
    for n in range(3):
        each_tile(lambda i, n=n: leaving(i, n).wait())


def run_attend(received, gains):
    hats = [((HEAD_DIM, LENGTH), BF16), ((LENGTH, HEAD_DIM), BF16)]
    return pl.pallas_call(
        attend_kernel,
        in_specs=[HBM_SPEC, VMEM_SPEC],
        out_specs=[SMEM_SPEC] * 2 + [VMEM_SPEC] + [HBM_SPEC] * 3 + [VMEM_SPEC] * 2 + [HBM_SPEC],
        out_shape=[
            shape((3, MOST_PAIRS), I32),
            shape((1,), I32),
            shape((TILES, 2, TILE), I32),
            *[shape(*hat) for hat in hats],
            shape((MOST_STEPS, UNROLL, KEYS, TILE), BF16),
            shape((TILES, 4, TILE), F32),
            shape((TILES, 2, TILE), F32),
            shape((TILES, HEAD_DIM, TILE), F32),
        ],
        scratch_shapes=[
            *[pltpu.VMEM(*hat) for hat in hats],
            pltpu.VMEM((BLOCKS, 3 * BLOCK, 128), BF16),
            pltpu.VMEM((BLOCKS, EXTRA, 128), BF16),
            pltpu.SMEM((IMAGES + 1,), I32),
            pltpu.VMEM((MOST_PAIRS, KEYS, TILE), F32),
            pltpu.VMEM((TILES, 8, TILE), F32),
            pltpu.VMEM((RING, UNROLL, KEYS, TILE), BF16),
            pltpu.VMEM((TILES, HEAD_DIM, TILE), F32),
            pltpu.SemaphoreType.DMA((TILES,)),
            pltpu.SemaphoreType.DMA((1,)),
            pltpu.SemaphoreType.DMA((3, TILES)),
            pltpu.SemaphoreType.DMA((RING,)),
        ],
        compiler_params=pltpu.CompilerParams(vmem_limit_bytes=VMEM_LIMIT),
        cost_estimate=WORK,
        name="attend",
    )(received, gains)


def loss_kernel(
    labels_ref, mixture_ref, pair_ref, total_ref,
    all_ref, out_in, probs_in,
    send_out, grad_turned_out, inner_ref, counts_ref,
    coef_rows, loss_rows, grad_low, grad_v, probs, recv_ref, extra_ref, out_ref, first_ref, value_ref,
    grad_turned_ref, sems, in_sems, extra_sem, out_sems,
):
    def arrival(i, n):
        source, target = (
            (all_ref.at[tile_blocks(i), pl.ds(0, BLOCK), :], recv_ref.at[tile_blocks(i)]),
            (out_in.at[i], out_ref.at[i]),
        )[n]
        return pltpu.make_async_copy(source, target, in_sems.at[n, i])

    def leaving(i, n):
        rows = tile_at(i)
        blocks = tile_blocks(i)
        source, target = (
            (first_ref.at[blocks], send_out.at[blocks, pl.ds(0, BLOCK), :]),
            (grad_turned_ref.at[:, rows], grad_turned_out.at[:, rows]),
            (value_ref.at[blocks], send_out.at[blocks, pl.ds(BLOCK, BLOCK + EXTRA), :]),
        )[n]
        return pltpu.make_async_copy(source, target, out_sems.at[n, i])

    def take_probs(n):
        return pltpu.make_async_copy(probs_in.at[n], probs.at[n], sems.at[n])

    def start_probs(n, carry):
        take_probs(n).start()
        return carry

    extra = pltpu.make_async_copy(
        all_ref.at[:, pl.ds(BLOCK, EXTRA), :], extra_ref, extra_sem.at[0]
    )
    extra.start()
    for n in range(2):
        each_tile(lambda i, n=n: arrival(i, n).start())
    lax.fori_loop(0, pair_steps(total_ref[0]), start_probs, 0)

    extra.wait()
    seg_all = extra_ref[:, 0, :].astype(F32)
    group = jnp.zeros((BLOCKS, 128), F32)
    for s in range(IMAGES):
        group = jnp.where(seg_all == float(s), labels_ref[0, s].astype(F32), group)
    others = [extra_ref[:, 1 + p, :].astype(F32) for p in range(PACKS)]
    total_mix = mixture_ref[0]
    for g in range(1, GROUPS):
        total_mix = total_mix + mixture_ref[g]
    lane = lax.broadcasted_iota(I32, (1, 128), 1)
    coef = jnp.zeros((BLOCKS, 128), F32)
    count_row = jnp.zeros((1, 128), F32)
    for g in range(GROUPS):
        hits = sum((other == float(g)).astype(F32) for other in others)
        count = jnp.sum(jnp.sum(hits, 0, keepdims=True), 1, keepdims=True)
        share = jnp.full((1, 1), mixture_ref[g], F32) / total_mix
        coef = jnp.where(group == float(g), share / (count * (HEADS * HEAD_DIM)), coef)
        count_row = jnp.where(lane == g, count, count_row)
    counts_ref[...] = count_row
    for b in range(BLOCKS):
        tile, at = block_row(b)
        coef_rows[tile, 0:1, at] = coef[b : b + 1, :]

    def finish(i, carry):
        for n in range(2):
            arrival(i, n).wait()
        rows = tile_at(i)
        head_out = out_ref[i]
        misfit = head_out - tile_turned(recv_ref, i * PAIR, 0).astype(F32)
        loss_rows[i, 0:1, :] = 0.5 * jnp.sum(misfit * misfit, 0, keepdims=True)
        grad_out = coef_rows[i, 0:1, :] * misfit
        inner_ref[i, 0:1, :] = jnp.sum(grad_out * head_out, 0, keepdims=True)
        grad_turned = grad_out.astype(BF16)
        grad_turned_ref[:, rows] = grad_turned
        grad_low[rows, :] = grad_turned.T
        grad_v[rows, :] = jnp.zeros((TILE, HEAD_DIM), F32)
        low = head_out.astype(BF16)
        for b in range(PAIR):
            first_ref[i * PAIR + b] = low[:, b * BLOCK : (b + 1) * BLOCK]
        for n in range(2):
            leaving(i, n).start()
        return carry

    lax.fori_loop(0, TILES, finish, 0, unroll=TILES)

    rows = [block_row(b) for b in range(BLOCKS)]
    losses = jnp.concatenate([loss_rows[tile, 0:1, at] for tile, at in rows], 0)
    loss_row = group_sums(group, losses)
    high = loss_row.astype(BF16)
    left = loss_row - high.astype(F32)
    middle = left.astype(BF16)
    low = (left - middle.astype(F32)).astype(BF16)
    row = lax.broadcasted_iota(I32, (EXTRA, 128), 0)
    pieces = jnp.zeros((EXTRA, 128), F32)
    for n, piece in enumerate((high, middle, low)):
        pieces = jnp.where(row == n, piece.astype(F32), pieces)
    value_ref[:, BLOCK:, :] = jnp.broadcast_to(pieces.astype(BF16)[None], (BLOCKS, EXTRA, 128))

    def add_pairs(n, pairs):
        take_probs(n).wait()
        tiles = [dot(probs[n, u], grad_low[tile_at(pair[1]), :]) for u, pair in enumerate(pairs)]
        for tile, (_, _, at, _) in zip(tiles, pairs):
            grad_v[pl.ds(at, KEYS), :] += tile

    each_pairs(total_ref[0], pair_ref, add_pairs)

    def give(i, carry):
        value_ref[pl.ds(i * PAIR, PAIR), 0:BLOCK, :] = (
            grad_v[tile_at(i), :].astype(BF16).reshape(PAIR, BLOCK, HEAD_DIM)
        )
        leaving(i, 2).start()
        return carry

    lax.fori_loop(0, TILES, give, 0, unroll=TILES)
    for n in range(3):
        each_tile(lambda i, n=n: leaving(i, n).wait())


def run_loss(labels, mixture, pairs, total, second, head_out, probs):
    return pl.pallas_call(
        loss_kernel,
        in_specs=[SMEM_SPEC] * 4 + [HBM_SPEC] * 3,
        out_specs=[HBM_SPEC] * 2 + [VMEM_SPEC] * 2,
        out_shape=[
            shape((BLOCKS, 2 * BLOCK + EXTRA, 128), BF16),
            shape((HEAD_DIM, LENGTH), BF16),
            shape((TILES, 1, TILE), F32),
            shape((1, 128), F32),
        ],
        scratch_shapes=[
            pltpu.VMEM((TILES, 1, TILE), F32),
            pltpu.VMEM((TILES, 1, TILE), F32),
            pltpu.VMEM((LENGTH, HEAD_DIM), BF16),
            pltpu.VMEM((LENGTH, HEAD_DIM), F32),
            pltpu.VMEM((MOST_STEPS, UNROLL, KEYS, TILE), BF16),
            pltpu.VMEM((BLOCKS, BLOCK, 128), BF16),
            pltpu.VMEM((BLOCKS, EXTRA, 128), BF16),
            pltpu.VMEM((TILES, HEAD_DIM, TILE), F32),
            pltpu.VMEM((BLOCKS, BLOCK, 128), BF16),
            pltpu.VMEM((BLOCKS, BLOCK + EXTRA, 128), BF16),
            pltpu.VMEM((HEAD_DIM, LENGTH), BF16),
            pltpu.SemaphoreType.DMA((MOST_STEPS,)),
            pltpu.SemaphoreType.DMA((2, TILES)),
            pltpu.SemaphoreType.DMA((1,)),
            pltpu.SemaphoreType.DMA((3, TILES)),
        ],
        compiler_params=pltpu.CompilerParams(vmem_limit_bytes=VMEM_LIMIT),
        name="loss_and_grad_value",
    )(labels, mixture, pairs, total, second, head_out, probs)


def backward_kernel(
    pair_ref, total_ref,
    all_ref, q_turned_in, k_hat_in, grad_turned_in,
    gains_ref, moments_ref, span_rows_ref, norm_ref, inner_ref,
    send_out, gain_out_ref,
    grad_q, grad_k, q_hat_ref, k_turned_ref, value_ref, raw_ref, q_turned_ref, k_hat_ref,
    grad_turned_ref, send_ref, in_sems, out_sems,
):
    def arrival(i, n):
        rows = tile_at(i)
        blocks = tile_blocks(i)
        source, target = (
            (q_turned_in.at[:, rows], q_turned_ref.at[:, rows]),
            (k_hat_in.at[rows, :], k_hat_ref.at[rows, :]),
            (all_ref.at[blocks, pl.ds(0, 3 * BLOCK), :], raw_ref.at[blocks]),
            (grad_turned_in.at[:, rows], grad_turned_ref.at[:, rows]),
        )[n]
        return pltpu.make_async_copy(source, target, in_sems.at[n, i])

    def leaving(i):
        blocks = tile_blocks(i)
        return pltpu.make_async_copy(send_ref.at[blocks], send_out.at[blocks], out_sems.at[i])

    for n in range(4):
        each_tile(lambda i, n=n: arrival(i, n).start())

    def clear(i, carry):
        for n in range(2):
            arrival(i, n).wait()
        q_hat_ref[tile_at(i), :] = q_turned_ref[:, tile_at(i)].T
        k_turned_ref[:, tile_at(i)] = k_hat_ref[tile_at(i), :].T
        arrival(i, 2).wait()
        value_ref[tile_at(i), :] = tile_turned(raw_ref, i * PAIR, 2).T
        grad_q[i] = jnp.zeros((HEAD_DIM, TILE), F32)
        grad_k[tile_at(i), :] = jnp.zeros((TILE, HEAD_DIM), F32)
        return carry

    lax.fori_loop(0, TILES, clear, 0, unroll=TILES)
    each_tile(lambda i: arrival(i, 3).wait())

    def add_pairs(n, pairs):
        tiles = [
            dot(k_hat_ref[pl.ds(at, KEYS), :], q_turned_ref[:, tile_at(i)]) for _, i, at, _ in pairs
        ]
        prob_grads = [
            dot(value_ref[pl.ds(at, KEYS), :], grad_turned_ref[:, tile_at(i)])
            for _, i, at, _ in pairs
        ]
        tiles = [
            softmax_tile(tile, span_rows_ref, norm_ref, i, mask_at)
            for tile, (_, i, _, mask_at) in zip(tiles, pairs)
        ]
        tiles = [
            (tile * (prob - inner_ref[i, 0:1, :]) * SCALE).astype(BF16)
            for tile, prob, (_, i, _, _) in zip(tiles, prob_grads, pairs)
        ]
        keys = [dot(tile, q_hat_ref[tile_at(i), :]) for tile, (_, i, _, _) in zip(tiles, pairs)]
        queries = [
            dot(k_turned_ref[:, pl.ds(at, KEYS)], tile) for tile, (_, _, at, _) in zip(tiles, pairs)
        ]
        for key, query, (_, i, at, _) in zip(keys, queries, pairs):
            grad_k[pl.ds(at, KEYS), :] += key
            grad_q[i] += query

    each_pairs(total_ref[0], pair_ref, add_pairs)

    gains = jnp.concatenate([gains_ref[...], jnp.zeros((6, HEAD_DIM), F32)], 0).T

    def norm_backward(i, n, grad_hat):
        mean = moments_ref[i, 2 * n : 2 * n + 1, :]
        inverse = moments_ref[i, 2 * n + 1 : 2 * n + 2, :]
        normed = (tile_turned(raw_ref, i * PAIR, n).astype(F32) - mean) * inverse
        grad_normed = grad_hat * gains[:, n : n + 1]
        inner = mean_down(grad_normed * normed)
        grad_in = inverse * (grad_normed - mean_down(grad_normed) - normed * inner)
        send_ref[pl.ds(i * PAIR, PAIR), n * BLOCK : (n + 1) * BLOCK, :] = grad_in.astype(
            BF16
        ).T.reshape(PAIR, BLOCK, HEAD_DIM)
        grad_gain = grad_hat * normed
        return sum(grad_gain[:, c : c + 128] for c in range(0, TILE, 128))

    def finish(i, gain_sums):
        gain_q, gain_k = gain_sums
        gain_q = gain_q + norm_backward(i, 0, grad_q[i])
        gain_k = gain_k + norm_backward(i, 1, grad_k[tile_at(i), :].T)
        leaving(i).start()
        return gain_q, gain_k

    zero = jnp.zeros((HEAD_DIM, 128), F32)
    gain_q, gain_k = lax.fori_loop(0, TILES, finish, (zero, zero), unroll=TILES)
    gain_out_ref[0:1, :] = jnp.sum(gain_q.T, 0, keepdims=True)
    gain_out_ref[1:2, :] = jnp.sum(gain_k.T, 0, keepdims=True)
    each_tile(lambda i: leaving(i).wait())


def run_backward(pairs, total, received, q_turned, k_hat, grad_turned, *arrays):
    return pl.pallas_call(
        backward_kernel,
        in_specs=[SMEM_SPEC] * 2 + [HBM_SPEC] * 4 + [VMEM_SPEC] * len(arrays),
        out_specs=[HBM_SPEC, VMEM_SPEC],
        out_shape=[shape((BLOCKS, 2 * BLOCK, 128), BF16), shape((2, HEAD_DIM), F32)],
        scratch_shapes=[
            pltpu.VMEM((TILES, HEAD_DIM, TILE), F32),
            pltpu.VMEM((LENGTH, HEAD_DIM), F32),
            pltpu.VMEM((LENGTH, HEAD_DIM), BF16),
            pltpu.VMEM((HEAD_DIM, LENGTH), BF16),
            pltpu.VMEM((LENGTH, HEAD_DIM), BF16),
            pltpu.VMEM((BLOCKS, 3 * BLOCK, 128), BF16),
            pltpu.VMEM((HEAD_DIM, LENGTH), BF16),
            pltpu.VMEM((LENGTH, HEAD_DIM), BF16),
            pltpu.VMEM((HEAD_DIM, LENGTH), BF16),
            pltpu.VMEM((BLOCKS, 2 * BLOCK, 128), BF16),
            pltpu.SemaphoreType.DMA((4, TILES)),
            pltpu.SemaphoreType.DMA((TILES,)),
        ],
        compiler_params=pltpu.CompilerParams(vmem_limit_bytes=VMEM_LIMIT),
        cost_estimate=WORK,
        name="backward",
    )(pairs, total, received, q_turned, k_hat, grad_turned, *arrays)


def over_packs(value):
    moved = [value]
    for shift in range(1, PACKS):
        pairs = [(i, (i + shift) % PACKS) for i in range(PACKS)]
        moved.append(lax.ppermute(value, "pack", pairs))
    return moved


def exchange(slab):
    return lax.all_to_all(slab, "seq", split_axis=0, concat_axis=0, tiled=True)


def on_device(
    query_rows, key_rows, value_rows, target_rows, norm_gains, segment_ids, group_labels, mixture
):
    gains = norm_gains.reshape(2, HEAD_DIM)
    first = exchange(pack_rows((query_rows, key_rows, value_rows), segment_ids, "pack_first"))

    image_hot = segment_ids[0][:, None] == jnp.arange(IMAGES, dtype=I32)[None, :]
    labels = jnp.sum(jnp.where(image_hot, group_labels[0][None, :], 0), 1)[None, :]
    extra = jnp.concatenate([segment_ids.astype(F32), *over_packs(labels.astype(F32))], 0)
    second = exchange(pack_rows((target_rows,), extra, "pack_second"))

    pairs, total, span_rows, *hats, probs, moments, norms, head_out = run_attend(first, gains)
    send, grad_turned, inner, counts = run_loss(
        group_labels, mixture, pairs, total, second, head_out, probs
    )
    back = exchange(send)
    send, gain_part = run_backward(
        pairs, total, first, *hats, grad_turned, gains, moments, span_rows, norms, inner
    )
    back, send = lax.optimization_barrier((back, send))
    last = exchange(send)
    attended, grad_value = unpack_rows(back, 2, (0,), "unpack_first")
    losses = jnp.sum(back[:, 2 * BLOCK : 2 * BLOCK + 3, :GROUPS].astype(F32), (0, 1))
    group_total = sum(over_packs(losses))
    group_loss = group_total / (counts[0, :GROUPS] * (HEADS * HEAD_DIM))
    shares = mixture / jnp.sum(mixture)
    raised = shares * jnp.exp(ETA * group_loss)
    new_mixture = raised / jnp.sum(raised)
    grad_gains = sum(over_packs(gain_part)).reshape(2, 1, HEAD_DIM)
    grad_query, grad_key = unpack_rows(last, 2, (), "unpack_last")
    return (attended, grad_query, grad_key, grad_value, grad_gains, new_mixture)


def solution(mesh):
    rows = P("pack", "seq", None)
    gains = P(None, "seq", None)
    return jax.shard_map(
        on_device,
        mesh=mesh,
        in_specs=(rows, rows, rows, rows, gains, P("pack", "seq"), P("pack", None), P()),
        out_specs=(rows, rows, rows, rows, gains, P()),
        check_vma=False,
    )
```

```python
import functools

import jax
import jax.numpy as jnp
from jax import lax
from jax.experimental import pallas as pl
from jax.experimental.pallas import tpu as pltpu
from jax.sharding import PartitionSpec as P

HEADS = 32
HEAD_DIM = 128
IMAGES = 16
GROUPS = 8
PACKS = 4
LENGTH = 4096

NEG = -1e30
EPS = 1e-06
ETA = 2.0
SCALE = HEAD_DIM ** (-0.5)
EXP_SCALE = SCALE * 1.4426950408889634

BLOCK = 128
BLOCKS = LENGTH // BLOCK
TILE = 256
TILES = LENGTH // TILE
PAIR = TILE // BLOCK
KEYS = 256
UNROLL = 8
MOST_PAIRS = (LENGTH * (1024 // TILE + 1) + TILES * (BLOCK - 1 + KEYS - 1)) // KEYS
MOST_STEPS = MOST_PAIRS // UNROLL + 1
MOST_PAIRS = MOST_STEPS * UNROLL
RING = 4
SAFE_LOGIT = 70.0
EXTRA = 16
CHUNK = 4
CHUNKS = HEADS // CHUNK
VMEM_LIMIT = 63 * 1024 * 1024

BF16 = jnp.bfloat16
F32 = jnp.float32
I32 = jnp.int32

WORK = pl.CostEstimate(flops=1 << 33, bytes_accessed=1 << 25, transcendentals=1 << 22)

VMEM_SPEC = pl.BlockSpec(memory_space=pltpu.VMEM)
SMEM_SPEC = pl.BlockSpec(memory_space=pltpu.SMEM)
HBM_SPEC = pl.BlockSpec(memory_space=pltpu.HBM)


def shape(dims, dtype):
    return jax.ShapeDtypeStruct(dims, dtype)


def head_columns(h):
    return pl.ds(h * HEAD_DIM, HEAD_DIM)


def pack_kernel(count, *refs):
    row_refs, (extra_ref, out_ref, rows, slab, in_sems, out_sems) = refs[:count], refs[count:]

    def arrival(c, n):
        columns = pl.ds(c * CHUNK * HEAD_DIM, CHUNK * HEAD_DIM)
        return pltpu.make_async_copy(
            row_refs[n].at[0, :, columns], rows.at[n, :, columns], in_sems.at[n, c]
        )

    def leaving(c):
        heads = pl.ds(c * CHUNK, CHUNK)
        return pltpu.make_async_copy(slab.at[heads], out_ref.at[heads], out_sems.at[c])

    for c in range(CHUNKS):
        for n in range(count):
            arrival(c, n).start()
    extra = extra_ref[...].astype(F32)
    extra = jnp.concatenate([extra, jnp.zeros((EXTRA - extra.shape[0], 128), F32)], 0)
    slab[:, count * BLOCK :, :] = jnp.broadcast_to(extra.astype(BF16)[None], (HEADS, EXTRA, 128))
    for c in range(CHUNKS):
        for n in range(count):
            arrival(c, n).wait()
            for h in range(c * CHUNK, (c + 1) * CHUNK):
                block = rows[n, :, h * HEAD_DIM : (h + 1) * HEAD_DIM]
                slab[h, n * BLOCK : (n + 1) * BLOCK, :] = block.T
        leaving(c).start()
    for c in range(CHUNKS):
        leaving(c).wait()


def pack_rows(rows, extra, name):
    count = len(rows)
    slab = (HEADS, count * BLOCK + EXTRA, 128)
    return pl.pallas_call(
        functools.partial(pack_kernel, count),
        in_specs=[HBM_SPEC] * count + [VMEM_SPEC],
        out_specs=HBM_SPEC,
        out_shape=shape(slab, BF16),
        scratch_shapes=[
            pltpu.VMEM((count, BLOCK, HEADS * HEAD_DIM), BF16),
            pltpu.VMEM(slab, BF16),
            pltpu.SemaphoreType.DMA((count, CHUNKS)),
            pltpu.SemaphoreType.DMA((CHUNKS,)),
        ],
        compiler_params=pltpu.CompilerParams(vmem_limit_bytes=VMEM_LIMIT),
        name=name,
    )(*rows, extra)


def unpack_kernel(turned, in_ref, *refs):
    *row_refs, slab, rows, in_sems, out_sems = refs
    lines = len(row_refs) * BLOCK

    def arrival(c):
        heads = pl.ds(c * CHUNK, CHUNK)
        return pltpu.make_async_copy(
            in_ref.at[heads, pl.ds(0, lines), :], slab.at[heads], in_sems.at[c]
        )

    def leaving(h, n):
        columns = head_columns(h)
        source = slab.at[h, pl.ds(n * BLOCK, BLOCK), :]
        if n in turned:
            source = rows.at[:, columns]
        return pltpu.make_async_copy(source, row_refs[n].at[0, :, columns], out_sems.at[n, h])

    for c in range(CHUNKS):
        arrival(c).start()
    for c in range(CHUNKS):
        arrival(c).wait()
        for h in range(c * CHUNK, (c + 1) * CHUNK):
            for n in range(len(row_refs)):
                if n in turned:
                    block = slab[h, n * BLOCK : (n + 1) * BLOCK, :]
                    rows[:, h * HEAD_DIM : (h + 1) * HEAD_DIM] = block.T
                leaving(h, n).start()
    for h in range(HEADS):
        for n in range(len(row_refs)):
            leaving(h, n).wait()


def unpack_rows(slab, count, turned, name):
    return pl.pallas_call(
        functools.partial(unpack_kernel, turned),
        in_specs=[HBM_SPEC],
        out_specs=[HBM_SPEC] * count,
        out_shape=[shape((1, BLOCK, HEADS * HEAD_DIM), BF16)] * count,
        scratch_shapes=[
            pltpu.VMEM((HEADS, count * BLOCK, 128), BF16),
            pltpu.VMEM((BLOCK, HEADS * HEAD_DIM), BF16),
            pltpu.SemaphoreType.DMA((CHUNKS,)),
            pltpu.SemaphoreType.DMA((count, HEADS)),
        ],
        compiler_params=pltpu.CompilerParams(vmem_limit_bytes=VMEM_LIMIT),
        name=name,
    )(slab)


def dot(a, b, contract=((1,), (0,))):
    return lax.dot_general(a, b, (contract, ((), ())), preferred_element_type=F32)


def tile_turned(ref, block, part):
    lines = slice(part * BLOCK, (part + 1) * BLOCK)
    return jnp.concatenate([ref[block + b, lines, :] for b in range(PAIR)], 1)


def tile_at(i, size=TILE):
    return pl.ds(pl.multiple_of(i * size, size), size)


def mean_down(values):
    return jnp.sum(values, 0, keepdims=True) * (1.0 / HEAD_DIM)


def block_row(b):
    return b // PAIR, slice((b % PAIR) * BLOCK, (b % PAIR + 1) * BLOCK)


def group_sums(group, values):
    lane = lax.broadcasted_iota(I32, (1, 128), 1)
    sums = jnp.zeros((1, 128), F32)
    for g in range(GROUPS):
        part = jnp.sum(jnp.where(group == float(g), values, 0.0), 0, keepdims=True)
        sums = jnp.where(lane == g, jnp.sum(part, 1, keepdims=True), sums)
    return sums


def key_mask(span_rows_ref, i, start, step):
    first = span_rows_ref[i, 0:1, :] - start
    count = span_rows_ref[i, 1:2, :]
    row = lax.broadcasted_iota(I32, (step, TILE), 0)
    return (row - first).astype(jnp.uint32) < count.astype(jnp.uint32)


def masked(scores, span_rows_ref, i, mask_at):
    return jnp.where(key_mask(span_rows_ref, i, mask_at, KEYS), scores, NEG)


def pair_steps(total):
    return (total + UNROLL - 1) // UNROLL


def each_pairs(total, pair_ref, body):
    def some(n, carry):
        pairs = []
        for u in range(UNROLL):
            p = n * UNROLL + u
            at = pl.multiple_of(pair_ref[1, p], BLOCK)
            pairs.append((p, pair_ref[0, p], at, pair_ref[2, p]))
        body(n, pairs)
        return carry

    lax.fori_loop(0, pair_steps(total), some, 0)


def softmax_tile(scores, span_rows_ref, norm_ref, i, mask_at):
    scores = masked(scores, span_rows_ref, i, mask_at)
    return jnp.exp2(scores * EXP_SCALE - norm_ref[i, 0:1, :]) * norm_ref[i, 1:2, :]


def find_pairs(seg_all, starts, pair_ref, span_rows_ref):
    for s in range(IMAGES + 1):
        starts[s] = jnp.sum((seg_all < float(s)).astype(F32)).astype(I32)
    first = jnp.zeros((BLOCKS, 128), I32)
    count = jnp.zeros((BLOCKS, 128), I32)
    for s in range(IMAGES):
        here = seg_all == float(s)
        first = jnp.where(here, starts[s], first)
        count = jnp.where(here, starts[s + 1] - starts[s], count)
    for b in range(BLOCKS):
        tile, at = block_row(b)
        span_rows_ref[tile, 0:1, at] = first[b : b + 1, :]
        span_rows_ref[tile, 1:2, at] = count[b : b + 1, :]

    def span(i, total):
        low, high = jnp.int32(0), jnp.int32(LENGTH)
        for s in range(1, IMAGES):
            low = jnp.where(starts[s] <= i * TILE, starts[s], low)
        for s in range(IMAGES - 1, 0, -1):
            high = jnp.where(starts[s] > i * TILE + TILE - 1, starts[s], high)
        low = (low // BLOCK) * BLOCK
        steps = (high - low + KEYS - 1) // KEYS
        low = jnp.minimum(low, LENGTH - steps * KEYS)

        def add(j, carry):
            pair_ref[0, total + j] = i
            pair_ref[1, total + j] = low + j * KEYS
            pair_ref[2, total + j] = low + j * KEYS
            return carry

        lax.fori_loop(0, steps, add, 0)
        return total + steps

    total = lax.fori_loop(0, TILES, span, jnp.int32(0))
    for u in range(UNROLL):
        pair_ref[0, total + u] = 0
        pair_ref[1, total + u] = 0
        pair_ref[2, total + u] = -(1 << 20)
    return total


def each_tile(what):
    def one(i, carry):
        what(i)
        return carry

    lax.fori_loop(0, TILES, one, 0)


def tile_blocks(i):
    return pl.ds(i * PAIR, PAIR)


def attend_kernel(
    all_ref, gains_ref,
    pair_ref, total_ref, span_rows_ref, *refs,
):
    hat_outs, probs_out, refs = refs[:2], refs[2], refs[3:]
    (moments_ref, norm_ref, out_ref), refs = refs[:3], refs[3:]
    (q_turned_ref, k_hat_ref), refs = refs[:2], refs[2:]
    recv_ref, extra_ref, starts, terms, fold, probs, sums = refs[:7]
    in_sems, extra_sem, out_sems, prob_sems = refs[7:]

    def arrival(i):
        return pltpu.make_async_copy(
            all_ref.at[tile_blocks(i), pl.ds(0, 3 * BLOCK), :],
            recv_ref.at[tile_blocks(i)],
            in_sems.at[i],
        )

    def leaving(i, n):
        rows = tile_at(i)
        source, target = (
            (q_turned_ref.at[pl.ds(0, HEAD_DIM), rows], hat_outs[0].at[:, rows]),
            (k_hat_ref.at[rows, pl.ds(0, HEAD_DIM)], hat_outs[1].at[rows, :]),
            (sums.at[i], out_ref.at[i]),
        )[n]
        return pltpu.make_async_copy(source, target, out_sems.at[n, i])

    extra = pltpu.make_async_copy(
        all_ref.at[:, pl.ds(3 * BLOCK, EXTRA), :], extra_ref, extra_sem.at[0]
    )
    extra.start()
    each_tile(lambda i: arrival(i).start())
    extra.wait()
    total = find_pairs(extra_ref[:, 0, :].astype(F32), starts, pair_ref, span_rows_ref)
    total_ref[0] = total
    gains = jnp.concatenate([gains_ref[...], jnp.zeros((6, HEAD_DIM), F32)], 0).T

    lane = lax.broadcasted_iota(I32, (1, HEAD_DIM), 1)
    seg_from = jnp.full((1, HEAD_DIM), LENGTH, I32)
    seg_to = jnp.full((1, HEAD_DIM), LENGTH, I32)
    for s in range(IMAGES):
        seg_from = jnp.where(lane == s, starts[s], seg_from)
        seg_to = jnp.where(lane == s, starts[s + 1], seg_to)
    k_hat_ref[LENGTH:, :HEAD_DIM] = jnp.zeros((KEYS, HEAD_DIM), BF16)
    nobody = jnp.where(lane == IMAGES, 1.0, 0.0)
    k_hat_ref[LENGTH:, HEAD_DIM:] = jnp.broadcast_to(nobody, (KEYS, HEAD_DIM)).astype(BF16)

    def prepare(i, most):
        arrival(i).wait()
        rows = tile_at(i)
        sizes = []
        for n in range(2):
            values = tile_turned(recv_ref, i * PAIR, n).astype(F32)
            mean = mean_down(values)
            centre = values - mean
            inverse = lax.rsqrt(mean_down(centre * centre) + EPS)
            moments_ref[i, 2 * n : 2 * n + 1, :] = mean
            moments_ref[i, 2 * n + 1 : 2 * n + 2, :] = inverse
            hat = centre * inverse * gains[:, n : n + 1]
            sizes.append(jnp.maximum(most[n], mean_down(hat * hat)))
            if n == 0:
                q_turned_ref[:HEAD_DIM, rows] = hat.astype(BF16)
            else:
                k_hat_ref[rows, :HEAD_DIM] = hat.astype(BF16).T
        seg_q = [extra_ref[i * PAIR + b, 0:1, :].astype(F32) for b in range(PAIR)]
        own = jnp.concatenate(seg_q, 1).astype(I32)
        segment = lax.broadcasted_iota(I32, (HEAD_DIM, TILE), 0)
        q_turned_ref[HEAD_DIM:, rows] = jnp.where(segment == own, 0.0, NEG).astype(BF16)
        row = lax.broadcasted_iota(I32, (TILE, HEAD_DIM), 0) + i * TILE
        inside = (row >= seg_from) & (row < seg_to)
        k_hat_ref[rows, HEAD_DIM:] = jnp.where(inside, 1.0, 0.0).astype(BF16)
        for n in range(2):
            leaving(i, n).start()
        sums[i] = jnp.zeros((HEAD_DIM, TILE), F32)
        norm_ref[i] = jnp.zeros((2, TILE), F32)
        fold[i] = jnp.zeros((8, TILE), F32)
        return tuple(sizes)

    zero = jnp.zeros((1, TILE), F32)
    most_q, most_k = lax.fori_loop(0, TILES, prepare, (zero, zero), unroll=TILES)
    bound = jnp.max(most_q) * jnp.max(most_k) * HEAD_DIM

    def scores_of(pairs):
        tiles = []
        for _, i, at, mask_at in pairs:
            at = pl.multiple_of(jnp.where(mask_at < 0, LENGTH, at), BLOCK)
            tiles.append(dot(k_hat_ref[pl.ds(at, KEYS), :], q_turned_ref[:, tile_at(i)]))
        return tiles

    @pl.when(jnp.logical_not(bound <= SAFE_LOGIT * SAFE_LOGIT))
    def _():
        def clear(i, carry):
            fold[i] = jnp.full((8, TILE), NEG, F32)
            return carry

        lax.fori_loop(0, TILES, clear, 0)

        def top_pairs(n, pairs):
            for tile, (_, i, _, _) in zip(scores_of(pairs), pairs):
                top = jnp.max(tile.reshape(KEYS // 8, 8, TILE), 0)
                fold[i] = jnp.maximum(fold[i], top)

        each_pairs(total, pair_ref, top_pairs)

        def finish(i, carry):
            norm_ref[i, 0:1, :] = jnp.max(fold[i], 0, keepdims=True) * EXP_SCALE
            fold[i] = jnp.zeros((8, TILE), F32)
            return carry

        lax.fori_loop(0, TILES, finish, 0)

    def exp_pairs(n, pairs):
        sums = []
        for tile, (p, i, _, _) in zip(scores_of(pairs), pairs):
            tile = jnp.exp2(tile * EXP_SCALE - norm_ref[i, 0:1, :])
            terms[p] = tile
            sums.append(jnp.sum(tile.reshape(KEYS // 8, 8, TILE), 0))
        for part, (_, i, _, _) in zip(sums, pairs):
            fold[i] += part

    each_pairs(total, pair_ref, exp_pairs)

    def invert(i, carry):
        norm_ref[i, 1:2, :] = 1.0 / jnp.sum(fold[i], 0, keepdims=True)
        return carry

    lax.fori_loop(0, TILES, invert, 0)

    def give_probs(n):
        slot = lax.rem(n, RING)
        return pltpu.make_async_copy(probs.at[slot], probs_out.at[n], prob_sems.at[slot])

    def out_pairs(n, pairs):
        slot = lax.rem(n, RING)

        @pl.when(n >= RING)
        def _():
            give_probs(n - RING).wait()

        tiles = [(terms[p] * norm_ref[i, 1:2, :]).astype(BF16) for p, i, _, _ in pairs]
        for u, tile in enumerate(tiles):
            probs[slot, u] = tile
        give_probs(n).start()
        tiles = [
            dot(tile_turned(recv_ref, at // BLOCK, 2), tile)
            for tile, (_, _, at, _) in zip(tiles, pairs)
        ]
        for tile, (_, i, _, _) in zip(tiles, pairs):
            sums[i] += tile

    each_pairs(total, pair_ref, out_pairs)
    each_tile(lambda i: leaving(i, 2).start())
    steps = pair_steps(total)

    def end(n, carry):
        give_probs(n).wait()
        return carry

    lax.fori_loop(jnp.maximum(steps - RING, 0), steps, end, 0)
    for n in range(3):
        each_tile(lambda i, n=n: leaving(i, n).wait())


def run_attend(received, gains):
    hats = [((HEAD_DIM, LENGTH), BF16), ((LENGTH, HEAD_DIM), BF16)]
    return pl.pallas_call(
        attend_kernel,
        in_specs=[HBM_SPEC, VMEM_SPEC],
        out_specs=[SMEM_SPEC] * 2 + [VMEM_SPEC] + [HBM_SPEC] * 3 + [VMEM_SPEC] * 2 + [HBM_SPEC],
        out_shape=[
            shape((3, MOST_PAIRS + UNROLL), I32),
            shape((1,), I32),
            shape((TILES, 2, TILE), I32),
            *[shape(*hat) for hat in hats],
            shape((MOST_STEPS, UNROLL, KEYS, TILE), BF16),
            shape((TILES, 4, TILE), F32),
            shape((TILES, 2, TILE), F32),
            shape((TILES, HEAD_DIM, TILE), F32),
        ],
        scratch_shapes=[
            pltpu.VMEM((2 * HEAD_DIM, LENGTH), BF16),
            pltpu.VMEM((LENGTH + KEYS, 2 * HEAD_DIM), BF16),
            pltpu.VMEM((BLOCKS, 3 * BLOCK, 128), BF16),
            pltpu.VMEM((BLOCKS, EXTRA, 128), BF16),
            pltpu.SMEM((IMAGES + 1,), I32),
            pltpu.VMEM((MOST_PAIRS, KEYS, TILE), F32),
            pltpu.VMEM((TILES, 8, TILE), F32),
            pltpu.VMEM((RING, UNROLL, KEYS, TILE), BF16),
            pltpu.VMEM((TILES, HEAD_DIM, TILE), F32),
            pltpu.SemaphoreType.DMA((TILES,)),
            pltpu.SemaphoreType.DMA((1,)),
            pltpu.SemaphoreType.DMA((3, TILES)),
            pltpu.SemaphoreType.DMA((RING,)),
        ],
        compiler_params=pltpu.CompilerParams(vmem_limit_bytes=VMEM_LIMIT),
        cost_estimate=WORK,
        name="attend",
    )(received, gains)


def loss_kernel(
    labels_ref, mixture_ref, pair_ref, total_ref,
    all_ref, out_in, probs_in,
    send_out, grad_turned_out, inner_ref, counts_ref,
    coef_rows, loss_rows, grad_low, grad_v, probs, recv_ref, extra_ref, out_ref, first_ref, value_ref,
    grad_turned_ref, sems, in_sems, extra_sem, out_sems,
):
    def arrival(i, n):
        source, target = (
            (all_ref.at[tile_blocks(i), pl.ds(0, BLOCK), :], recv_ref.at[tile_blocks(i)]),
            (out_in.at[i], out_ref.at[i]),
        )[n]
        return pltpu.make_async_copy(source, target, in_sems.at[n, i])

    def leaving(i, n):
        rows = tile_at(i)
        blocks = tile_blocks(i)
        source, target = (
            (first_ref.at[blocks], send_out.at[blocks, pl.ds(0, BLOCK), :]),
            (grad_turned_ref.at[:, rows], grad_turned_out.at[:, rows]),
            (value_ref.at[blocks], send_out.at[blocks, pl.ds(BLOCK, BLOCK + EXTRA), :]),
        )[n]
        return pltpu.make_async_copy(source, target, out_sems.at[n, i])

    def take_probs(n):
        return pltpu.make_async_copy(probs_in.at[n], probs.at[n], sems.at[n])

    def start_probs(n, carry):
        take_probs(n).start()
        return carry

    extra = pltpu.make_async_copy(
        all_ref.at[:, pl.ds(BLOCK, EXTRA), :], extra_ref, extra_sem.at[0]
    )
    extra.start()
    for n in range(2):
        each_tile(lambda i, n=n: arrival(i, n).start())
    lax.fori_loop(0, pair_steps(total_ref[0]), start_probs, 0)

    extra.wait()
    seg_all = extra_ref[:, 0, :].astype(F32)
    group = jnp.zeros((BLOCKS, 128), F32)
    for s in range(IMAGES):
        group = jnp.where(seg_all == float(s), labels_ref[0, s].astype(F32), group)
    others = [extra_ref[:, 1 + p, :].astype(F32) for p in range(PACKS)]
    total_mix = mixture_ref[0]
    for g in range(1, GROUPS):
        total_mix = total_mix + mixture_ref[g]
    lane = lax.broadcasted_iota(I32, (1, 128), 1)
    coef = jnp.zeros((BLOCKS, 128), F32)
    count_row = jnp.zeros((1, 128), F32)
    for g in range(GROUPS):
        hits = sum((other == float(g)).astype(F32) for other in others)
        count = jnp.sum(jnp.sum(hits, 0, keepdims=True), 1, keepdims=True)
        share = jnp.full((1, 1), mixture_ref[g], F32) / total_mix
        coef = jnp.where(group == float(g), share / (count * (HEADS * HEAD_DIM)), coef)
        count_row = jnp.where(lane == g, count, count_row)
    counts_ref[...] = count_row
    for b in range(BLOCKS):
        tile, at = block_row(b)
        coef_rows[tile, 0:1, at] = coef[b : b + 1, :]

    def finish(i, carry):
        for n in range(2):
            arrival(i, n).wait()
        rows = tile_at(i)
        head_out = out_ref[i]
        misfit = head_out - tile_turned(recv_ref, i * PAIR, 0).astype(F32)
        loss_rows[i, 0:1, :] = 0.5 * jnp.sum(misfit * misfit, 0, keepdims=True)
        grad_out = coef_rows[i, 0:1, :] * misfit
        inner_ref[i, 0:1, :] = jnp.sum(grad_out * head_out, 0, keepdims=True)
        grad_turned = grad_out.astype(BF16)
        grad_turned_ref[:, rows] = grad_turned
        grad_low[rows, :] = grad_turned.T
        grad_v[rows, :] = jnp.zeros((TILE, HEAD_DIM), F32)
        low = head_out.astype(BF16)
        for b in range(PAIR):
            first_ref[i * PAIR + b] = low[:, b * BLOCK : (b + 1) * BLOCK]
        for n in range(2):
            leaving(i, n).start()
        return carry

    lax.fori_loop(0, TILES, finish, 0, unroll=TILES)

    rows = [block_row(b) for b in range(BLOCKS)]
    losses = jnp.concatenate([loss_rows[tile, 0:1, at] for tile, at in rows], 0)
    loss_row = group_sums(group, losses)
    high = loss_row.astype(BF16)
    left = loss_row - high.astype(F32)
    middle = left.astype(BF16)
    low = (left - middle.astype(F32)).astype(BF16)
    row = lax.broadcasted_iota(I32, (EXTRA, 128), 0)
    pieces = jnp.zeros((EXTRA, 128), F32)
    for n, piece in enumerate((high, middle, low)):
        pieces = jnp.where(row == n, piece.astype(F32), pieces)
    value_ref[:, BLOCK:, :] = jnp.broadcast_to(pieces.astype(BF16)[None], (BLOCKS, EXTRA, 128))

    def add_pairs(n, pairs):
        take_probs(n).wait()
        tiles = [dot(probs[n, u], grad_low[tile_at(pair[1]), :]) for u, pair in enumerate(pairs)]
        for tile, (_, _, at, _) in zip(tiles, pairs):
            grad_v[pl.ds(at, KEYS), :] += tile

    each_pairs(total_ref[0], pair_ref, add_pairs)

    def give(i, carry):
        value_ref[pl.ds(i * PAIR, PAIR), 0:BLOCK, :] = (
            grad_v[tile_at(i), :].astype(BF16).reshape(PAIR, BLOCK, HEAD_DIM)
        )
        leaving(i, 2).start()
        return carry

    lax.fori_loop(0, TILES, give, 0, unroll=TILES)
    for n in range(3):
        each_tile(lambda i, n=n: leaving(i, n).wait())


def run_loss(labels, mixture, pairs, total, second, head_out, probs):
    return pl.pallas_call(
        loss_kernel,
        in_specs=[SMEM_SPEC] * 4 + [HBM_SPEC] * 3,
        out_specs=[HBM_SPEC] * 2 + [VMEM_SPEC] * 2,
        out_shape=[
            shape((BLOCKS, 2 * BLOCK + EXTRA, 128), BF16),
            shape((HEAD_DIM, LENGTH), BF16),
            shape((TILES, 1, TILE), F32),
            shape((1, 128), F32),
        ],
        scratch_shapes=[
            pltpu.VMEM((TILES, 1, TILE), F32),
            pltpu.VMEM((TILES, 1, TILE), F32),
            pltpu.VMEM((LENGTH, HEAD_DIM), BF16),
            pltpu.VMEM((LENGTH, HEAD_DIM), F32),
            pltpu.VMEM((MOST_STEPS, UNROLL, KEYS, TILE), BF16),
            pltpu.VMEM((BLOCKS, BLOCK, 128), BF16),
            pltpu.VMEM((BLOCKS, EXTRA, 128), BF16),
            pltpu.VMEM((TILES, HEAD_DIM, TILE), F32),
            pltpu.VMEM((BLOCKS, BLOCK, 128), BF16),
            pltpu.VMEM((BLOCKS, BLOCK + EXTRA, 128), BF16),
            pltpu.VMEM((HEAD_DIM, LENGTH), BF16),
            pltpu.SemaphoreType.DMA((MOST_STEPS,)),
            pltpu.SemaphoreType.DMA((2, TILES)),
            pltpu.SemaphoreType.DMA((1,)),
            pltpu.SemaphoreType.DMA((3, TILES)),
        ],
        compiler_params=pltpu.CompilerParams(vmem_limit_bytes=VMEM_LIMIT),
        name="loss_and_grad_value",
    )(labels, mixture, pairs, total, second, head_out, probs)


def backward_kernel(
    pair_ref, total_ref,
    all_ref, q_turned_in, k_hat_in, grad_turned_in,
    gains_ref, moments_ref, span_rows_ref, norm_ref, inner_ref,
    send_out, gain_out_ref,
    grad_q, grad_k, q_hat_ref, k_turned_ref, value_ref, raw_ref, q_turned_ref, k_hat_ref,
    grad_turned_ref, send_ref, in_sems, out_sems,
):
    def arrival(i, n):
        rows = tile_at(i)
        blocks = tile_blocks(i)
        source, target = (
            (q_turned_in.at[:, rows], q_turned_ref.at[:, rows]),
            (k_hat_in.at[rows, :], k_hat_ref.at[rows, :]),
            (all_ref.at[blocks, pl.ds(0, 3 * BLOCK), :], raw_ref.at[blocks]),
            (grad_turned_in.at[:, rows], grad_turned_ref.at[:, rows]),
        )[n]
        return pltpu.make_async_copy(source, target, in_sems.at[n, i])

    def leaving(i):
        blocks = tile_blocks(i)
        return pltpu.make_async_copy(send_ref.at[blocks], send_out.at[blocks], out_sems.at[i])

    for n in range(4):
        each_tile(lambda i, n=n: arrival(i, n).start())

    def clear(i, carry):
        for n in range(2):
            arrival(i, n).wait()
        q_hat_ref[tile_at(i), :] = q_turned_ref[:, tile_at(i)].T
        k_turned_ref[:, tile_at(i)] = k_hat_ref[tile_at(i), :].T
        arrival(i, 2).wait()
        value_ref[tile_at(i), :] = tile_turned(raw_ref, i * PAIR, 2).T
        grad_q[i] = jnp.zeros((HEAD_DIM, TILE), F32)
        grad_k[tile_at(i), :] = jnp.zeros((TILE, HEAD_DIM), F32)
        return carry

    lax.fori_loop(0, TILES, clear, 0, unroll=TILES)
    each_tile(lambda i: arrival(i, 3).wait())

    def add_pairs(n, pairs):
        tiles = [
            dot(k_hat_ref[pl.ds(at, KEYS), :], q_turned_ref[:, tile_at(i)]) for _, i, at, _ in pairs
        ]
        prob_grads = [
            dot(value_ref[pl.ds(at, KEYS), :], grad_turned_ref[:, tile_at(i)])
            for _, i, at, _ in pairs
        ]
        tiles = [
            softmax_tile(tile, span_rows_ref, norm_ref, i, mask_at)
            for tile, (_, i, _, mask_at) in zip(tiles, pairs)
        ]
        tiles = [
            (tile * (prob - inner_ref[i, 0:1, :]) * SCALE).astype(BF16)
            for tile, prob, (_, i, _, _) in zip(tiles, prob_grads, pairs)
        ]
        keys = [dot(tile, q_hat_ref[tile_at(i), :]) for tile, (_, i, _, _) in zip(tiles, pairs)]
        queries = [
            dot(k_turned_ref[:, pl.ds(at, KEYS)], tile) for tile, (_, _, at, _) in zip(tiles, pairs)
        ]
        for key, query, (_, i, at, _) in zip(keys, queries, pairs):
            grad_k[pl.ds(at, KEYS), :] += key
            grad_q[i] += query

    each_pairs(total_ref[0], pair_ref, add_pairs)

    gains = jnp.concatenate([gains_ref[...], jnp.zeros((6, HEAD_DIM), F32)], 0).T

    def norm_backward(i, n, grad_hat):
        mean = moments_ref[i, 2 * n : 2 * n + 1, :]
        inverse = moments_ref[i, 2 * n + 1 : 2 * n + 2, :]
        normed = (tile_turned(raw_ref, i * PAIR, n).astype(F32) - mean) * inverse
        grad_normed = grad_hat * gains[:, n : n + 1]
        inner = mean_down(grad_normed * normed)
        grad_in = inverse * (grad_normed - mean_down(grad_normed) - normed * inner)
        send_ref[pl.ds(i * PAIR, PAIR), n * BLOCK : (n + 1) * BLOCK, :] = grad_in.astype(
            BF16
        ).T.reshape(PAIR, BLOCK, HEAD_DIM)
        grad_gain = grad_hat * normed
        return sum(grad_gain[:, c : c + 128] for c in range(0, TILE, 128))

    def finish(i, gain_sums):
        gain_q, gain_k = gain_sums
        gain_q = gain_q + norm_backward(i, 0, grad_q[i])
        gain_k = gain_k + norm_backward(i, 1, grad_k[tile_at(i), :].T)
        leaving(i).start()
        return gain_q, gain_k

    zero = jnp.zeros((HEAD_DIM, 128), F32)
    gain_q, gain_k = lax.fori_loop(0, TILES, finish, (zero, zero), unroll=TILES)
    gain_out_ref[0:1, :] = jnp.sum(gain_q.T, 0, keepdims=True)
    gain_out_ref[1:2, :] = jnp.sum(gain_k.T, 0, keepdims=True)
    each_tile(lambda i: leaving(i).wait())


def run_backward(pairs, total, received, q_turned, k_hat, grad_turned, *arrays):
    return pl.pallas_call(
        backward_kernel,
        in_specs=[SMEM_SPEC] * 2 + [HBM_SPEC] * 4 + [VMEM_SPEC] * len(arrays),
        out_specs=[HBM_SPEC, VMEM_SPEC],
        out_shape=[shape((BLOCKS, 2 * BLOCK, 128), BF16), shape((2, HEAD_DIM), F32)],
        scratch_shapes=[
            pltpu.VMEM((TILES, HEAD_DIM, TILE), F32),
            pltpu.VMEM((LENGTH, HEAD_DIM), F32),
            pltpu.VMEM((LENGTH, HEAD_DIM), BF16),
            pltpu.VMEM((HEAD_DIM, LENGTH), BF16),
            pltpu.VMEM((LENGTH, HEAD_DIM), BF16),
            pltpu.VMEM((BLOCKS, 3 * BLOCK, 128), BF16),
            pltpu.VMEM((HEAD_DIM, LENGTH), BF16),
            pltpu.VMEM((LENGTH, HEAD_DIM), BF16),
            pltpu.VMEM((HEAD_DIM, LENGTH), BF16),
            pltpu.VMEM((BLOCKS, 2 * BLOCK, 128), BF16),
            pltpu.SemaphoreType.DMA((4, TILES)),
            pltpu.SemaphoreType.DMA((TILES,)),
        ],
        compiler_params=pltpu.CompilerParams(vmem_limit_bytes=VMEM_LIMIT),
        cost_estimate=WORK,
        name="backward",
    )(pairs, total, received, q_turned, k_hat, grad_turned, *arrays)


def over_packs(value):
    moved = [value]
    for shift in range(1, PACKS):
        pairs = [(i, (i + shift) % PACKS) for i in range(PACKS)]
        moved.append(lax.ppermute(value, "pack", pairs))
    return moved


def exchange(slab):
    return lax.all_to_all(slab, "seq", split_axis=0, concat_axis=0, tiled=True)


def on_device(
    query_rows, key_rows, value_rows, target_rows, norm_gains, segment_ids, group_labels, mixture
):
    gains = norm_gains.reshape(2, HEAD_DIM)
    first = exchange(pack_rows((query_rows, key_rows, value_rows), segment_ids, "pack_first"))

    image_hot = segment_ids[0][:, None] == jnp.arange(IMAGES, dtype=I32)[None, :]
    labels = jnp.sum(jnp.where(image_hot, group_labels[0][None, :], 0), 1)[None, :]
    extra = jnp.concatenate([segment_ids.astype(F32), *over_packs(labels.astype(F32))], 0)
    second = exchange(pack_rows((target_rows,), extra, "pack_second"))

    pairs, total, span_rows, *hats, probs, moments, norms, head_out = run_attend(first, gains)
    send, grad_turned, inner, counts = run_loss(
        group_labels, mixture, pairs, total, second, head_out, probs
    )
    back = exchange(send)
    send, gain_part = run_backward(
        pairs, total, first, *hats, grad_turned, gains, moments, span_rows, norms, inner
    )
    back, send = lax.optimization_barrier((back, send))
    last = exchange(send)
    attended, grad_value = unpack_rows(back, 2, (0,), "unpack_first")
    losses = jnp.sum(back[:, 2 * BLOCK : 2 * BLOCK + 3, :GROUPS].astype(F32), (0, 1))
    group_total = sum(over_packs(losses))
    group_loss = group_total / (counts[0, :GROUPS] * (HEADS * HEAD_DIM))
    shares = mixture / jnp.sum(mixture)
    raised = shares * jnp.exp(ETA * group_loss)
    new_mixture = raised / jnp.sum(raised)
    grad_gains = sum(over_packs(gain_part)).reshape(2, 1, HEAD_DIM)
    grad_query, grad_key = unpack_rows(last, 2, (), "unpack_last")
    return (attended, grad_query, grad_key, grad_value, grad_gains, new_mixture)


def solution(mesh):
    rows = P("pack", "seq", None)
    gains = P(None, "seq", None)
    return jax.shard_map(
        on_device,
        mesh=mesh,
        in_specs=(rows, rows, rows, rows, gains, P("pack", "seq"), P("pack", None), P()),
        out_specs=(rows, rows, rows, rows, gains, P()),
        check_vma=False,
    )
```

```python
import functools

import jax
import jax.numpy as jnp
from jax import lax
from jax.experimental import pallas as pl
from jax.experimental.pallas import tpu as pltpu
from jax.sharding import PartitionSpec as P

HEADS = 32
HEAD_DIM = 128
IMAGES = 16
GROUPS = 8
PACKS = 4
LENGTH = 4096

NEG = -1e30
EPS = 1e-06
ETA = 2.0
SCALE = HEAD_DIM ** (-0.5)
EXP_SCALE = SCALE * 1.4426950408889634

BLOCK = 128
BLOCKS = LENGTH // BLOCK
TILE = 256
TILES = LENGTH // TILE
PAIR = TILE // BLOCK
KEYS = 256
UNROLL = 8
MOST_PAIRS = (LENGTH * (1024 // TILE + 1) + TILES * (BLOCK - 1 + KEYS - 1)) // KEYS
MOST_STEPS = MOST_PAIRS // UNROLL + 1
MOST_PAIRS = MOST_STEPS * UNROLL
RING = 4
SAFE_LOGIT = 70.0
EXTRA = 16
CHUNK = 8
CHUNKS = HEADS // CHUNK
VMEM_LIMIT = 63 * 1024 * 1024

BF16 = jnp.bfloat16
F32 = jnp.float32
I32 = jnp.int32

WORK = pl.CostEstimate(flops=1 << 33, bytes_accessed=1 << 25, transcendentals=1 << 22)

VMEM_SPEC = pl.BlockSpec(memory_space=pltpu.VMEM)
SMEM_SPEC = pl.BlockSpec(memory_space=pltpu.SMEM)
HBM_SPEC = pl.BlockSpec(memory_space=pltpu.HBM)


def shape(dims, dtype):
    return jax.ShapeDtypeStruct(dims, dtype)


def head_columns(h):
    return pl.ds(h * HEAD_DIM, HEAD_DIM)


def pack_kernel(count, *refs):
    row_refs, (extra_ref, out_ref, rows, slab, in_sems, out_sems) = refs[:count], refs[count:]

    def arrival(c, n):
        columns = pl.ds(c * CHUNK * HEAD_DIM, CHUNK * HEAD_DIM)
        return pltpu.make_async_copy(
            row_refs[n].at[0, :, columns], rows.at[n, :, columns], in_sems.at[n, c]
        )

    def leaving(c):
        heads = pl.ds(c * CHUNK, CHUNK)
        return pltpu.make_async_copy(slab.at[heads], out_ref.at[heads], out_sems.at[c])

    for c in range(CHUNKS):
        for n in range(count):
            arrival(c, n).start()
    extra = extra_ref[...].astype(F32)
    extra = jnp.concatenate([extra, jnp.zeros((EXTRA - extra.shape[0], 128), F32)], 0)
    slab[:, count * BLOCK :, :] = jnp.broadcast_to(extra.astype(BF16)[None], (HEADS, EXTRA, 128))
    for c in range(CHUNKS):
        for n in range(count):
            arrival(c, n).wait()
            for h in range(c * CHUNK, (c + 1) * CHUNK):
                block = rows[n, :, h * HEAD_DIM : (h + 1) * HEAD_DIM]
                slab[h, n * BLOCK : (n + 1) * BLOCK, :] = block.T
        leaving(c).start()
    for c in range(CHUNKS):
        leaving(c).wait()


def pack_rows(rows, extra, name):
    count = len(rows)
    slab = (HEADS, count * BLOCK + EXTRA, 128)
    return pl.pallas_call(
        functools.partial(pack_kernel, count),
        in_specs=[HBM_SPEC] * count + [VMEM_SPEC],
        out_specs=HBM_SPEC,
        out_shape=shape(slab, BF16),
        scratch_shapes=[
            pltpu.VMEM((count, BLOCK, HEADS * HEAD_DIM), BF16),
            pltpu.VMEM(slab, BF16),
            pltpu.SemaphoreType.DMA((count, CHUNKS)),
            pltpu.SemaphoreType.DMA((CHUNKS,)),
        ],
        compiler_params=pltpu.CompilerParams(vmem_limit_bytes=VMEM_LIMIT),
        name=name,
    )(*rows, extra)


def unpack_kernel(turned, in_ref, *refs):
    *row_refs, slab, rows, in_sems, out_sems = refs
    lines = len(row_refs) * BLOCK

    def arrival(c):
        heads = pl.ds(c * CHUNK, CHUNK)
        return pltpu.make_async_copy(
            in_ref.at[heads, pl.ds(0, lines), :], slab.at[heads], in_sems.at[c]
        )

    def leaving(h, n):
        columns = head_columns(h)
        source = slab.at[h, pl.ds(n * BLOCK, BLOCK), :]
        if n in turned:
            source = rows.at[:, columns]
        return pltpu.make_async_copy(source, row_refs[n].at[0, :, columns], out_sems.at[n, h])

    for c in range(CHUNKS):
        arrival(c).start()
    for c in range(CHUNKS):
        arrival(c).wait()
        for h in range(c * CHUNK, (c + 1) * CHUNK):
            for n in range(len(row_refs)):
                if n in turned:
                    block = slab[h, n * BLOCK : (n + 1) * BLOCK, :]
                    rows[:, h * HEAD_DIM : (h + 1) * HEAD_DIM] = block.T
                leaving(h, n).start()
    for h in range(HEADS):
        for n in range(len(row_refs)):
            leaving(h, n).wait()


def unpack_rows(slab, count, turned, name):
    return pl.pallas_call(
        functools.partial(unpack_kernel, turned),
        in_specs=[HBM_SPEC],
        out_specs=[HBM_SPEC] * count,
        out_shape=[shape((1, BLOCK, HEADS * HEAD_DIM), BF16)] * count,
        scratch_shapes=[
            pltpu.VMEM((HEADS, count * BLOCK, 128), BF16),
            pltpu.VMEM((BLOCK, HEADS * HEAD_DIM), BF16),
            pltpu.SemaphoreType.DMA((CHUNKS,)),
            pltpu.SemaphoreType.DMA((count, HEADS)),
        ],
        compiler_params=pltpu.CompilerParams(vmem_limit_bytes=VMEM_LIMIT),
        name=name,
    )(slab)


def dot(a, b, contract=((1,), (0,))):
    return lax.dot_general(a, b, (contract, ((), ())), preferred_element_type=F32)


def tile_turned(ref, block, part):
    lines = slice(part * BLOCK, (part + 1) * BLOCK)
    return jnp.concatenate([ref[block + b, lines, :] for b in range(PAIR)], 1)


def tile_at(i, size=TILE):
    return pl.ds(pl.multiple_of(i * size, size), size)


def mean_down(values):
    return jnp.sum(values, 0, keepdims=True) * (1.0 / HEAD_DIM)


def block_row(b):
    return b // PAIR, slice((b % PAIR) * BLOCK, (b % PAIR + 1) * BLOCK)


def group_sums(group, values):
    lane = lax.broadcasted_iota(I32, (1, 128), 1)
    sums = jnp.zeros((1, 128), F32)
    for g in range(GROUPS):
        part = jnp.sum(jnp.where(group == float(g), values, 0.0), 0, keepdims=True)
        sums = jnp.where(lane == g, jnp.sum(part, 1, keepdims=True), sums)
    return sums


def key_mask(span_rows_ref, i, start, step):
    first = span_rows_ref[i, 0:1, :] - start
    count = span_rows_ref[i, 1:2, :]
    row = lax.broadcasted_iota(I32, (step, TILE), 0)
    return (row - first).astype(jnp.uint32) < count.astype(jnp.uint32)


def masked(scores, span_rows_ref, i, mask_at):
    return jnp.where(key_mask(span_rows_ref, i, mask_at, KEYS), scores, NEG)


def pair_steps(total):
    return (total + UNROLL - 1) // UNROLL


def each_pairs(total, pair_ref, body):
    def some(n, carry):
        pairs = []
        for u in range(UNROLL):
            p = n * UNROLL + u
            at = pl.multiple_of(pair_ref[1, p], BLOCK)
            pairs.append((p, pair_ref[0, p], at, pair_ref[2, p]))
        body(n, pairs)
        return carry

    lax.fori_loop(0, pair_steps(total), some, 0)


def softmax_tile(scores, span_rows_ref, norm_ref, i, mask_at):
    scores = masked(scores, span_rows_ref, i, mask_at)
    return jnp.exp2(scores * EXP_SCALE - norm_ref[i, 0:1, :]) * norm_ref[i, 1:2, :]


def find_pairs(seg_all, starts, pair_ref, span_rows_ref):
    for s in range(IMAGES + 1):
        starts[s] = jnp.sum((seg_all < float(s)).astype(F32)).astype(I32)
    first = jnp.zeros((BLOCKS, 128), I32)
    count = jnp.zeros((BLOCKS, 128), I32)
    for s in range(IMAGES):
        here = seg_all == float(s)
        first = jnp.where(here, starts[s], first)
        count = jnp.where(here, starts[s + 1] - starts[s], count)
    for b in range(BLOCKS):
        tile, at = block_row(b)
        span_rows_ref[tile, 0:1, at] = first[b : b + 1, :]
        span_rows_ref[tile, 1:2, at] = count[b : b + 1, :]

    def span(i, total):
        low, high = jnp.int32(0), jnp.int32(LENGTH)
        for s in range(1, IMAGES):
            low = jnp.where(starts[s] <= i * TILE, starts[s], low)
        for s in range(IMAGES - 1, 0, -1):
            high = jnp.where(starts[s] > i * TILE + TILE - 1, starts[s], high)
        low = (low // BLOCK) * BLOCK
        steps = (high - low + KEYS - 1) // KEYS
        low = jnp.minimum(low, LENGTH - steps * KEYS)

        def add(j, carry):
            pair_ref[0, total + j] = i
            pair_ref[1, total + j] = low + j * KEYS
            pair_ref[2, total + j] = low + j * KEYS
            return carry

        lax.fori_loop(0, steps, add, 0)
        return total + steps

    total = lax.fori_loop(0, TILES, span, jnp.int32(0))
    for u in range(UNROLL):
        pair_ref[0, total + u] = 0
        pair_ref[1, total + u] = 0
        pair_ref[2, total + u] = -(1 << 20)
    return total


def each_tile(what):
    def one(i, carry):
        what(i)
        return carry

    lax.fori_loop(0, TILES, one, 0)


def tile_blocks(i):
    return pl.ds(i * PAIR, PAIR)


def attend_kernel(
    all_ref, gains_ref,
    pair_ref, total_ref, span_rows_ref, *refs,
):
    hat_outs, probs_out, refs = refs[:2], refs[2], refs[3:]
    (moments_ref, norm_ref, out_ref), refs = refs[:3], refs[3:]
    (q_turned_ref, k_hat_ref), refs = refs[:2], refs[2:]
    recv_ref, extra_ref, starts, terms, fold, probs, sums = refs[:7]
    in_sems, extra_sem, out_sems, prob_sems = refs[7:]

    def arrival(i):
        return pltpu.make_async_copy(
            all_ref.at[tile_blocks(i), pl.ds(0, 3 * BLOCK), :],
            recv_ref.at[tile_blocks(i)],
            in_sems.at[i],
        )

    def leaving(i, n):
        rows = tile_at(i)
        source, target = (
            (q_turned_ref.at[pl.ds(0, HEAD_DIM), rows], hat_outs[0].at[:, rows]),
            (k_hat_ref.at[rows, pl.ds(0, HEAD_DIM)], hat_outs[1].at[rows, :]),
            (sums.at[i], out_ref.at[i]),
        )[n]
        return pltpu.make_async_copy(source, target, out_sems.at[n, i])

    extra = pltpu.make_async_copy(
        all_ref.at[:, pl.ds(3 * BLOCK, EXTRA), :], extra_ref, extra_sem.at[0]
    )
    extra.start()
    each_tile(lambda i: arrival(i).start())
    extra.wait()
    total = find_pairs(extra_ref[:, 0, :].astype(F32), starts, pair_ref, span_rows_ref)
    total_ref[0] = total
    gains = jnp.concatenate([gains_ref[...], jnp.zeros((6, HEAD_DIM), F32)], 0).T

    lane = lax.broadcasted_iota(I32, (1, HEAD_DIM), 1)
    seg_from = jnp.full((1, HEAD_DIM), LENGTH, I32)
    seg_to = jnp.full((1, HEAD_DIM), LENGTH, I32)
    for s in range(IMAGES):
        seg_from = jnp.where(lane == s, starts[s], seg_from)
        seg_to = jnp.where(lane == s, starts[s + 1], seg_to)
    k_hat_ref[LENGTH:, :HEAD_DIM] = jnp.zeros((KEYS, HEAD_DIM), BF16)
    nobody = jnp.where(lane == IMAGES, 1.0, 0.0)
    k_hat_ref[LENGTH:, HEAD_DIM:] = jnp.broadcast_to(nobody, (KEYS, HEAD_DIM)).astype(BF16)

    def prepare(i, most):
        arrival(i).wait()
        rows = tile_at(i)
        sizes = []
        for n in range(2):
            values = tile_turned(recv_ref, i * PAIR, n).astype(F32)
            mean = mean_down(values)
            centre = values - mean
            inverse = lax.rsqrt(mean_down(centre * centre) + EPS)
            moments_ref[i, 2 * n : 2 * n + 1, :] = mean
            moments_ref[i, 2 * n + 1 : 2 * n + 2, :] = inverse
            hat = centre * inverse * gains[:, n : n + 1]
            sizes.append(jnp.maximum(most[n], mean_down(hat * hat)))
            if n == 0:
                q_turned_ref[:HEAD_DIM, rows] = hat.astype(BF16)
            else:
                k_hat_ref[rows, :HEAD_DIM] = hat.astype(BF16).T
        seg_q = [extra_ref[i * PAIR + b, 0:1, :].astype(F32) for b in range(PAIR)]
        own = jnp.concatenate(seg_q, 1).astype(I32)
        segment = lax.broadcasted_iota(I32, (HEAD_DIM, TILE), 0)
        q_turned_ref[HEAD_DIM:, rows] = jnp.where(segment == own, 0.0, NEG).astype(BF16)
        row = lax.broadcasted_iota(I32, (TILE, HEAD_DIM), 0) + i * TILE
        inside = (row >= seg_from) & (row < seg_to)
        k_hat_ref[rows, HEAD_DIM:] = jnp.where(inside, 1.0, 0.0).astype(BF16)
        for n in range(2):
            leaving(i, n).start()
        sums[i] = jnp.zeros((HEAD_DIM, TILE), F32)
        norm_ref[i] = jnp.zeros((2, TILE), F32)
        fold[i] = jnp.zeros((8, TILE), F32)
        return tuple(sizes)

    zero = jnp.zeros((1, TILE), F32)
    most_q, most_k = lax.fori_loop(0, TILES, prepare, (zero, zero), unroll=TILES)
    bound = jnp.max(most_q) * jnp.max(most_k) * HEAD_DIM

    def scores_of(pairs):
        tiles = []
        for _, i, at, mask_at in pairs:
            at = pl.multiple_of(jnp.where(mask_at < 0, LENGTH, at), BLOCK)
            tiles.append(dot(k_hat_ref[pl.ds(at, KEYS), :], q_turned_ref[:, tile_at(i)]))
        return tiles

    @pl.when(jnp.logical_not(bound <= SAFE_LOGIT * SAFE_LOGIT))
    def _():
        def clear(i, carry):
            fold[i] = jnp.full((8, TILE), NEG, F32)
            return carry

        lax.fori_loop(0, TILES, clear, 0)

        def top_pairs(n, pairs):
            for tile, (_, i, _, _) in zip(scores_of(pairs), pairs):
                top = jnp.max(tile.reshape(KEYS // 8, 8, TILE), 0)
                fold[i] = jnp.maximum(fold[i], top)

        each_pairs(total, pair_ref, top_pairs)

        def finish(i, carry):
            norm_ref[i, 0:1, :] = jnp.max(fold[i], 0, keepdims=True) * EXP_SCALE
            fold[i] = jnp.zeros((8, TILE), F32)
            return carry

        lax.fori_loop(0, TILES, finish, 0)

    def exp_pairs(n, pairs):
        sums = []
        for tile, (p, i, _, _) in zip(scores_of(pairs), pairs):
            tile = jnp.exp2(tile * EXP_SCALE - norm_ref[i, 0:1, :])
            terms[p] = tile
            sums.append(jnp.sum(tile.reshape(KEYS // 8, 8, TILE), 0))
        for part, (_, i, _, _) in zip(sums, pairs):
            fold[i] += part

    each_pairs(total, pair_ref, exp_pairs)

    def invert(i, carry):
        norm_ref[i, 1:2, :] = 1.0 / jnp.sum(fold[i], 0, keepdims=True)
        return carry

    lax.fori_loop(0, TILES, invert, 0)

    def give_probs(n):
        slot = lax.rem(n, RING)
        return pltpu.make_async_copy(probs.at[slot], probs_out.at[n], prob_sems.at[slot])

    def out_pairs(n, pairs):
        slot = lax.rem(n, RING)

        @pl.when(n >= RING)
        def _():
            give_probs(n - RING).wait()

        tiles = [(terms[p] * norm_ref[i, 1:2, :]).astype(BF16) for p, i, _, _ in pairs]
        for u, tile in enumerate(tiles):
            probs[slot, u] = tile
        give_probs(n).start()
        tiles = [
            dot(tile_turned(recv_ref, at // BLOCK, 2), tile)
            for tile, (_, _, at, _) in zip(tiles, pairs)
        ]
        for tile, (_, i, _, _) in zip(tiles, pairs):
            sums[i] += tile

    each_pairs(total, pair_ref, out_pairs)
    each_tile(lambda i: leaving(i, 2).start())
    steps = pair_steps(total)

    def end(n, carry):
        give_probs(n).wait()
        return carry

    lax.fori_loop(jnp.maximum(steps - RING, 0), steps, end, 0)
    for n in range(3):
        each_tile(lambda i, n=n: leaving(i, n).wait())


def run_attend(received, gains):
    hats = [((HEAD_DIM, LENGTH), BF16), ((LENGTH, HEAD_DIM), BF16)]
    return pl.pallas_call(
        attend_kernel,
        in_specs=[HBM_SPEC, VMEM_SPEC],
        out_specs=[SMEM_SPEC] * 2 + [VMEM_SPEC] + [HBM_SPEC] * 3 + [VMEM_SPEC] * 2 + [HBM_SPEC],
        out_shape=[
            shape((3, MOST_PAIRS + UNROLL), I32),
            shape((1,), I32),
            shape((TILES, 2, TILE), I32),
            *[shape(*hat) for hat in hats],
            shape((MOST_STEPS, UNROLL, KEYS, TILE), BF16),
            shape((TILES, 4, TILE), F32),
            shape((TILES, 2, TILE), F32),
            shape((TILES, HEAD_DIM, TILE), F32),
        ],
        scratch_shapes=[
            pltpu.VMEM((2 * HEAD_DIM, LENGTH), BF16),
            pltpu.VMEM((LENGTH + KEYS, 2 * HEAD_DIM), BF16),
            pltpu.VMEM((BLOCKS, 3 * BLOCK, 128), BF16),
            pltpu.VMEM((BLOCKS, EXTRA, 128), BF16),
            pltpu.SMEM((IMAGES + 1,), I32),
            pltpu.VMEM((MOST_PAIRS, KEYS, TILE), F32),
            pltpu.VMEM((TILES, 8, TILE), F32),
            pltpu.VMEM((RING, UNROLL, KEYS, TILE), BF16),
            pltpu.VMEM((TILES, HEAD_DIM, TILE), F32),
            pltpu.SemaphoreType.DMA((TILES,)),
            pltpu.SemaphoreType.DMA((1,)),
            pltpu.SemaphoreType.DMA((3, TILES)),
            pltpu.SemaphoreType.DMA((RING,)),
        ],
        compiler_params=pltpu.CompilerParams(vmem_limit_bytes=VMEM_LIMIT),
        cost_estimate=WORK,
        name="attend",
    )(received, gains)


def loss_kernel(
    labels_ref, mixture_ref, pair_ref, total_ref,
    all_ref, out_in, probs_in,
    send_out, grad_turned_out, inner_ref, counts_ref,
    coef_rows, loss_rows, grad_low, grad_v, probs, recv_ref, extra_ref, out_ref, first_ref, value_ref,
    grad_turned_ref, sems, in_sems, extra_sem, out_sems,
):
    def arrival(i, n):
        source, target = (
            (all_ref.at[tile_blocks(i), pl.ds(0, BLOCK), :], recv_ref.at[tile_blocks(i)]),
            (out_in.at[i], out_ref.at[i]),
        )[n]
        return pltpu.make_async_copy(source, target, in_sems.at[n, i])

    def leaving(i, n):
        rows = tile_at(i)
        blocks = tile_blocks(i)
        source, target = (
            (first_ref.at[blocks], send_out.at[blocks, pl.ds(0, BLOCK), :]),
            (grad_turned_ref.at[:, rows], grad_turned_out.at[:, rows]),
            (value_ref.at[blocks], send_out.at[blocks, pl.ds(BLOCK, BLOCK + EXTRA), :]),
        )[n]
        return pltpu.make_async_copy(source, target, out_sems.at[n, i])

    def take_probs(n):
        return pltpu.make_async_copy(probs_in.at[n], probs.at[n], sems.at[n])

    def start_probs(n, carry):
        take_probs(n).start()
        return carry

    extra = pltpu.make_async_copy(
        all_ref.at[:, pl.ds(BLOCK, EXTRA), :], extra_ref, extra_sem.at[0]
    )
    extra.start()
    for n in range(2):
        each_tile(lambda i, n=n: arrival(i, n).start())
    lax.fori_loop(0, pair_steps(total_ref[0]), start_probs, 0)

    extra.wait()
    seg_all = extra_ref[:, 0, :].astype(F32)
    group = jnp.zeros((BLOCKS, 128), F32)
    for s in range(IMAGES):
        group = jnp.where(seg_all == float(s), labels_ref[0, s].astype(F32), group)
    others = [extra_ref[:, 1 + p, :].astype(F32) for p in range(PACKS)]
    total_mix = mixture_ref[0]
    for g in range(1, GROUPS):
        total_mix = total_mix + mixture_ref[g]
    lane = lax.broadcasted_iota(I32, (1, 128), 1)
    coef = jnp.zeros((BLOCKS, 128), F32)
    count_row = jnp.zeros((1, 128), F32)
    for g in range(GROUPS):
        hits = sum((other == float(g)).astype(F32) for other in others)
        count = jnp.sum(jnp.sum(hits, 0, keepdims=True), 1, keepdims=True)
        share = jnp.full((1, 1), mixture_ref[g], F32) / total_mix
        coef = jnp.where(group == float(g), share / (count * (HEADS * HEAD_DIM)), coef)
        count_row = jnp.where(lane == g, count, count_row)
    counts_ref[...] = count_row
    for b in range(BLOCKS):
        tile, at = block_row(b)
        coef_rows[tile, 0:1, at] = coef[b : b + 1, :]

    def finish(i, carry):
        for n in range(2):
            arrival(i, n).wait()
        rows = tile_at(i)
        head_out = out_ref[i]
        misfit = head_out - tile_turned(recv_ref, i * PAIR, 0).astype(F32)
        loss_rows[i, 0:1, :] = 0.5 * jnp.sum(misfit * misfit, 0, keepdims=True)
        grad_out = coef_rows[i, 0:1, :] * misfit
        inner_ref[i, 0:1, :] = jnp.sum(grad_out * head_out, 0, keepdims=True)
        grad_turned = grad_out.astype(BF16)
        grad_turned_ref[:, rows] = grad_turned
        grad_low[rows, :] = grad_turned.T
        grad_v[rows, :] = jnp.zeros((TILE, HEAD_DIM), F32)
        low = head_out.astype(BF16)
        for b in range(PAIR):
            first_ref[i * PAIR + b] = low[:, b * BLOCK : (b + 1) * BLOCK]
        for n in range(2):
            leaving(i, n).start()
        return carry

    lax.fori_loop(0, TILES, finish, 0, unroll=TILES)

    rows = [block_row(b) for b in range(BLOCKS)]
    losses = jnp.concatenate([loss_rows[tile, 0:1, at] for tile, at in rows], 0)
    loss_row = group_sums(group, losses)
    high = loss_row.astype(BF16)
    left = loss_row - high.astype(F32)
    middle = left.astype(BF16)
    low = (left - middle.astype(F32)).astype(BF16)
    row = lax.broadcasted_iota(I32, (EXTRA, 128), 0)
    pieces = jnp.zeros((EXTRA, 128), F32)
    for n, piece in enumerate((high, middle, low)):
        pieces = jnp.where(row == n, piece.astype(F32), pieces)
    value_ref[:, BLOCK:, :] = jnp.broadcast_to(pieces.astype(BF16)[None], (BLOCKS, EXTRA, 128))

    def add_pairs(n, pairs):
        take_probs(n).wait()
        tiles = [dot(probs[n, u], grad_low[tile_at(pair[1]), :]) for u, pair in enumerate(pairs)]
        for tile, (_, _, at, _) in zip(tiles, pairs):
            grad_v[pl.ds(at, KEYS), :] += tile

    each_pairs(total_ref[0], pair_ref, add_pairs)

    def give(i, carry):
        value_ref[pl.ds(i * PAIR, PAIR), 0:BLOCK, :] = (
            grad_v[tile_at(i), :].astype(BF16).reshape(PAIR, BLOCK, HEAD_DIM)
        )
        leaving(i, 2).start()
        return carry

    lax.fori_loop(0, TILES, give, 0, unroll=TILES)
    for n in range(3):
        each_tile(lambda i, n=n: leaving(i, n).wait())


def run_loss(labels, mixture, pairs, total, second, head_out, probs):
    return pl.pallas_call(
        loss_kernel,
        in_specs=[SMEM_SPEC] * 4 + [HBM_SPEC] * 3,
        out_specs=[HBM_SPEC] * 2 + [VMEM_SPEC] * 2,
        out_shape=[
            shape((BLOCKS, 2 * BLOCK + EXTRA, 128), BF16),
            shape((HEAD_DIM, LENGTH), BF16),
            shape((TILES, 1, TILE), F32),
            shape((1, 128), F32),
        ],
        scratch_shapes=[
            pltpu.VMEM((TILES, 1, TILE), F32),
            pltpu.VMEM((TILES, 1, TILE), F32),
            pltpu.VMEM((LENGTH, HEAD_DIM), BF16),
            pltpu.VMEM((LENGTH, HEAD_DIM), F32),
            pltpu.VMEM((MOST_STEPS, UNROLL, KEYS, TILE), BF16),
            pltpu.VMEM((BLOCKS, BLOCK, 128), BF16),
            pltpu.VMEM((BLOCKS, EXTRA, 128), BF16),
            pltpu.VMEM((TILES, HEAD_DIM, TILE), F32),
            pltpu.VMEM((BLOCKS, BLOCK, 128), BF16),
            pltpu.VMEM((BLOCKS, BLOCK + EXTRA, 128), BF16),
            pltpu.VMEM((HEAD_DIM, LENGTH), BF16),
            pltpu.SemaphoreType.DMA((MOST_STEPS,)),
            pltpu.SemaphoreType.DMA((2, TILES)),
            pltpu.SemaphoreType.DMA((1,)),
            pltpu.SemaphoreType.DMA((3, TILES)),
        ],
        compiler_params=pltpu.CompilerParams(vmem_limit_bytes=VMEM_LIMIT),
        name="loss_and_grad_value",
    )(labels, mixture, pairs, total, second, head_out, probs)


def backward_kernel(
    pair_ref, total_ref,
    all_ref, q_turned_in, k_hat_in, grad_turned_in,
    gains_ref, moments_ref, span_rows_ref, norm_ref, inner_ref,
    send_out, gain_out_ref,
    grad_q, grad_k, q_hat_ref, k_turned_ref, value_ref, raw_ref, q_turned_ref, k_hat_ref,
    grad_turned_ref, send_ref, in_sems, out_sems,
):
    def arrival(i, n):
        rows = tile_at(i)
        blocks = tile_blocks(i)
        source, target = (
            (q_turned_in.at[:, rows], q_turned_ref.at[:, rows]),
            (k_hat_in.at[rows, :], k_hat_ref.at[rows, :]),
            (all_ref.at[blocks, pl.ds(0, 3 * BLOCK), :], raw_ref.at[blocks]),
            (grad_turned_in.at[:, rows], grad_turned_ref.at[:, rows]),
        )[n]
        return pltpu.make_async_copy(source, target, in_sems.at[n, i])

    def leaving(i):
        blocks = tile_blocks(i)
        return pltpu.make_async_copy(send_ref.at[blocks], send_out.at[blocks], out_sems.at[i])

    for n in range(4):
        each_tile(lambda i, n=n: arrival(i, n).start())

    def clear(i, carry):
        for n in range(2):
            arrival(i, n).wait()
        q_hat_ref[tile_at(i), :] = q_turned_ref[:, tile_at(i)].T
        k_turned_ref[:, tile_at(i)] = k_hat_ref[tile_at(i), :].T
        arrival(i, 2).wait()
        value_ref[tile_at(i), :] = tile_turned(raw_ref, i * PAIR, 2).T
        grad_q[i] = jnp.zeros((HEAD_DIM, TILE), F32)
        grad_k[tile_at(i), :] = jnp.zeros((TILE, HEAD_DIM), F32)
        return carry

    lax.fori_loop(0, TILES, clear, 0, unroll=TILES)
    each_tile(lambda i: arrival(i, 3).wait())

    def add_pairs(n, pairs):
        tiles = [
            dot(k_hat_ref[pl.ds(at, KEYS), :], q_turned_ref[:, tile_at(i)]) for _, i, at, _ in pairs
        ]
        prob_grads = [
            dot(value_ref[pl.ds(at, KEYS), :], grad_turned_ref[:, tile_at(i)])
            for _, i, at, _ in pairs
        ]
        tiles = [
            softmax_tile(tile, span_rows_ref, norm_ref, i, mask_at)
            for tile, (_, i, _, mask_at) in zip(tiles, pairs)
        ]
        tiles = [
            (tile * (prob - inner_ref[i, 0:1, :]) * SCALE).astype(BF16)
            for tile, prob, (_, i, _, _) in zip(tiles, prob_grads, pairs)
        ]
        keys = [dot(tile, q_hat_ref[tile_at(i), :]) for tile, (_, i, _, _) in zip(tiles, pairs)]
        queries = [
            dot(k_turned_ref[:, pl.ds(at, KEYS)], tile) for tile, (_, _, at, _) in zip(tiles, pairs)
        ]
        for key, query, (_, i, at, _) in zip(keys, queries, pairs):
            grad_k[pl.ds(at, KEYS), :] += key
            grad_q[i] += query

    each_pairs(total_ref[0], pair_ref, add_pairs)

    gains = jnp.concatenate([gains_ref[...], jnp.zeros((6, HEAD_DIM), F32)], 0).T

    def norm_backward(i, n, grad_hat):
        mean = moments_ref[i, 2 * n : 2 * n + 1, :]
        inverse = moments_ref[i, 2 * n + 1 : 2 * n + 2, :]
        normed = (tile_turned(raw_ref, i * PAIR, n).astype(F32) - mean) * inverse
        grad_normed = grad_hat * gains[:, n : n + 1]
        inner = mean_down(grad_normed * normed)
        grad_in = inverse * (grad_normed - mean_down(grad_normed) - normed * inner)
        send_ref[pl.ds(i * PAIR, PAIR), n * BLOCK : (n + 1) * BLOCK, :] = grad_in.astype(
            BF16
        ).T.reshape(PAIR, BLOCK, HEAD_DIM)
        grad_gain = grad_hat * normed
        return sum(grad_gain[:, c : c + 128] for c in range(0, TILE, 128))

    def finish(i, gain_sums):
        gain_q, gain_k = gain_sums
        gain_q = gain_q + norm_backward(i, 0, grad_q[i])
        gain_k = gain_k + norm_backward(i, 1, grad_k[tile_at(i), :].T)
        leaving(i).start()
        return gain_q, gain_k

    zero = jnp.zeros((HEAD_DIM, 128), F32)
    gain_q, gain_k = lax.fori_loop(0, TILES, finish, (zero, zero), unroll=TILES)
    gain_out_ref[0:1, :] = jnp.sum(gain_q.T, 0, keepdims=True)
    gain_out_ref[1:2, :] = jnp.sum(gain_k.T, 0, keepdims=True)
    each_tile(lambda i: leaving(i).wait())


def run_backward(pairs, total, received, q_turned, k_hat, grad_turned, *arrays):
    return pl.pallas_call(
        backward_kernel,
        in_specs=[SMEM_SPEC] * 2 + [HBM_SPEC] * 4 + [VMEM_SPEC] * len(arrays),
        out_specs=[HBM_SPEC, VMEM_SPEC],
        out_shape=[shape((BLOCKS, 2 * BLOCK, 128), BF16), shape((2, HEAD_DIM), F32)],
        scratch_shapes=[
            pltpu.VMEM((TILES, HEAD_DIM, TILE), F32),
            pltpu.VMEM((LENGTH, HEAD_DIM), F32),
            pltpu.VMEM((LENGTH, HEAD_DIM), BF16),
            pltpu.VMEM((HEAD_DIM, LENGTH), BF16),
            pltpu.VMEM((LENGTH, HEAD_DIM), BF16),
            pltpu.VMEM((BLOCKS, 3 * BLOCK, 128), BF16),
            pltpu.VMEM((HEAD_DIM, LENGTH), BF16),
            pltpu.VMEM((LENGTH, HEAD_DIM), BF16),
            pltpu.VMEM((HEAD_DIM, LENGTH), BF16),
            pltpu.VMEM((BLOCKS, 2 * BLOCK, 128), BF16),
            pltpu.SemaphoreType.DMA((4, TILES)),
            pltpu.SemaphoreType.DMA((TILES,)),
        ],
        compiler_params=pltpu.CompilerParams(vmem_limit_bytes=VMEM_LIMIT),
        cost_estimate=WORK,
        name="backward",
    )(pairs, total, received, q_turned, k_hat, grad_turned, *arrays)


def over_packs(value):
    moved = [value]
    for shift in range(1, PACKS):
        pairs = [(i, (i + shift) % PACKS) for i in range(PACKS)]
        moved.append(lax.ppermute(value, "pack", pairs))
    return moved


def exchange(slab):
    return lax.all_to_all(slab, "seq", split_axis=0, concat_axis=0, tiled=True)


def on_device(
    query_rows, key_rows, value_rows, target_rows, norm_gains, segment_ids, group_labels, mixture
):
    gains = norm_gains.reshape(2, HEAD_DIM)
    first = exchange(pack_rows((query_rows, key_rows, value_rows), segment_ids, "pack_first"))

    image_hot = segment_ids[0][:, None] == jnp.arange(IMAGES, dtype=I32)[None, :]
    labels = jnp.sum(jnp.where(image_hot, group_labels[0][None, :], 0), 1)[None, :]
    extra = jnp.concatenate([segment_ids.astype(F32), *over_packs(labels.astype(F32))], 0)
    second = exchange(pack_rows((target_rows,), extra, "pack_second"))

    pairs, total, span_rows, *hats, probs, moments, norms, head_out = run_attend(first, gains)
    send, grad_turned, inner, counts = run_loss(
        group_labels, mixture, pairs, total, second, head_out, probs
    )
    back = exchange(send)
    send, gain_part = run_backward(
        pairs, total, first, *hats, grad_turned, gains, moments, span_rows, norms, inner
    )
    back, send = lax.optimization_barrier((back, send))
    last = exchange(send)
    attended, grad_value = unpack_rows(back, 2, (0,), "unpack_first")
    losses = jnp.sum(back[:, 2 * BLOCK : 2 * BLOCK + 3, :GROUPS].astype(F32), (0, 1))
    group_total = sum(over_packs(losses))
    group_loss = group_total / (counts[0, :GROUPS] * (HEADS * HEAD_DIM))
    shares = mixture / jnp.sum(mixture)
    raised = shares * jnp.exp(ETA * group_loss)
    new_mixture = raised / jnp.sum(raised)
    grad_gains = sum(over_packs(gain_part)).reshape(2, 1, HEAD_DIM)
    grad_query, grad_key = unpack_rows(last, 2, (), "unpack_last")
    return (attended, grad_query, grad_key, grad_value, grad_gains, new_mixture)


def solution(mesh):
    rows = P("pack", "seq", None)
    gains = P(None, "seq", None)
    return jax.shard_map(
        on_device,
        mesh=mesh,
        in_specs=(rows, rows, rows, rows, gains, P("pack", "seq"), P("pack", None), P()),
        out_specs=(rows, rows, rows, rows, gains, P()),
        check_vma=False,
    )
```

```python
import functools

import jax
import jax.numpy as jnp
from jax import lax
from jax.experimental import pallas as pl
from jax.experimental.pallas import tpu as pltpu
from jax.sharding import PartitionSpec as P

HEADS = 32
HEAD_DIM = 128
IMAGES = 16
GROUPS = 8
PACKS = 4
LENGTH = 4096

NEG = -1e30
EPS = 1e-06
ETA = 2.0
SCALE = HEAD_DIM ** (-0.5)
EXP_SCALE = SCALE * 1.4426950408889634

BLOCK = 128
BLOCKS = LENGTH // BLOCK
TILE = 256
TILES = LENGTH // TILE
PAIR = TILE // BLOCK
KEYS = 256
UNROLL = 10
MOST_PAIRS = (LENGTH * (1024 // TILE + 1) + TILES * (BLOCK - 1 + KEYS - 1)) // KEYS
MOST_STEPS = MOST_PAIRS // UNROLL + 1
MOST_PAIRS = MOST_STEPS * UNROLL
RING = 4
SAFE_LOGIT = 70.0
EXTRA = 16
CHUNK = 8
CHUNKS = HEADS // CHUNK
VMEM_LIMIT = 63 * 1024 * 1024

BF16 = jnp.bfloat16
F32 = jnp.float32
I32 = jnp.int32

WORK = pl.CostEstimate(flops=1 << 33, bytes_accessed=1 << 25, transcendentals=1 << 22)

VMEM_SPEC = pl.BlockSpec(memory_space=pltpu.VMEM)
SMEM_SPEC = pl.BlockSpec(memory_space=pltpu.SMEM)
HBM_SPEC = pl.BlockSpec(memory_space=pltpu.HBM)


def shape(dims, dtype):
    return jax.ShapeDtypeStruct(dims, dtype)


def head_columns(h):
    return pl.ds(h * HEAD_DIM, HEAD_DIM)


def pack_kernel(count, *refs):
    row_refs, (extra_ref, out_ref, rows, slab, in_sems, out_sems) = refs[:count], refs[count:]

    def arrival(c, n):
        columns = pl.ds(c * CHUNK * HEAD_DIM, CHUNK * HEAD_DIM)
        return pltpu.make_async_copy(
            row_refs[n].at[0, :, columns], rows.at[n, :, columns], in_sems.at[n, c]
        )

    def leaving(c):
        heads = pl.ds(c * CHUNK, CHUNK)
        return pltpu.make_async_copy(slab.at[heads], out_ref.at[heads], out_sems.at[c])

    for c in range(CHUNKS):
        for n in range(count):
            arrival(c, n).start()
    extra = extra_ref[...].astype(F32)
    extra = jnp.concatenate([extra, jnp.zeros((EXTRA - extra.shape[0], 128), F32)], 0)
    slab[:, count * BLOCK :, :] = jnp.broadcast_to(extra.astype(BF16)[None], (HEADS, EXTRA, 128))
    for c in range(CHUNKS):
        for n in range(count):
            arrival(c, n).wait()
            for h in range(c * CHUNK, (c + 1) * CHUNK):
                block = rows[n, :, h * HEAD_DIM : (h + 1) * HEAD_DIM]
                slab[h, n * BLOCK : (n + 1) * BLOCK, :] = block.T
        leaving(c).start()
    for c in range(CHUNKS):
        leaving(c).wait()


def pack_rows(rows, extra, name):
    count = len(rows)
    slab = (HEADS, count * BLOCK + EXTRA, 128)
    return pl.pallas_call(
        functools.partial(pack_kernel, count),
        in_specs=[HBM_SPEC] * count + [VMEM_SPEC],
        out_specs=HBM_SPEC,
        out_shape=shape(slab, BF16),
        scratch_shapes=[
            pltpu.VMEM((count, BLOCK, HEADS * HEAD_DIM), BF16),
            pltpu.VMEM(slab, BF16),
            pltpu.SemaphoreType.DMA((count, CHUNKS)),
            pltpu.SemaphoreType.DMA((CHUNKS,)),
        ],
        compiler_params=pltpu.CompilerParams(vmem_limit_bytes=VMEM_LIMIT),
        name=name,
    )(*rows, extra)


def unpack_kernel(turned, in_ref, *refs):
    *row_refs, slab, rows, in_sems, out_sems = refs
    lines = len(row_refs) * BLOCK

    def arrival(c):
        heads = pl.ds(c * CHUNK, CHUNK)
        return pltpu.make_async_copy(
            in_ref.at[heads, pl.ds(0, lines), :], slab.at[heads], in_sems.at[c]
        )

    def leaving(h, n):
        columns = head_columns(h)
        source = slab.at[h, pl.ds(n * BLOCK, BLOCK), :]
        if n in turned:
            source = rows.at[:, columns]
        return pltpu.make_async_copy(source, row_refs[n].at[0, :, columns], out_sems.at[n, h])

    for c in range(CHUNKS):
        arrival(c).start()
    for c in range(CHUNKS):
        arrival(c).wait()
        for h in range(c * CHUNK, (c + 1) * CHUNK):
            for n in range(len(row_refs)):
                if n in turned:
                    block = slab[h, n * BLOCK : (n + 1) * BLOCK, :]
                    rows[:, h * HEAD_DIM : (h + 1) * HEAD_DIM] = block.T
                leaving(h, n).start()
    for h in range(HEADS):
        for n in range(len(row_refs)):
            leaving(h, n).wait()


def unpack_rows(slab, count, turned, name):
    return pl.pallas_call(
        functools.partial(unpack_kernel, turned),
        in_specs=[HBM_SPEC],
        out_specs=[HBM_SPEC] * count,
        out_shape=[shape((1, BLOCK, HEADS * HEAD_DIM), BF16)] * count,
        scratch_shapes=[
            pltpu.VMEM((HEADS, count * BLOCK, 128), BF16),
            pltpu.VMEM((BLOCK, HEADS * HEAD_DIM), BF16),
            pltpu.SemaphoreType.DMA((CHUNKS,)),
            pltpu.SemaphoreType.DMA((count, HEADS)),
        ],
        compiler_params=pltpu.CompilerParams(vmem_limit_bytes=VMEM_LIMIT),
        name=name,
    )(slab)


def dot(a, b, contract=((1,), (0,))):
    return lax.dot_general(a, b, (contract, ((), ())), preferred_element_type=F32)


def tile_turned(ref, block, part):
    lines = slice(part * BLOCK, (part + 1) * BLOCK)
    return jnp.concatenate([ref[block + b, lines, :] for b in range(PAIR)], 1)


def tile_at(i, size=TILE):
    return pl.ds(pl.multiple_of(i * size, size), size)


def mean_down(values):
    return jnp.sum(values, 0, keepdims=True) * (1.0 / HEAD_DIM)


def block_row(b):
    return b // PAIR, slice((b % PAIR) * BLOCK, (b % PAIR + 1) * BLOCK)


def group_sums(group, values):
    lane = lax.broadcasted_iota(I32, (1, 128), 1)
    sums = jnp.zeros((1, 128), F32)
    for g in range(GROUPS):
        part = jnp.sum(jnp.where(group == float(g), values, 0.0), 0, keepdims=True)
        sums = jnp.where(lane == g, jnp.sum(part, 1, keepdims=True), sums)
    return sums


def key_mask(span_rows_ref, i, start, step):
    first = span_rows_ref[i, 0:1, :] - start
    count = span_rows_ref[i, 1:2, :]
    row = lax.broadcasted_iota(I32, (step, TILE), 0)
    return (row - first).astype(jnp.uint32) < count.astype(jnp.uint32)


def masked(scores, span_rows_ref, i, mask_at):
    return jnp.where(key_mask(span_rows_ref, i, mask_at, KEYS), scores, NEG)


def pair_steps(total):
    return (total + UNROLL - 1) // UNROLL


def each_pairs(total, pair_ref, body):
    def some(n, carry):
        pairs = []
        for u in range(UNROLL):
            p = n * UNROLL + u
            at = pl.multiple_of(pair_ref[1, p], BLOCK)
            pairs.append((p, pair_ref[0, p], at, pair_ref[2, p]))
        body(n, pairs)
        return carry

    lax.fori_loop(0, pair_steps(total), some, 0)


def softmax_tile(scores, span_rows_ref, norm_ref, i, mask_at):
    scores = masked(scores, span_rows_ref, i, mask_at)
    return jnp.exp2(scores * EXP_SCALE - norm_ref[i, 0:1, :]) * norm_ref[i, 1:2, :]


def find_pairs(seg_all, starts, pair_ref, span_rows_ref):
    for s in range(IMAGES + 1):
        starts[s] = jnp.sum((seg_all < float(s)).astype(F32)).astype(I32)
    first = jnp.zeros((BLOCKS, 128), I32)
    count = jnp.zeros((BLOCKS, 128), I32)
    for s in range(IMAGES):
        here = seg_all == float(s)
        first = jnp.where(here, starts[s], first)
        count = jnp.where(here, starts[s + 1] - starts[s], count)
    for b in range(BLOCKS):
        tile, at = block_row(b)
        span_rows_ref[tile, 0:1, at] = first[b : b + 1, :]
        span_rows_ref[tile, 1:2, at] = count[b : b + 1, :]

    def span(i, total):
        low, high = jnp.int32(0), jnp.int32(LENGTH)
        for s in range(1, IMAGES):
            low = jnp.where(starts[s] <= i * TILE, starts[s], low)
        for s in range(IMAGES - 1, 0, -1):
            high = jnp.where(starts[s] > i * TILE + TILE - 1, starts[s], high)
        low = (low // BLOCK) * BLOCK
        steps = (high - low + KEYS - 1) // KEYS
        low = jnp.minimum(low, LENGTH - steps * KEYS)

        def add(j, carry):
            pair_ref[0, total + j] = i
            pair_ref[1, total + j] = low + j * KEYS
            pair_ref[2, total + j] = low + j * KEYS
            return carry

        lax.fori_loop(0, steps, add, 0)
        return total + steps

    total = lax.fori_loop(0, TILES, span, jnp.int32(0))
    for u in range(UNROLL):
        pair_ref[0, total + u] = 0
        pair_ref[1, total + u] = 0
        pair_ref[2, total + u] = -(1 << 20)
    return total


def each_tile(what):
    def one(i, carry):
        what(i)
        return carry

    lax.fori_loop(0, TILES, one, 0)


def tile_blocks(i):
    return pl.ds(i * PAIR, PAIR)


def attend_kernel(
    all_ref, gains_ref,
    pair_ref, total_ref, span_rows_ref, *refs,
):
    hat_outs, probs_out, refs = refs[:2], refs[2], refs[3:]
    (moments_ref, norm_ref, out_ref), refs = refs[:3], refs[3:]
    (q_turned_ref, k_hat_ref), refs = refs[:2], refs[2:]
    recv_ref, extra_ref, starts, terms, fold, probs, sums = refs[:7]
    in_sems, extra_sem, out_sems, prob_sems = refs[7:]

    def arrival(i):
        return pltpu.make_async_copy(
            all_ref.at[tile_blocks(i), pl.ds(0, 3 * BLOCK), :],
            recv_ref.at[tile_blocks(i)],
            in_sems.at[i],
        )

    def leaving(i, n):
        rows = tile_at(i)
        source, target = (
            (q_turned_ref.at[pl.ds(0, HEAD_DIM), rows], hat_outs[0].at[:, rows]),
            (k_hat_ref.at[rows, pl.ds(0, HEAD_DIM)], hat_outs[1].at[rows, :]),
            (sums.at[i], out_ref.at[i]),
        )[n]
        return pltpu.make_async_copy(source, target, out_sems.at[n, i])

    extra = pltpu.make_async_copy(
        all_ref.at[:, pl.ds(3 * BLOCK, EXTRA), :], extra_ref, extra_sem.at[0]
    )
    extra.start()
    each_tile(lambda i: arrival(i).start())
    extra.wait()
    total = find_pairs(extra_ref[:, 0, :].astype(F32), starts, pair_ref, span_rows_ref)
    total_ref[0] = total
    gains = jnp.concatenate([gains_ref[...], jnp.zeros((6, HEAD_DIM), F32)], 0).T

    lane = lax.broadcasted_iota(I32, (1, HEAD_DIM), 1)
    seg_from = jnp.full((1, HEAD_DIM), LENGTH, I32)
    seg_to = jnp.full((1, HEAD_DIM), LENGTH, I32)
    for s in range(IMAGES):
        seg_from = jnp.where(lane == s, starts[s], seg_from)
        seg_to = jnp.where(lane == s, starts[s + 1], seg_to)
    k_hat_ref[LENGTH:, :HEAD_DIM] = jnp.zeros((KEYS, HEAD_DIM), BF16)
    nobody = jnp.where(lane == IMAGES, 1.0, 0.0)
    k_hat_ref[LENGTH:, HEAD_DIM:] = jnp.broadcast_to(nobody, (KEYS, HEAD_DIM)).astype(BF16)

    def prepare(i, most):
        arrival(i).wait()
        rows = tile_at(i)
        sizes = []
        for n in range(2):
            values = tile_turned(recv_ref, i * PAIR, n).astype(F32)
            mean = mean_down(values)
            centre = values - mean
            inverse = lax.rsqrt(mean_down(centre * centre) + EPS)
            moments_ref[i, 2 * n : 2 * n + 1, :] = mean
            moments_ref[i, 2 * n + 1 : 2 * n + 2, :] = inverse
            hat = centre * inverse * gains[:, n : n + 1]
            sizes.append(jnp.maximum(most[n], mean_down(hat * hat)))
            if n == 0:
                q_turned_ref[:HEAD_DIM, rows] = hat.astype(BF16)
            else:
                k_hat_ref[rows, :HEAD_DIM] = hat.astype(BF16).T
        seg_q = [extra_ref[i * PAIR + b, 0:1, :].astype(F32) for b in range(PAIR)]
        own = jnp.concatenate(seg_q, 1).astype(I32)
        segment = lax.broadcasted_iota(I32, (HEAD_DIM, TILE), 0)
        q_turned_ref[HEAD_DIM:, rows] = jnp.where(segment == own, 0.0, NEG).astype(BF16)
        row = lax.broadcasted_iota(I32, (TILE, HEAD_DIM), 0) + i * TILE
        inside = (row >= seg_from) & (row < seg_to)
        k_hat_ref[rows, HEAD_DIM:] = jnp.where(inside, 1.0, 0.0).astype(BF16)
        for n in range(2):
            leaving(i, n).start()
        sums[i] = jnp.zeros((HEAD_DIM, TILE), F32)
        norm_ref[i] = jnp.zeros((2, TILE), F32)
        fold[i] = jnp.zeros((8, TILE), F32)
        return tuple(sizes)

    zero = jnp.zeros((1, TILE), F32)
    most_q, most_k = lax.fori_loop(0, TILES, prepare, (zero, zero), unroll=TILES)
    bound = jnp.max(most_q) * jnp.max(most_k) * HEAD_DIM

    def scores_of(pairs):
        tiles = []
        for _, i, at, mask_at in pairs:
            at = pl.multiple_of(jnp.where(mask_at < 0, LENGTH, at), BLOCK)
            tiles.append(dot(k_hat_ref[pl.ds(at, KEYS), :], q_turned_ref[:, tile_at(i)]))
        return tiles

    @pl.when(jnp.logical_not(bound <= SAFE_LOGIT * SAFE_LOGIT))
    def _():
        def clear(i, carry):
            fold[i] = jnp.full((8, TILE), NEG, F32)
            return carry

        lax.fori_loop(0, TILES, clear, 0)

        def top_pairs(n, pairs):
            for tile, (_, i, _, _) in zip(scores_of(pairs), pairs):
                top = jnp.max(tile.reshape(KEYS // 8, 8, TILE), 0)
                fold[i] = jnp.maximum(fold[i], top)

        each_pairs(total, pair_ref, top_pairs)

        def finish(i, carry):
            norm_ref[i, 0:1, :] = jnp.max(fold[i], 0, keepdims=True) * EXP_SCALE
            fold[i] = jnp.zeros((8, TILE), F32)
            return carry

        lax.fori_loop(0, TILES, finish, 0)

    def exp_pairs(n, pairs):
        sums = []
        for tile, (p, i, _, _) in zip(scores_of(pairs), pairs):
            tile = jnp.exp2(tile * EXP_SCALE - norm_ref[i, 0:1, :])
            terms[p] = tile
            sums.append(jnp.sum(tile.reshape(KEYS // 8, 8, TILE), 0))
        for part, (_, i, _, _) in zip(sums, pairs):
            fold[i] += part

    each_pairs(total, pair_ref, exp_pairs)

    def invert(i, carry):
        norm_ref[i, 1:2, :] = 1.0 / jnp.sum(fold[i], 0, keepdims=True)
        return carry

    lax.fori_loop(0, TILES, invert, 0)

    def give_probs(n):
        slot = lax.rem(n, RING)
        return pltpu.make_async_copy(probs.at[slot], probs_out.at[n], prob_sems.at[slot])

    def out_pairs(n, pairs):
        slot = lax.rem(n, RING)

        @pl.when(n >= RING)
        def _():
            give_probs(n - RING).wait()

        tiles = [(terms[p] * norm_ref[i, 1:2, :]).astype(BF16) for p, i, _, _ in pairs]
        for u, tile in enumerate(tiles):
            probs[slot, u] = tile
        give_probs(n).start()
        tiles = [
            dot(tile_turned(recv_ref, at // BLOCK, 2), tile)
            for tile, (_, _, at, _) in zip(tiles, pairs)
        ]
        for tile, (_, i, _, _) in zip(tiles, pairs):
            sums[i] += tile

    each_pairs(total, pair_ref, out_pairs)
    each_tile(lambda i: leaving(i, 2).start())
    steps = pair_steps(total)

    def end(n, carry):
        give_probs(n).wait()
        return carry

    lax.fori_loop(jnp.maximum(steps - RING, 0), steps, end, 0)
    for n in range(3):
        each_tile(lambda i, n=n: leaving(i, n).wait())


def run_attend(received, gains):
    hats = [((HEAD_DIM, LENGTH), BF16), ((LENGTH, HEAD_DIM), BF16)]
    return pl.pallas_call(
        attend_kernel,
        in_specs=[HBM_SPEC, VMEM_SPEC],
        out_specs=[SMEM_SPEC] * 2 + [VMEM_SPEC] + [HBM_SPEC] * 3 + [VMEM_SPEC] * 2 + [HBM_SPEC],
        out_shape=[
            shape((3, MOST_PAIRS + UNROLL), I32),
            shape((1,), I32),
            shape((TILES, 2, TILE), I32),
            *[shape(*hat) for hat in hats],
            shape((MOST_STEPS, UNROLL, KEYS, TILE), BF16),
            shape((TILES, 4, TILE), F32),
            shape((TILES, 2, TILE), F32),
            shape((TILES, HEAD_DIM, TILE), F32),
        ],
        scratch_shapes=[
            pltpu.VMEM((2 * HEAD_DIM, LENGTH), BF16),
            pltpu.VMEM((LENGTH + KEYS, 2 * HEAD_DIM), BF16),
            pltpu.VMEM((BLOCKS, 3 * BLOCK, 128), BF16),
            pltpu.VMEM((BLOCKS, EXTRA, 128), BF16),
            pltpu.SMEM((IMAGES + 1,), I32),
            pltpu.VMEM((MOST_PAIRS, KEYS, TILE), F32),
            pltpu.VMEM((TILES, 8, TILE), F32),
            pltpu.VMEM((RING, UNROLL, KEYS, TILE), BF16),
            pltpu.VMEM((TILES, HEAD_DIM, TILE), F32),
            pltpu.SemaphoreType.DMA((TILES,)),
            pltpu.SemaphoreType.DMA((1,)),
            pltpu.SemaphoreType.DMA((3, TILES)),
            pltpu.SemaphoreType.DMA((RING,)),
        ],
        compiler_params=pltpu.CompilerParams(vmem_limit_bytes=VMEM_LIMIT),
        cost_estimate=WORK,
        name="attend",
    )(received, gains)


def loss_kernel(
    labels_ref, mixture_ref, pair_ref, total_ref,
    all_ref, out_in, probs_in,
    send_out, grad_turned_out, inner_ref, counts_ref,
    coef_rows, loss_rows, grad_low, grad_v, probs, recv_ref, extra_ref, out_ref, first_ref, value_ref,
    grad_turned_ref, sems, in_sems, extra_sem, out_sems,
):
    def arrival(i, n):
        source, target = (
            (all_ref.at[tile_blocks(i), pl.ds(0, BLOCK), :], recv_ref.at[tile_blocks(i)]),
            (out_in.at[i], out_ref.at[i]),
        )[n]
        return pltpu.make_async_copy(source, target, in_sems.at[n, i])

    def leaving(i, n):
        rows = tile_at(i)
        blocks = tile_blocks(i)
        source, target = (
            (first_ref.at[blocks], send_out.at[blocks, pl.ds(0, BLOCK), :]),
            (grad_turned_ref.at[:, rows], grad_turned_out.at[:, rows]),
            (value_ref.at[blocks], send_out.at[blocks, pl.ds(BLOCK, BLOCK + EXTRA), :]),
        )[n]
        return pltpu.make_async_copy(source, target, out_sems.at[n, i])

    def take_probs(n):
        return pltpu.make_async_copy(probs_in.at[n], probs.at[n], sems.at[n])

    def start_probs(n, carry):
        take_probs(n).start()
        return carry

    extra = pltpu.make_async_copy(
        all_ref.at[:, pl.ds(BLOCK, EXTRA), :], extra_ref, extra_sem.at[0]
    )
    extra.start()
    for n in range(2):
        each_tile(lambda i, n=n: arrival(i, n).start())
    lax.fori_loop(0, pair_steps(total_ref[0]), start_probs, 0)

    extra.wait()
    seg_all = extra_ref[:, 0, :].astype(F32)
    group = jnp.zeros((BLOCKS, 128), F32)
    for s in range(IMAGES):
        group = jnp.where(seg_all == float(s), labels_ref[0, s].astype(F32), group)
    others = [extra_ref[:, 1 + p, :].astype(F32) for p in range(PACKS)]
    total_mix = mixture_ref[0]
    for g in range(1, GROUPS):
        total_mix = total_mix + mixture_ref[g]
    lane = lax.broadcasted_iota(I32, (1, 128), 1)
    coef = jnp.zeros((BLOCKS, 128), F32)
    count_row = jnp.zeros((1, 128), F32)
    for g in range(GROUPS):
        hits = sum((other == float(g)).astype(F32) for other in others)
        count = jnp.sum(jnp.sum(hits, 0, keepdims=True), 1, keepdims=True)
        share = jnp.full((1, 1), mixture_ref[g], F32) / total_mix
        coef = jnp.where(group == float(g), share / (count * (HEADS * HEAD_DIM)), coef)
        count_row = jnp.where(lane == g, count, count_row)
    counts_ref[...] = count_row
    for b in range(BLOCKS):
        tile, at = block_row(b)
        coef_rows[tile, 0:1, at] = coef[b : b + 1, :]

    def finish(i, carry):
        for n in range(2):
            arrival(i, n).wait()
        rows = tile_at(i)
        head_out = out_ref[i]
        misfit = head_out - tile_turned(recv_ref, i * PAIR, 0).astype(F32)
        loss_rows[i, 0:1, :] = 0.5 * jnp.sum(misfit * misfit, 0, keepdims=True)
        grad_out = coef_rows[i, 0:1, :] * misfit
        inner_ref[i, 0:1, :] = jnp.sum(grad_out * head_out, 0, keepdims=True)
        grad_turned = grad_out.astype(BF16)
        grad_turned_ref[:, rows] = grad_turned
        grad_low[rows, :] = grad_turned.T
        grad_v[rows, :] = jnp.zeros((TILE, HEAD_DIM), F32)
        low = head_out.astype(BF16)
        for b in range(PAIR):
            first_ref[i * PAIR + b] = low[:, b * BLOCK : (b + 1) * BLOCK]
        for n in range(2):
            leaving(i, n).start()
        return carry

    lax.fori_loop(0, TILES, finish, 0, unroll=TILES)

    rows = [block_row(b) for b in range(BLOCKS)]
    losses = jnp.concatenate([loss_rows[tile, 0:1, at] for tile, at in rows], 0)
    loss_row = group_sums(group, losses)
    high = loss_row.astype(BF16)
    left = loss_row - high.astype(F32)
    middle = left.astype(BF16)
    low = (left - middle.astype(F32)).astype(BF16)
    row = lax.broadcasted_iota(I32, (EXTRA, 128), 0)
    pieces = jnp.zeros((EXTRA, 128), F32)
    for n, piece in enumerate((high, middle, low)):
        pieces = jnp.where(row == n, piece.astype(F32), pieces)
    value_ref[:, BLOCK:, :] = jnp.broadcast_to(pieces.astype(BF16)[None], (BLOCKS, EXTRA, 128))

    def add_pairs(n, pairs):
        take_probs(n).wait()
        tiles = [dot(probs[n, u], grad_low[tile_at(pair[1]), :]) for u, pair in enumerate(pairs)]
        for tile, (_, _, at, _) in zip(tiles, pairs):
            grad_v[pl.ds(at, KEYS), :] += tile

    each_pairs(total_ref[0], pair_ref, add_pairs)

    def give(i, carry):
        value_ref[pl.ds(i * PAIR, PAIR), 0:BLOCK, :] = (
            grad_v[tile_at(i), :].astype(BF16).reshape(PAIR, BLOCK, HEAD_DIM)
        )
        leaving(i, 2).start()
        return carry

    lax.fori_loop(0, TILES, give, 0, unroll=TILES)
    for n in range(3):
        each_tile(lambda i, n=n: leaving(i, n).wait())


def run_loss(labels, mixture, pairs, total, second, head_out, probs):
    return pl.pallas_call(
        loss_kernel,
        in_specs=[SMEM_SPEC] * 4 + [HBM_SPEC] * 3,
        out_specs=[HBM_SPEC] * 2 + [VMEM_SPEC] * 2,
        out_shape=[
            shape((BLOCKS, 2 * BLOCK + EXTRA, 128), BF16),
            shape((HEAD_DIM, LENGTH), BF16),
            shape((TILES, 1, TILE), F32),
            shape((1, 128), F32),
        ],
        scratch_shapes=[
            pltpu.VMEM((TILES, 1, TILE), F32),
            pltpu.VMEM((TILES, 1, TILE), F32),
            pltpu.VMEM((LENGTH, HEAD_DIM), BF16),
            pltpu.VMEM((LENGTH, HEAD_DIM), F32),
            pltpu.VMEM((MOST_STEPS, UNROLL, KEYS, TILE), BF16),
            pltpu.VMEM((BLOCKS, BLOCK, 128), BF16),
            pltpu.VMEM((BLOCKS, EXTRA, 128), BF16),
            pltpu.VMEM((TILES, HEAD_DIM, TILE), F32),
            pltpu.VMEM((BLOCKS, BLOCK, 128), BF16),
            pltpu.VMEM((BLOCKS, BLOCK + EXTRA, 128), BF16),
            pltpu.VMEM((HEAD_DIM, LENGTH), BF16),
            pltpu.SemaphoreType.DMA((MOST_STEPS,)),
            pltpu.SemaphoreType.DMA((2, TILES)),
            pltpu.SemaphoreType.DMA((1,)),
            pltpu.SemaphoreType.DMA((3, TILES)),
        ],
        compiler_params=pltpu.CompilerParams(vmem_limit_bytes=VMEM_LIMIT),
        name="loss_and_grad_value",
    )(labels, mixture, pairs, total, second, head_out, probs)


def backward_kernel(
    pair_ref, total_ref,
    all_ref, q_turned_in, k_hat_in, grad_turned_in,
    gains_ref, moments_ref, span_rows_ref, norm_ref, inner_ref,
    send_out, gain_out_ref,
    grad_q, grad_k, q_hat_ref, k_turned_ref, value_ref, raw_ref, q_turned_ref, k_hat_ref,
    grad_turned_ref, send_ref, in_sems, out_sems,
):
    def arrival(i, n):
        rows = tile_at(i)
        blocks = tile_blocks(i)
        source, target = (
            (q_turned_in.at[:, rows], q_turned_ref.at[:, rows]),
            (k_hat_in.at[rows, :], k_hat_ref.at[rows, :]),
            (all_ref.at[blocks, pl.ds(0, 3 * BLOCK), :], raw_ref.at[blocks]),
            (grad_turned_in.at[:, rows], grad_turned_ref.at[:, rows]),
        )[n]
        return pltpu.make_async_copy(source, target, in_sems.at[n, i])

    def leaving(i):
        blocks = tile_blocks(i)
        return pltpu.make_async_copy(send_ref.at[blocks], send_out.at[blocks], out_sems.at[i])

    for n in range(4):
        each_tile(lambda i, n=n: arrival(i, n).start())

    def clear(i, carry):
        for n in range(2):
            arrival(i, n).wait()
        q_hat_ref[tile_at(i), :] = q_turned_ref[:, tile_at(i)].T
        k_turned_ref[:, tile_at(i)] = k_hat_ref[tile_at(i), :].T
        arrival(i, 2).wait()
        value_ref[tile_at(i), :] = tile_turned(raw_ref, i * PAIR, 2).T
        grad_q[i] = jnp.zeros((HEAD_DIM, TILE), F32)
        grad_k[tile_at(i), :] = jnp.zeros((TILE, HEAD_DIM), F32)
        return carry

    lax.fori_loop(0, TILES, clear, 0, unroll=TILES)
    each_tile(lambda i: arrival(i, 3).wait())

    def add_pairs(n, pairs):
        tiles = [
            dot(k_hat_ref[pl.ds(at, KEYS), :], q_turned_ref[:, tile_at(i)]) for _, i, at, _ in pairs
        ]
        prob_grads = [
            dot(value_ref[pl.ds(at, KEYS), :], grad_turned_ref[:, tile_at(i)])
            for _, i, at, _ in pairs
        ]
        tiles = [
            softmax_tile(tile, span_rows_ref, norm_ref, i, mask_at)
            for tile, (_, i, _, mask_at) in zip(tiles, pairs)
        ]
        tiles = [
            (tile * (prob - inner_ref[i, 0:1, :]) * SCALE).astype(BF16)
            for tile, prob, (_, i, _, _) in zip(tiles, prob_grads, pairs)
        ]
        keys = [dot(tile, q_hat_ref[tile_at(i), :]) for tile, (_, i, _, _) in zip(tiles, pairs)]
        queries = [
            dot(k_turned_ref[:, pl.ds(at, KEYS)], tile) for tile, (_, _, at, _) in zip(tiles, pairs)
        ]
        for key, query, (_, i, at, _) in zip(keys, queries, pairs):
            grad_k[pl.ds(at, KEYS), :] += key
            grad_q[i] += query

    each_pairs(total_ref[0], pair_ref, add_pairs)

    gains = jnp.concatenate([gains_ref[...], jnp.zeros((6, HEAD_DIM), F32)], 0).T

    def norm_backward(i, n, grad_hat):
        mean = moments_ref[i, 2 * n : 2 * n + 1, :]
        inverse = moments_ref[i, 2 * n + 1 : 2 * n + 2, :]
        normed = (tile_turned(raw_ref, i * PAIR, n).astype(F32) - mean) * inverse
        grad_normed = grad_hat * gains[:, n : n + 1]
        inner = mean_down(grad_normed * normed)
        grad_in = inverse * (grad_normed - mean_down(grad_normed) - normed * inner)
        send_ref[pl.ds(i * PAIR, PAIR), n * BLOCK : (n + 1) * BLOCK, :] = grad_in.astype(
            BF16
        ).T.reshape(PAIR, BLOCK, HEAD_DIM)
        grad_gain = grad_hat * normed
        return sum(grad_gain[:, c : c + 128] for c in range(0, TILE, 128))

    def finish(i, gain_sums):
        gain_q, gain_k = gain_sums
        gain_q = gain_q + norm_backward(i, 0, grad_q[i])
        gain_k = gain_k + norm_backward(i, 1, grad_k[tile_at(i), :].T)
        leaving(i).start()
        return gain_q, gain_k

    zero = jnp.zeros((HEAD_DIM, 128), F32)
    gain_q, gain_k = lax.fori_loop(0, TILES, finish, (zero, zero), unroll=TILES)
    gain_out_ref[0:1, :] = jnp.sum(gain_q.T, 0, keepdims=True)
    gain_out_ref[1:2, :] = jnp.sum(gain_k.T, 0, keepdims=True)
    each_tile(lambda i: leaving(i).wait())


def run_backward(pairs, total, received, q_turned, k_hat, grad_turned, *arrays):
    return pl.pallas_call(
        backward_kernel,
        in_specs=[SMEM_SPEC] * 2 + [HBM_SPEC] * 4 + [VMEM_SPEC] * len(arrays),
        out_specs=[HBM_SPEC, VMEM_SPEC],
        out_shape=[shape((BLOCKS, 2 * BLOCK, 128), BF16), shape((2, HEAD_DIM), F32)],
        scratch_shapes=[
            pltpu.VMEM((TILES, HEAD_DIM, TILE), F32),
            pltpu.VMEM((LENGTH, HEAD_DIM), F32),
            pltpu.VMEM((LENGTH, HEAD_DIM), BF16),
            pltpu.VMEM((HEAD_DIM, LENGTH), BF16),
            pltpu.VMEM((LENGTH, HEAD_DIM), BF16),
            pltpu.VMEM((BLOCKS, 3 * BLOCK, 128), BF16),
            pltpu.VMEM((HEAD_DIM, LENGTH), BF16),
            pltpu.VMEM((LENGTH, HEAD_DIM), BF16),
            pltpu.VMEM((HEAD_DIM, LENGTH), BF16),
            pltpu.VMEM((BLOCKS, 2 * BLOCK, 128), BF16),
            pltpu.SemaphoreType.DMA((4, TILES)),
            pltpu.SemaphoreType.DMA((TILES,)),
        ],
        compiler_params=pltpu.CompilerParams(vmem_limit_bytes=VMEM_LIMIT),
        cost_estimate=WORK,
        name="backward",
    )(pairs, total, received, q_turned, k_hat, grad_turned, *arrays)


def over_packs(value):
    moved = [value]
    for shift in range(1, PACKS):
        pairs = [(i, (i + shift) % PACKS) for i in range(PACKS)]
        moved.append(lax.ppermute(value, "pack", pairs))
    return moved


def exchange(slab):
    return lax.all_to_all(slab, "seq", split_axis=0, concat_axis=0, tiled=True)


def on_device(
    query_rows, key_rows, value_rows, target_rows, norm_gains, segment_ids, group_labels, mixture
):
    gains = norm_gains.reshape(2, HEAD_DIM)
    first = exchange(pack_rows((query_rows, key_rows, value_rows), segment_ids, "pack_first"))

    image_hot = segment_ids[0][:, None] == jnp.arange(IMAGES, dtype=I32)[None, :]
    labels = jnp.sum(jnp.where(image_hot, group_labels[0][None, :], 0), 1)[None, :]
    extra = jnp.concatenate([segment_ids.astype(F32), *over_packs(labels.astype(F32))], 0)
    second = exchange(pack_rows((target_rows,), extra, "pack_second"))

    pairs, total, span_rows, *hats, probs, moments, norms, head_out = run_attend(first, gains)
    send, grad_turned, inner, counts = run_loss(
        group_labels, mixture, pairs, total, second, head_out, probs
    )
    back = exchange(send)
    send, gain_part = run_backward(
        pairs, total, first, *hats, grad_turned, gains, moments, span_rows, norms, inner
    )
    back, send = lax.optimization_barrier((back, send))
    last = exchange(send)
    attended, grad_value = unpack_rows(back, 2, (0,), "unpack_first")
    losses = jnp.sum(back[:, 2 * BLOCK : 2 * BLOCK + 3, :GROUPS].astype(F32), (0, 1))
    group_total = sum(over_packs(losses))
    group_loss = group_total / (counts[0, :GROUPS] * (HEADS * HEAD_DIM))
    shares = mixture / jnp.sum(mixture)
    raised = shares * jnp.exp(ETA * group_loss)
    new_mixture = raised / jnp.sum(raised)
    grad_gains = sum(over_packs(gain_part)).reshape(2, 1, HEAD_DIM)
    grad_query, grad_key = unpack_rows(last, 2, (), "unpack_last")
    return (attended, grad_query, grad_key, grad_value, grad_gains, new_mixture)


def solution(mesh):
    rows = P("pack", "seq", None)
    gains = P(None, "seq", None)
    return jax.shard_map(
        on_device,
        mesh=mesh,
        in_specs=(rows, rows, rows, rows, gains, P("pack", "seq"), P("pack", None), P()),
        out_specs=(rows, rows, rows, rows, gains, P()),
        check_vma=False,
    )
```
